32 devices in a mesh: dp: 8 (over z, y), seq: 4 (over x, core).
Axes of the slice: x: 2, y: 2, z: 4, core: 2. Of those that a mesh axis runs over, the one named last changes fastest.
Arguments:
- hidden_in: bfloat16 [6144, 2048], P(('dp', 'seq')), may hold values from -6 to 6
- valid_len: int32 [8], replicated, may hold values from 481 to 640, as said below
- doc_lengths: int32 [4, 8, 8], replicated, may hold values from 1 to 4, as said below
- doc_perm: int32 [4, 64], replicated, may hold values from 0 to 63, as said below
- attn_norm: bfloat16 [2048], P('dp'), may hold values from 0.5 to 1.5
- w_query: bfloat16 [2048, 2048], P('dp', 'seq'), may hold values from -0.125 to 0.125
- key_weight: bfloat16 [2048, 1024], P('dp', 'seq'), may hold values from -0.125 to 0.125
- value_weight: bfloat16 [2048, 1024], P('dp', 'seq'), may hold values from -0.125 to 0.125
- w_out: bfloat16 [2048, 2048], P('seq', 'dp'), may hold values from -0.5 to 0.5
- query_norm: bfloat16 [128], P('dp'), may hold values from 0.5 to 1.5
- key_norm_gain: bfloat16 [128], P('dp'), may hold values from 0.5 to 1.5
- mlp_norm: bfloat16 [2048], P('dp'), may hold values from 0.5 to 1.5
- w_gate: bfloat16 [2048, 6144], P('dp', 'seq'), may hold values from -0.125 to 0.125
- w_up: bfloat16 [2048, 6144], P('dp', 'seq'), may hold values from -0.125 to 0.125
- w_down: bfloat16 [6144, 2048], P('seq', 'dp'), may hold values from -0.078125 to 0.078125
- out_grad: bfloat16 [6144, 2048], P(('dp', 'seq')), may hold values from -6 to 6
Outputs:
- mixed: bfloat16 [6144, 2048], P(('dp', 'seq'))
- grad_hidden: bfloat16 [6144, 2048], P(('dp', 'seq'))
- grad_attn_norm: float32 [2048], P(('dp', 'seq'))
- grad_query: float32 [2048, 2048], P('dp', 'seq')
- grad_key: float32 [2048, 1024], P('dp', 'seq')
- grad_value: float32 [2048, 1024], P('dp', 'seq')
- grad_out: float32 [2048, 2048], P('seq', 'dp')
- grad_query_norm: float32 [128], P(('dp', 'seq'))
- grad_key_norm: float32 [128], P(('dp', 'seq'))
- grad_mlp_norm: float32 [2048], P(('dp', 'seq'))
- grad_gate: float32 [2048, 6144], P('dp', 'seq')
- grad_up: float32 [2048, 6144], P('dp', 'seq')
- grad_down: float32 [6144, 2048], P('seq', 'dp')
The draws below stay inside these ranges and needn't reach their ends.
Inputs may be any that keep to these rules, and one draw needn't show every extreme that they name: `valid_len`: one row's long document fills all its reserved slots and one row has the least length, in every draw. `doc_lengths`: both ends are reached in every part. `doc_perm`: for each index of seq a permutation of the 64 short documents; the short documents of one row go to distinct rows, and every row receives exactly 8 of them, from distinct rows.
All inputs are finite; a program needn't handle non-finite values.
Results may differ from the reference program's by a relative error of at most 0.035.
Values may be sent and summed in bfloat16 or wider, within the bound.
A program may use at most 448 MiB of HBM per device.

```python
import math
import jax
import jax.numpy as jnp
from jax import lax

MODEL_DIM = 2048
QUERY_HEADS = 16
KEY_VALUE_HEADS = 8
HEAD_SIZE = 128
FF = 6144
TOK_DEV = 192
MAXSHORT = 4
K_SHORT = 8
BODY = 160
ROW = 768
TOKENS = 6144
N_DP = 8
N_SEQ = 4


def chosen_rows(key):
    order = jax.random.permutation(key, N_DP)
    return (order[0], order[1])


def draw_valid_len(key, part):
    top_row, bottom_row = chosen_rows(key)
    key = jax.random.fold_in(key, 3)
    lowest = (N_SEQ - 1) * BODY + 1
    highest = N_SEQ * BODY
    lengths_all = jax.random.randint(key, (N_DP,), lowest, highest + 1, dtype=jnp.int32)
    row_ids = jnp.arange(N_DP, dtype=jnp.int32)
    lengths_all = jnp.where(row_ids == top_row, highest, lengths_all)
    lengths_all = jnp.where(row_ids == bottom_row, lowest, lengths_all)
    return lengths_all.astype(jnp.int32)


def draw_doc_lengths(key, part):
    top_row, bottom_row = chosen_rows(key)
    key = jax.random.fold_in(key, 5)
    shortest = MAXSHORT // 3
    short_part = jax.random.randint(key, (N_SEQ, N_DP, K_SHORT), shortest, MAXSHORT + 1, dtype=jnp.int32)
    row_ids = jnp.arange(N_DP, dtype=jnp.int32)[None, :, None]
    col_ids = jnp.arange(K_SHORT, dtype=jnp.int32)[None, None, :]
    short_part = jnp.where((row_ids == top_row) & (col_ids == 0), MAXSHORT, short_part)
    short_part = jnp.where((row_ids == bottom_row) & (col_ids == 0), shortest, short_part)
    return short_part.astype(jnp.int32)


def perm_group(key):
    key_first, key_second, key_third = jax.random.split(key, 3)
    spread_rows = jax.random.permutation(key_first, N_DP).astype(jnp.int32)
    target_rows = jax.random.permutation(key_second, N_DP).astype(jnp.int32)
    rank_shift = jax.random.randint(key_third, (N_DP,), 0, K_SHORT, dtype=jnp.int32)
    col_ids = jnp.arange(K_SHORT, dtype=jnp.int32)[None, :]
    dest_rows = target_rows[(spread_rows[:, None] + col_ids) % N_DP]
    dest_rank = (col_ids + rank_shift[dest_rows]) % K_SHORT
    return (dest_rows * K_SHORT + dest_rank).reshape(N_DP * K_SHORT).astype(jnp.int32)


def draw_doc_perm(key, part):
    key = jax.random.fold_in(key, 7)
    group_keys = jax.random.split(key, N_SEQ)
    return jax.vmap(perm_group)(group_keys).astype(jnp.int32)


def block_levels(own_key, dims, shards, smallest, high):
    def one(dim, blocks):
        draws = jax.random.uniform(jax.random.fold_in(jax.random.fold_in(own_key, 6), dim), (blocks,), jnp.float32, smallest / len(shards), high / len(shards))
        return jnp.repeat(jnp.exp(draws), dims[dim] // blocks).reshape((-1,) + (1,) * (len(dims) - dim - 1))

    loudness = one(*shards[0])
    for cut in shards[1:]:
        loudness = loudness * one(*cut)
    return loudness


def noise(own_key, shape, scale, most, cuts=(), held_as=jnp.bfloat16):
    entries = jax.random.normal(own_key, shape, jnp.float32) * scale
    if len(cuts) > 0:
        entries = block_levels(own_key, shape, cuts, -0.22, 0.18) * entries
    return jnp.clip(entries, min=-most, max=most).astype(held_as)


def setup_inputs(seed: int = 0) -> dict:
    seeds = jax.random.split(jax.random.key(seed), 17)
    return {
        "hidden_in": noise(seeds[0], (TOKENS, MODEL_DIM), 1.0, 6.0, ((0, 32),)),
        "valid_len": draw_valid_len(jax.random.fold_in(seeds[16], 71), 0),
        "doc_lengths": draw_doc_lengths(jax.random.fold_in(seeds[16], 71), 0),
        "doc_perm": draw_doc_perm(jax.random.fold_in(seeds[16], 71), 0),
        "attn_norm": jnp.clip(1.0 + 0.1 * jax.random.normal(seeds[4], (MODEL_DIM,), jnp.float32), 0.5, 1.5).astype(jnp.bfloat16),
        "w_query": noise(seeds[5], (MODEL_DIM, QUERY_HEADS * HEAD_SIZE), MODEL_DIM ** -0.5, 0.125, ((0, 8), (1, 4))),
        "key_weight": noise(seeds[6], (MODEL_DIM, KEY_VALUE_HEADS * HEAD_SIZE), MODEL_DIM ** -0.5, 0.125, ((0, 8), (1, 4))),
        "value_weight": noise(seeds[7], (MODEL_DIM, KEY_VALUE_HEADS * HEAD_SIZE), MODEL_DIM ** -0.5, 0.125, ((0, 8), (1, 4))),
        "w_out": noise(seeds[8], (QUERY_HEADS * HEAD_SIZE, MODEL_DIM), (MODEL_DIM // 16) ** -0.5, 0.5, ((0, 4), (1, 8))),
        "query_norm": jnp.clip(1.0 + 0.1 * jax.random.normal(seeds[9], (HEAD_SIZE,), jnp.float32), 0.5, 1.5).astype(jnp.bfloat16),
        "key_norm_gain": jnp.clip(1.0 + 0.1 * jax.random.normal(seeds[10], (HEAD_SIZE,), jnp.float32), 0.5, 1.5).astype(jnp.bfloat16),
        "mlp_norm": jnp.clip(1.0 + 0.1 * jax.random.normal(seeds[11], (MODEL_DIM,), jnp.float32), 0.5, 1.5).astype(jnp.bfloat16),
        "w_gate": noise(seeds[12], (MODEL_DIM, FF), MODEL_DIM ** -0.5, 0.125, ((0, 8), (1, 4))),
        "w_up": noise(seeds[13], (MODEL_DIM, FF), MODEL_DIM ** -0.5, 0.125, ((0, 8), (1, 4))),
        "w_down": noise(seeds[14], (FF, MODEL_DIM), FF ** -0.5, 0.078125, ((0, 4), (1, 8))),
        "out_grad": noise(seeds[15], (TOKENS, MODEL_DIM), 1.0, 6.0, ((0, 32),)),
    }


NORM_EPS = 1e-06
ROPE_BASE = 1000000.0
MASKED = -1e+30
PRECISE = lax.Precision.HIGHEST

@jax.custom_vjp
def lowered_precision(v):
    return lax.optimization_barrier(v.astype(jnp.bfloat16)).astype(jnp.float32)

@jax.custom_vjp
def low_back(v):
    return v

def low_keep(v):
    return (lowered_precision(v), None)

def low_pass(kept, grad):
    return (grad,)

def back_keep(v):
    return (v, None)

def back_low(kept, grad):
    return (lowered_precision(grad),)
lowered_precision.defvjp(low_keep, low_pass)
low_back.defvjp(back_keep, back_low)

def root_mean_norm(values, gain):
    return values * lax.rsqrt(lax.optimization_barrier(jnp.mean(values * values, axis=-1, keepdims=True)) + NORM_EPS) * gain

def apply_rotary(values, position):
    half_width = values.shape[-1] // 2
    freq_index = jnp.arange(half_width, dtype=jnp.float32)
    inverse = jnp.exp(freq_index * (-2.0 * math.log(ROPE_BASE) / values.shape[-1]))
    angles = position.astype(jnp.float32)[:, None] * inverse[None, :]
    cosine = jnp.cos(angles)[:, None, :]
    sine_part = jnp.sin(angles)[:, None, :]
    first = values[..., :half_width]
    second = values[..., half_width:]
    return jnp.concatenate([first * cosine - second * sine_part, second * cosine + first * sine_part], axis=-1)

def layout(lengths_part, perm_part):
    row_count, shorts = lengths_part.shape
    doc_total = row_count * shorts
    starts = (BODY + jnp.cumsum(lengths_part, axis=1) - lengths_part).astype(jnp.int32)
    kept_flat = lengths_part.reshape(doc_total).astype(jnp.int32)
    matched = perm_part[:, None] == jnp.arange(doc_total, dtype=jnp.int32)[None, :]
    placed = lax.optimization_barrier(jnp.sum(jnp.where(matched, kept_flat[:, None], 0), axis=0)).astype(jnp.int32).reshape(row_count, shorts)
    new_at = (BODY + jnp.cumsum(placed, axis=1) - placed).astype(jnp.int32)
    new_start = lax.optimization_barrier(jnp.sum(jnp.where(matched, new_at.reshape(doc_total)[None, :], 0), axis=1)).astype(jnp.int32)
    return (starts.reshape(doc_total), kept_flat, new_start, (perm_part // shorts).astype(jnp.int32))

def balanced(valid_len, doc_lengths, doc_perm):
    seq_count, row_count, shorts = doc_lengths.shape
    doc_total = row_count * shorts
    local = jnp.arange(TOK_DEV, dtype=jnp.int32)
    row_ids = jnp.arange(row_count, dtype=jnp.int32)
    doc_ids = jnp.arange(doc_total, dtype=jnp.int32)
    sources, segments, positions, lives = ([], [], [], [])
    for part in range(seq_count):
        starts, kept_flat, new_start, dest_row = layout(doc_lengths[part], doc_perm[part])
        inside = (dest_row[None, None, :] == row_ids[:, None, None]) & (local[None, :, None] >= new_start[None, None, :]) & (local[None, :, None] < (new_start + kept_flat)[None, None, :])
        offset = local[None, :, None] - new_start[None, None, :]
        in_short = jnp.any(inside, axis=2)
        source_slots = doc_ids // shorts * ROW + part * TOK_DEV + starts
        short_src = lax.optimization_barrier(jnp.sum(jnp.where(inside, source_slots[None, None, :] + offset, 0), axis=2)).astype(jnp.int32)
        short_seg = lax.optimization_barrier(jnp.sum(jnp.where(inside, row_count + part * doc_total + doc_ids[None, None, :], 0), axis=2)).astype(jnp.int32)
        short_pos = lax.optimization_barrier(jnp.sum(jnp.where(inside, offset, 0), axis=2)).astype(jnp.int32)
        long_pos = (part * BODY + local).astype(jnp.int32)
        in_long = (local[None, :] < BODY) & (long_pos[None, :] < valid_len[:, None])
        flat_slot = (row_ids[:, None] * ROW + part * TOK_DEV + local[None, :]).astype(jnp.int32)
        sources.append(jnp.where(in_long, flat_slot, short_src).astype(jnp.int32))
        segments.append(jnp.where(in_long, row_ids[:, None], jnp.where(in_short, short_seg, -1 - flat_slot)).astype(jnp.int32))
        positions.append(jnp.where(in_long, long_pos[None, :], short_pos).astype(jnp.int32))
        lives.append(in_long | in_short)
    return (jnp.concatenate(sources, axis=1), jnp.concatenate(segments, axis=1), jnp.concatenate(positions, axis=1), jnp.concatenate(lives, axis=1))

def row_layer(weights, x_row, seg_row, position_row, live_row):
    attn_norm, w_query, key_weight, value_weight, w_out, query_norm, key_norm_gain, mlp_norm, w_gate, w_up, w_down = weights
    token_rows = x_row.shape[0]
    normed = lowered_precision(root_mean_norm(x_row, attn_norm))
    query_lin = low_back(jnp.dot(normed, w_query, precision=PRECISE))
    key_linear = low_back(jnp.dot(normed, key_weight, precision=PRECISE))
    value_linear = low_back(jnp.dot(normed, value_weight, precision=PRECISE))
    query_rows = lowered_precision(apply_rotary(root_mean_norm(query_lin.reshape(token_rows, QUERY_HEADS, HEAD_SIZE), query_norm), position_row))
    rotated_keys = lowered_precision(apply_rotary(root_mean_norm(key_linear.reshape(token_rows, KEY_VALUE_HEADS, HEAD_SIZE), key_norm_gain), position_row))
    value_heads = lowered_precision(value_linear.reshape(token_rows, KEY_VALUE_HEADS, HEAD_SIZE))
    grouped_heads = query_rows.reshape(token_rows, KEY_VALUE_HEADS, QUERY_HEADS // KEY_VALUE_HEADS, HEAD_SIZE)
    scores = low_back(jnp.einsum('tngd,und->ngtu', grouped_heads, rotated_keys, precision=PRECISE) * HEAD_SIZE ** (-0.5))
    allowed = (seg_row[:, None] == seg_row[None, :]) & (position_row[None, :] <= position_row[:, None])
    masked = jnp.where(allowed, scores, MASKED)
    peak = lax.optimization_barrier(jnp.max(masked, axis=-1, keepdims=True))
    expd = jnp.exp(masked - peak)
    probs = lowered_precision(expd / lax.optimization_barrier(jnp.sum(expd, axis=-1, keepdims=True)))
    context = jnp.einsum('ngtu,und->tngd', probs, value_heads, precision=PRECISE).reshape(token_rows, QUERY_HEADS * HEAD_SIZE)
    attended = lowered_precision(low_back(context))
    resid = x_row + low_back(jnp.dot(attended, w_out, precision=PRECISE))
    normed_mlp = lowered_precision(root_mean_norm(resid, mlp_norm))
    gate = low_back(jnp.dot(normed_mlp, w_gate, precision=PRECISE))
    upper = low_back(jnp.dot(normed_mlp, w_up, precision=PRECISE))
    hidden = lowered_precision(jax.nn.silu(gate) * upper)
    output = resid + jnp.dot(hidden, w_down, precision=PRECISE)
    return output * live_row[:, None]

def reference(hidden_in, valid_len, doc_lengths, doc_perm, attn_norm, w_query, key_weight, value_weight, w_out, query_norm, key_norm_gain, mlp_norm, w_gate, w_up, w_down, out_grad):
    source, segment, position, live_slot = balanced(valid_len, doc_lengths, doc_perm)
    live_scale = live_slot.astype(jnp.float32)
    params = tuple((weight_arg.astype(jnp.float32) for weight_arg in (attn_norm, w_query, key_weight, value_weight, w_out, query_norm, key_norm_gain, mlp_norm, w_gate, w_up, w_down)))
    checked = jax.checkpoint(row_layer)

    def forward(weights, hidden_all):
        moved = jnp.where(live_slot[:, :, None], hidden_all[source], 0.0)
        return lax.map(lambda pieces: checked(weights, pieces[0], pieces[1], pieces[2], pieces[3]), (moved, segment, position, live_scale))
    result, pullback = jax.vjp(forward, params, hidden_in.astype(jnp.float32))
    weight_grads, grad_input = pullback(out_grad.astype(jnp.float32).reshape(result.shape))
    return (result.reshape(TOKENS, MODEL_DIM).astype(jnp.bfloat16), grad_input.astype(jnp.bfloat16), weight_grads[0], weight_grads[1], weight_grads[2], weight_grads[3], weight_grads[4], weight_grads[5], weight_grads[6], weight_grads[7], weight_grads[8], weight_grads[9], weight_grads[10])
```

```python
import functools
import math

import jax
import jax.numpy as jnp
from jax import lax
from jax.experimental import pallas as pl
from jax.experimental.pallas import tpu as pltpu
from jax.sharding import PartitionSpec as P

MAXSHORT = 4
GROUP = 4
MESH = pl.DeviceIdType.MESH
HBM = pl.BlockSpec(memory_space=pltpu.HBM)
VMEM = pl.BlockSpec(memory_space=pltpu.VMEM)
BF16 = jnp.bfloat16
F32 = jnp.float32


NORM_EPS = 1e-06
ROPE_BASE = 1000000.0
MASKED = -1e30
CONTRACT_ROWS = (((0,), (0,)), ((), ()))
CONTRACT_COLS = (((1,), (1,)), ((), ()))


def root_mean_norm(values, gain):
    return values * lax.rsqrt(jnp.mean(values * values, axis=-1, keepdims=True) + NORM_EPS) * gain


def apply_rotary(values, position):
    half_width = values.shape[-1] // 2
    freq_index = jnp.arange(half_width, dtype=jnp.float32)
    inverse = jnp.exp(freq_index * (-2.0 * math.log(ROPE_BASE) / values.shape[-1]))
    angles = position.astype(jnp.float32)[:, None] * inverse[None, :]
    cosine = jnp.cos(angles)[:, None, :]
    sine_part = jnp.sin(angles)[:, None, :]
    first = values[..., :half_width]
    second = values[..., half_width:]
    return jnp.concatenate(
        [first * cosine - second * sine_part, second * cosine + first * sine_part], axis=-1
    )


def head_prep(flat, gain, position):
    return apply_rotary(
        root_mean_norm(flat.reshape(flat.shape[0], -1, gain.shape[0]), gain), position
    )


def product(left, right, dims):
    return lax.dot_general(left, right, dims, preferred_element_type=jnp.float32)


def layout(lengths_part, perm_part, body_len):
    row_count, shorts = lengths_part.shape
    doc_total = row_count * shorts
    starts = body_len + jnp.cumsum(lengths_part, axis=1) - lengths_part
    kept_flat = lengths_part.reshape(doc_total)
    matched = perm_part[:, None] == jnp.arange(doc_total, dtype=jnp.int32)[None, :]
    placed = jnp.sum(jnp.where(matched, kept_flat[:, None], 0), axis=0).reshape(row_count, shorts)
    new_at = body_len + jnp.cumsum(placed, axis=1) - placed
    new_start = jnp.sum(jnp.where(matched, new_at.reshape(doc_total)[None, :], 0), axis=1)
    return (starts.reshape(doc_total), kept_flat, new_start, perm_part // shorts)


def slot_labels(
    kept_flat,
    new_start,
    dest_row,
    part,
    my_row,
    valid_here,
    body_len,
    shard_len,
    row_len,
    row_count,
):
    doc_total = kept_flat.shape[0]
    local = jnp.arange(shard_len, dtype=jnp.int32)
    doc_ids = jnp.arange(doc_total, dtype=jnp.int32)
    inside = (
        (dest_row == my_row)[None, :]
        & (local[:, None] >= new_start[None, :])
        & (local[:, None] < (new_start + kept_flat)[None, :])
    )
    offset = local[:, None] - new_start[None, :]
    in_short = jnp.any(inside, axis=1)
    short_seg = jnp.sum(
        jnp.where(inside, row_count + part * doc_total + doc_ids[None, :], 0), axis=1
    )
    short_pos = jnp.sum(jnp.where(inside, offset, 0), axis=1)
    long_pos = part * body_len + local
    in_long = (local < body_len) & (long_pos < valid_here)
    flat_slot = my_row * row_len + part * shard_len + local
    segment = jnp.where(in_long, my_row, jnp.where(in_short, short_seg, -1 - flat_slot))
    position = jnp.where(in_long, long_pos, short_pos)
    return (segment, position, in_long, in_short)


def attend_scores(query_rows, keys_all, seg_query, pos_query, seg_key, pos_key):
    grouped_heads = query_rows.reshape(
        query_rows.shape[0], keys_all.shape[1], -1, query_rows.shape[-1]
    )
    raw = jnp.einsum(
        "tngd,und->ngtu", grouped_heads, keys_all, preferred_element_type=jnp.float32
    ) * query_rows.shape[-1] ** (-0.5)
    allowed = (seg_query[:, None] == seg_key[None, :]) & (pos_key[None, :] <= pos_query[:, None])
    return (jnp.where(allowed, raw, MASKED), grouped_heads)


def attend_forward(query_rows, keys_all, values_all, seg_query, pos_query, seg_key, pos_key):
    masked, grouped_heads = attend_scores(
        query_rows, keys_all, seg_query, pos_query, seg_key, pos_key
    )
    peak = jnp.max(masked, axis=-1, keepdims=True)
    expd = jnp.exp(masked - peak)
    total_weight = jnp.sum(expd, axis=-1, keepdims=True)
    probs = (expd / total_weight).astype(jnp.bfloat16)
    log_total = peak + jnp.log(total_weight)
    context = jnp.einsum(
        "ngtu,und->tngd", probs, values_all, preferred_element_type=jnp.float32
    ).reshape(query_rows.shape[0], -1)
    return (context.astype(jnp.bfloat16), log_total)


def attend_backward(
    query_rows, keys_all, values_all, grad_att, log_total, seg_query, pos_query, seg_key, pos_key
):
    masked, grouped_heads = attend_scores(
        query_rows, keys_all, seg_query, pos_query, seg_key, pos_key
    )
    probs_full = jnp.exp(masked - log_total)
    probs_low = probs_full.astype(jnp.bfloat16)
    grad_group = grad_att.reshape(grouped_heads.shape)
    grad_probs = jnp.einsum(
        "tngd,und->ngtu", grad_group, values_all, preferred_element_type=jnp.float32
    )
    grad_values = jnp.einsum(
        "ngtu,tngd->und", probs_low, grad_group, preferred_element_type=jnp.float32
    )
    spread_sum = jnp.sum(probs_full * grad_probs, axis=-1, keepdims=True)
    grad_scores = (probs_full * (grad_probs - spread_sum)).astype(jnp.bfloat16)
    scale_factor = query_rows.shape[-1] ** (-0.5)
    grad_queries = (
        jnp.einsum(
            "ngtu,und->tngd", grad_scores, keys_all, preferred_element_type=jnp.float32
        ).reshape(query_rows.shape)
        * scale_factor
    )
    grad_keys = (
        jnp.einsum("ngtu,tngd->und", grad_scores, grouped_heads, preferred_element_type=jnp.float32)
        * scale_factor
    )
    return (grad_queries, grad_keys, grad_values)


class Place:
    def __init__(self, dp_size, seq_size):
        self.dp_size = dp_size
        self.seq_size = seq_size
        self.high = dp_size // GROUP
        self.cores = seq_size // 2
        self.d = lax.axis_index("dp")
        self.s = lax.axis_index("seq")
        self.g = lax.rem(self.d, GROUP)
        self.h = lax.div(self.d, GROUP)
        self.x = lax.div(self.s, self.cores)
        self.c = lax.rem(self.s, self.cores)
        self.y = lax.rem(self.g, 2)
        self.l = lax.div(self.g, 2)
        self.gy = self.g + 1 - 2 * self.y
        self.gl = lax.rem(self.g + 2, GROUP)
        self.gd = 3 - self.g
        self.y_peer = (self.h * GROUP + self.gy, self.s)
        self.l_peer = (self.h * GROUP + self.gl, self.s)
        self.d_peer = (self.h * GROUP + self.gd, self.s)
        self.x_peer = (self.d, (1 - self.x) * self.cores + self.c)
        self.c_peer = (self.d, self.x * self.cores + 1 - self.c)

    def h_peer(self, step):
        return (lax.rem(self.h + step, self.high) * GROUP + self.g, self.s)

    def h_from(self, step):
        return lax.rem(self.h + self.high - step, self.high)

    def g_peer(self, step):
        return (self.h * GROUP + lax.rem(self.g + step, GROUP), self.s)


class Mover:
    def __init__(self, send_sems, recv_sems, local_sems):
        self.send_sems = send_sems
        self.recv_sems = recv_sems
        self.local_sems = local_sems
        self.count = 0
        self.local_count = 0
        self.sent = []

    def send(self, source, target, device):
        index = self.count
        self.count += 1
        copy = pltpu.make_async_remote_copy(
            src_ref=source,
            dst_ref=target,
            send_sem=self.send_sems.at[index],
            recv_sem=self.recv_sems.at[index],
            device_id=device,
            device_id_type=MESH,
        )
        copy.start()
        self.sent.append(copy)
        return copy

    def local(self, source, target):
        index = self.local_count
        self.local_count += 1
        copy = pltpu.make_async_copy(source, target, self.local_sems.at[index])
        copy.start()
        return copy

    def finish(self):
        for copy in self.sent:
            copy.wait_send()


def greet(peers):
    barrier = pltpu.get_barrier_semaphore()
    for peer in peers:
        pl.semaphore_signal(barrier, inc=1, device_id=peer, device_id_type=MESH)
    pl.semaphore_wait(barrier, len(peers))


def dp_peers(place):
    return [
        (lax.rem(place.d + step, place.dp_size), place.s) for step in range(1, place.dp_size)
    ]


def sems(count, local):
    return [
        pltpu.SemaphoreType.DMA((count,)),
        pltpu.SemaphoreType.DMA((count,)),
        pltpu.SemaphoreType.DMA((max(local, 1),)),
    ]


def comm_params(collective_id, vmem=None):
    return pltpu.CompilerParams(
        collective_id=collective_id,
        has_side_effects=True,
        vmem_limit_bytes=vmem if vmem is not None else 60 * 1024 * 1024,
    )


def add_rows(target, terms, rows, chunk):
    def step(index, carry):
        part = pl.ds(pl.multiple_of(index * chunk, chunk), chunk)
        total = terms[0][part, :].astype(F32)
        for term in terms[1:]:
            total = total + term[part, :].astype(F32)
        target[part, :] = total.astype(target.dtype)
        return carry

    lax.fori_loop(0, rows // chunk, step, 0)


def exchange_kernel(sizes, with_row, *refs):
    place = Place(*sizes)
    if with_row:
        out_ref, row_ref, in_ref, rows_ref, send_sems, recv_sems, local_sems = refs
    else:
        out_ref, in_ref, send_sems, recv_sems, local_sems = refs
    mover = Mover(send_sems, recv_sems, local_sems)
    greet(dp_peers(place))
    copies = []
    for step in range(1, place.dp_size):
        other = lax.rem(place.d + step, place.dp_size)
        copies.append(mover.send(out_ref.at[other], in_ref.at[place.d], (other, place.s)))
        if with_row:
            copies.append(mover.send(row_ref, rows_ref.at[place.d], (other, place.s)))
    in_ref[place.d] = out_ref[place.d]
    if with_row:
        rows_ref[place.d] = row_ref[...]
    for copy in copies:
        copy.wait_recv()
    mover.finish()


def exchange(sizes, collective_id, blocks, row=None):
    dp_size = sizes[0]
    args = (blocks,) if row is None else (blocks, row)
    shapes = [jax.ShapeDtypeStruct(blocks.shape, blocks.dtype)]
    if row is not None:
        shapes.append(jax.ShapeDtypeStruct((dp_size,) + row.shape, row.dtype))
    return pl.pallas_call(
        functools.partial(exchange_kernel, sizes, row is not None),
        out_shape=shapes,
        in_specs=[VMEM] * len(args),
        out_specs=[VMEM] * len(shapes),
        scratch_shapes=sems((dp_size - 1) * len(args), 0),
        compiler_params=comm_params(collective_id),
        name="exchange_rows",
    )(*args)


class GatherSeq:
    sends = 3

    def __init__(self, place, mover, own, full):
        self.place, self.mover, self.full = place, mover, full
        self.local = mover.local(own, full.at[place.s])
        self.over_x = mover.send(own, full.at[place.s], place.x_peer)
        self.over_c = mover.send(own, full.at[place.s], place.c_peer)

    def forward(self):
        self.over_x.wait_recv()
        block = self.full.at[self.place.x_peer[1]]
        self.passed = self.mover.send(block, block, self.place.c_peer)

    def finish(self):
        self.local.wait()
        self.over_c.wait_recv()
        self.passed.wait_recv()


class GatherGroup:
    sends = 10

    def __init__(self, place, mover, own, full):
        self.place, self.mover, self.full = place, mover, full
        half = own.shape[0] // 2
        self.low, self.top = pl.ds(0, half), pl.ds(half, half)
        self.local = mover.local(own, full.at[place.g, place.c])
        spot = full.at[place.g, place.c]
        self.y_low = mover.send(own.at[self.low], spot.at[self.low], place.y_peer)
        self.l_top = mover.send(own.at[self.top], spot.at[self.top], place.l_peer)
        self.y_top = mover.send(own.at[self.top], spot.at[self.top], place.y_peer)
        self.l_low = mover.send(own.at[self.low], spot.at[self.low], place.l_peer)
        self.core = [mover.send(own, spot, place.c_peer)]

    def forward(self):
        place, mover, full = self.place, self.mover, self.full
        self.y_low.wait_recv()
        part = full.at[place.gy, place.c, self.low]
        self.d_low = mover.send(part, part, place.l_peer)
        self.l_top.wait_recv()
        part = full.at[place.gl, place.c, self.top]
        self.d_top = mover.send(part, part, place.y_peer)
        self.y_top.wait_recv()
        part = full.at[place.gy, place.c]
        self.core.append(mover.send(part, part, place.c_peer))
        self.l_low.wait_recv()
        part = full.at[place.gl, place.c]
        self.core.append(mover.send(part, part, place.c_peer))

    def finish(self):
        place = self.place
        self.d_low.wait_recv()
        self.d_top.wait_recv()
        part = self.full.at[place.gd, place.c]
        self.core.append(self.mover.send(part, part, place.c_peer))
        self.local.wait()
        for copy in self.core:
            copy.wait_recv()


def gather_seq_kernel(sizes, own, full, send_sems, recv_sems, local_sems):
    place = Place(*sizes)
    mover = Mover(send_sems, recv_sems, local_sems)
    greet([place.x_peer, place.c_peer])
    gather = GatherSeq(place, mover, own, full)
    gather.forward()
    gather.finish()
    mover.finish()


def gather_seq(sizes, collective_id, own):
    return pl.pallas_call(
        functools.partial(gather_seq_kernel, sizes),
        out_shape=jax.ShapeDtypeStruct((sizes[1],) + own.shape, own.dtype),
        in_specs=[HBM],
        out_specs=HBM,
        scratch_shapes=sems(GatherSeq.sends, 1),
        compiler_params=comm_params(collective_id),
        name="gather_row",
    )(own)


def gather_group_kernel(sizes, own, full, send_sems, recv_sems, local_sems):
    place = Place(*sizes)
    mover = Mover(send_sems, recv_sems, local_sems)
    greet([place.y_peer, place.l_peer, place.c_peer])
    gather = GatherGroup(place, mover, own, full)
    gather.forward()
    gather.finish()
    mover.finish()


def gather_group(sizes, collective_id, own):
    return pl.pallas_call(
        functools.partial(gather_group_kernel, sizes),
        out_shape=jax.ShapeDtypeStruct((GROUP, sizes[1] // 2) + own.shape, own.dtype),
        in_specs=[HBM],
        out_specs=HBM,
        scratch_shapes=sems(GatherGroup.sends, 1),
        compiler_params=comm_params(collective_id),
        name="gather_group",
    )(own)


class ScatterSeq:
    sends = 3
    locals = 2

    @staticmethod
    def scratch(rows, width):
        block = (rows, width)
        return [
            pltpu.VMEM((2,) + block, BF16),
            pltpu.VMEM((2,) + block, BF16),
            pltpu.VMEM(block, BF16),
        ]

    def __init__(self, place, mover, parts, out, own, from_c, from_x):
        self.place, self.mover, self.out = place, mover, out
        self.own, self.from_c, self.from_x = own, from_c, from_x
        cores = place.cores
        places = ((1 - place.x) * cores, place.x * cores)
        self.over_c, self.mine = [], []
        for index, base in enumerate(places):
            self.over_c.append(
                mover.send(parts.at[base + 1 - place.c], from_c.at[index], place.c_peer)
            )
            self.mine.append(mover.local(parts.at[base + place.c], own.at[index]))

    def forward(self):
        rows = self.own.shape[1]
        self.over_c[0].wait_recv()
        self.mine[0].wait()
        add_rows(self.own.at[0], [self.own.at[0], self.from_c.at[0]], rows, 32)
        self.over_x = self.mover.send(self.own.at[0], self.from_x, self.place.x_peer)

    def finish(self):
        rows = self.own.shape[1]
        self.over_c[1].wait_recv()
        self.mine[1].wait()
        self.over_x.wait_recv()
        add_rows(self.out, [self.own.at[1], self.from_c.at[1], self.from_x], rows, 32)


class ScatterGroup:
    sends = 10
    locals = 4

    @staticmethod
    def scratch(rows, width):
        block = (GROUP, rows, width)
        half = (rows // 2, width)
        return [
            pltpu.VMEM(block, BF16),
            pltpu.VMEM(block, BF16),
            pltpu.VMEM((6,) + half, BF16),
        ]

    def __init__(self, place, mover, parts, out, own, from_c, landed):
        self.place, self.mover, self.out = place, mover, out
        self.own, self.from_c, self.landed = own, from_c, landed
        self.over_c, self.mine = [], []
        for index, owner in enumerate((place.gd, place.gy, place.gl, place.g)):
            self.over_c.append(
                mover.send(parts.at[owner, 1 - place.c], from_c.at[index], place.c_peer)
            )
            self.mine.append(mover.local(parts.at[owner, place.c], own.at[index]))

    def ready(self, index):
        self.over_c[index].wait_recv()
        self.mine[index].wait()
        rows = self.own.shape[1]
        add_rows(self.own.at[index], [self.own.at[index], self.from_c.at[index]], rows, 32)

    def forward(self):
        place, mover, own, landed = self.place, self.mover, self.own, self.landed
        half = own.shape[1] // 2
        low, top = pl.ds(0, half), pl.ds(half, half)
        self.ready(0)
        self.y_diag = mover.send(own.at[0, low], landed.at[0], place.y_peer)
        self.l_diag = mover.send(own.at[0, top], landed.at[1], place.l_peer)
        self.ready(1)
        self.y_own = mover.send(own.at[1, low], landed.at[2], place.y_peer)
        self.ready(2)
        self.l_own = mover.send(own.at[2, top], landed.at[3], place.l_peer)
        self.y_diag.wait_recv()
        add_rows(own.at[2, low], [own.at[2, low], landed.at[0]], half, 32)
        self.l_last = mover.send(own.at[2, low], landed.at[4], place.l_peer)
        self.l_diag.wait_recv()
        add_rows(own.at[1, top], [own.at[1, top], landed.at[1]], half, 32)
        self.y_last = mover.send(own.at[1, top], landed.at[5], place.y_peer)
        self.ready(3)

    def finish(self):
        own, landed = self.own, self.landed
        half = own.shape[1] // 2
        low, top = pl.ds(0, half), pl.ds(half, half)
        self.y_own.wait_recv()
        self.l_last.wait_recv()
        add_rows(self.out.at[low], [own.at[3, low], landed.at[2], landed.at[4]], half, 32)
        self.l_own.wait_recv()
        self.y_last.wait_recv()
        add_rows(self.out.at[top], [own.at[3, top], landed.at[3], landed.at[5]], half, 32)


def scatter_seq_kernel(sizes, parts, out, own, from_c, from_x, send_sems, recv_sems, local_sems):
    place = Place(*sizes)
    mover = Mover(send_sems, recv_sems, local_sems)
    greet([place.x_peer, place.c_peer])
    scatter = ScatterSeq(place, mover, parts, out, own, from_c, from_x)
    scatter.forward()
    scatter.finish()
    mover.finish()


def scatter_seq(sizes, collective_id, parts):
    rows, width = parts.shape[1:]
    return pl.pallas_call(
        functools.partial(scatter_seq_kernel, sizes),
        out_shape=jax.ShapeDtypeStruct((rows, width), F32),
        in_specs=[HBM],
        out_specs=VMEM,
        scratch_shapes=ScatterSeq.scratch(rows, width) + sems(ScatterSeq.sends, ScatterSeq.locals),
        compiler_params=comm_params(collective_id),
        name="scatter_row",
    )(parts)


def scatter_group_kernel(sizes, parts, out, own, from_c, landed, send_sems, recv_sems, local_sems):
    place = Place(*sizes)
    mover = Mover(send_sems, recv_sems, local_sems)
    greet([place.y_peer, place.l_peer, place.c_peer])
    scatter = ScatterGroup(place, mover, parts, out, own, from_c, landed)
    scatter.forward()
    scatter.finish()
    mover.finish()


def scatter_group(sizes, collective_id, parts):
    rows, width = parts.shape[2:]
    return pl.pallas_call(
        functools.partial(scatter_group_kernel, sizes),
        out_shape=jax.ShapeDtypeStruct((rows, width), F32),
        in_specs=[HBM],
        out_specs=VMEM,
        scratch_shapes=ScatterGroup.scratch(rows, width)
        + sems(ScatterGroup.sends, ScatterGroup.locals),
        compiler_params=comm_params(collective_id),
        name="scatter_group",
    )(parts)


class GatherDp:
    def __init__(self, place, mover, own, full):
        self.place, self.mover, self.own, self.full = place, mover, own, full
        self.local = mover.local(own, full.at[place.d])
        spot = full.at[place.d]
        self.over_h = [
            mover.send(own, spot, place.h_peer(step)) for step in range(1, place.high)
        ]
        self.over_l = [mover.send(own, spot, place.l_peer)]
        self.over_y = [mover.send(own, spot, place.y_peer)]

    def forward_high(self):
        place = self.place
        for step, copy in enumerate(self.over_h, 1):
            copy.wait_recv()
            block = self.full.at[place.h_from(step) * GROUP + place.g]
            self.over_l.append(self.mover.send(block, block, place.l_peer))
            self.over_y.append(self.mover.send(block, block, place.y_peer))

    def forward_l(self):
        place = self.place
        for step, copy in enumerate(self.over_l):
            copy.wait_recv()
            high = place.h if step == 0 else place.h_from(step)
            block = self.full.at[high * GROUP + place.gl]
            self.over_y.append(self.mover.send(block, block, place.y_peer))

    def finish(self):
        self.local.wait()
        for copy in self.over_y:
            copy.wait_recv()


class GatherColumns:
    def __init__(self, place, mover, own, full):
        self.place, self.mover, self.full = place, mover, full
        self.quarter = own.shape[1] // GROUP
        self.near = pl.ds(0, self.quarter)
        self.far = pl.ds(self.quarter, self.quarter)
        self.over_g = []
        spot = full.at[place.h, place.g, :, self.near]
        for step in (3, 1, 2):
            to = lax.rem(place.g + step, GROUP)
            columns = pl.ds(pl.multiple_of(to * self.quarter, self.quarter), self.quarter)
            self.over_g.append(mover.send(own.at[:, columns], spot, place.g_peer(step)))
        columns = pl.ds(pl.multiple_of(place.g * self.quarter, self.quarter), self.quarter)
        self.local = mover.local(own.at[:, columns], spot)

    def forward_g(self):
        place = self.place
        self.local.wait()
        for copy in self.over_g:
            copy.wait_recv()
        near = self.full.at[place.h, :, :, self.near]
        far = self.full.at[place.h, :, :, self.far]
        self.over_h = [
            self.mover.send(near, near, place.h_peer(step)) for step in range(1, place.high)
        ]
        self.over_x = [self.mover.send(near, far, place.x_peer)]

    def forward_high(self):
        place = self.place
        for step, copy in enumerate(self.over_h, 1):
            copy.wait_recv()
            high = place.h_from(step)
            self.over_x.append(
                self.mover.send(
                    self.full.at[high, :, :, self.near],
                    self.full.at[high, :, :, self.far],
                    place.x_peer,
                )
            )

    def finish(self):
        for copy in self.over_x:
            copy.wait_recv()


def gather_all_kernel(sizes, *refs):
    qkv, wo, wg, wu, wd, gy, nrm = refs[:7]
    full_qkv, full_wo, full_g, full_u, full_d, full_gy, full_nrm = refs[7:14]
    send_sems, recv_sems, local_sems = refs[14:]
    place = Place(*sizes)
    mover = Mover(send_sems, recv_sems, local_sems)
    greet(dp_peers(place) + [place.x_peer, place.c_peer])
    row = GatherSeq(place, mover, nrm, full_nrm)
    attn = [GatherDp(place, mover, qkv, full_qkv)]
    mlp = [GatherColumns(place, mover, wg, full_g)]
    mlp.append(GatherColumns(place, mover, wu, full_u))
    mlp[0].forward_g()
    attn[0].forward_high()
    attn.append(GatherDp(place, mover, wo, full_wo))
    mlp[1].forward_g()
    mlp.append(GatherColumns(place, mover, wd, full_d))
    row.forward()
    attn[0].forward_l()
    mlp[0].forward_high()
    attn[1].forward_high()
    mlp[2].forward_g()
    attn[1].forward_l()
    group = GatherGroup(place, mover, gy, full_gy)
    mlp[1].forward_high()
    group.forward()
    mlp[2].forward_high()
    for part in [row, group] + attn + mlp:
        part.finish()
    mover.finish()


def gather_all(sizes, collective_id, qkv, wo, wg, wu, wd, gy, nrm):
    dp_size, seq_size = sizes
    high = dp_size // GROUP
    rows = qkv.shape[0]
    wide = (high, GROUP, rows, wg.shape[1] // 2)
    shapes = [
        (dp_size,) + qkv.shape,
        (dp_size,) + wo.shape,
        wide,
        wide,
        wide,
        (GROUP, seq_size // 2) + gy.shape,
        (seq_size,) + nrm.shape,
    ]
    sends = 2 * (high + 1 + high * 3) + 3 * (3 + 2 * high) + GatherGroup.sends + GatherSeq.sends
    return pl.pallas_call(
        functools.partial(gather_all_kernel, sizes),
        out_shape=[jax.ShapeDtypeStruct(shape, BF16) for shape in shapes],
        in_specs=[HBM] * 7,
        out_specs=[HBM] * 7,
        scratch_shapes=sems(sends, 7),
        compiler_params=comm_params(collective_id),
        name="gather_weights",
    )(qkv, wo, wg, wu, wd, gy, nrm)


class ScatterColumns:
    @staticmethod
    def scratch(place_high, rows, quarter):
        group_rows = GROUP * rows
        return [
            pltpu.VMEM((place_high * group_rows, quarter), BF16),
            pltpu.VMEM((place_high * group_rows, quarter), BF16),
            pltpu.VMEM((max(place_high - 1, 1), group_rows, quarter), BF16),
            pltpu.VMEM((group_rows, quarter), BF16),
            pltpu.VMEM((GROUP - 1, rows, quarter), BF16),
        ]

    def __init__(self, place, mover, parts, out, own, from_x, from_h, mine, from_g):
        self.place, self.mover, self.out = place, mover, out
        self.own, self.from_x, self.from_h = own, from_x, from_h
        self.mine, self.from_g = mine, from_g
        quarter = own.shape[1]
        self.over_x = mover.send(parts.at[:, pl.ds(quarter, quarter)], from_x, place.x_peer)
        self.local = mover.local(parts.at[:, pl.ds(0, quarter)], own)

    def forward_x(self):
        place, own = self.place, self.own
        group_rows = self.mine.shape[0]
        self.over_x.wait_recv()
        self.local.wait()
        add_rows(own, [own, self.from_x], own.shape[0], 64)
        self.over_h = []
        for step in range(1, place.high):
            high = lax.rem(place.h + step, place.high)
            rows = pl.ds(pl.multiple_of(high * group_rows, group_rows), group_rows)
            self.over_h.append(
                self.mover.send(own.at[rows], self.from_h.at[step - 1], place.h_peer(step))
            )

    def forward_high(self):
        place = self.place
        group_rows = self.mine.shape[0]
        own_rows = pl.ds(pl.multiple_of(place.h * group_rows, group_rows), group_rows)
        for copy in self.over_h:
            copy.wait_recv()
        terms = [self.own.at[own_rows]]
        terms += [self.from_h.at[step] for step in range(place.high - 1)]
        add_rows(self.mine, terms, group_rows, 64)
        rows = group_rows // GROUP
        self.over_g = []
        for step in range(1, GROUP):
            to = lax.rem(place.g + step, GROUP)
            block = pl.ds(pl.multiple_of(to * rows, rows), rows)
            self.over_g.append(
                self.mover.send(self.mine.at[block], self.from_g.at[step - 1], place.g_peer(step))
            )

    def finish(self):
        place, quarter = self.place, self.own.shape[1]
        rows = self.mine.shape[0] // GROUP
        block = pl.ds(pl.multiple_of(place.g * rows, rows), rows)
        columns = pl.ds(pl.multiple_of(place.g * quarter, quarter), quarter)
        self.out[:, columns] = self.mine[block, :].astype(F32)
        for step, copy in enumerate(self.over_g, 1):
            copy.wait_recv()
            source = lax.rem(place.g + GROUP - step, GROUP)
            columns = pl.ds(pl.multiple_of(source * quarter, quarter), quarter)
            self.out[:, columns] = self.from_g[step - 1].astype(F32)


class ScatterDp:
    @staticmethod
    def scratch(high, rows, width):
        return [
            pltpu.VMEM((2, high, rows, width), BF16),
            pltpu.VMEM((2, high, rows, width), BF16),
            pltpu.VMEM((high, rows, width), BF16),
            pltpu.VMEM((max(high - 1, 1), rows, width), BF16),
        ]

    def __init__(self, place, mover, parts, out, own, from_y, from_l, from_h):
        self.place, self.mover, self.out = place, mover, out
        self.own, self.from_y, self.from_l, self.from_h = own, from_y, from_l, from_h
        self.over_y, self.local = [], []
        for index, l_owner in enumerate((1 - place.l, place.l)):
            self.over_y.append(
                mover.send(parts.at[:, l_owner, 1 - place.y], from_y.at[index], place.y_peer)
            )
            self.local.append(mover.local(parts.at[:, l_owner, place.y], own.at[index]))

    def ready(self, index):
        self.over_y[index].wait_recv()
        self.local[index].wait()
        for high in range(self.place.high):
            own = self.own.at[index, high]
            add_rows(own, [own, self.from_y.at[index, high]], own.shape[0], 32)

    def forward_y(self):
        self.ready(0)
        self.over_l = self.mover.send(self.own.at[0], self.from_l, self.place.l_peer)

    def forward_l(self):
        place = self.place
        self.ready(1)
        self.over_l.wait_recv()
        for high in range(place.high):
            own = self.own.at[1, high]
            add_rows(own, [own, self.from_l.at[high]], own.shape[0], 32)
        self.over_h = []
        for step in range(1, place.high):
            high = lax.rem(place.h + step, place.high)
            self.over_h.append(
                self.mover.send(self.own.at[1, high], self.from_h.at[step - 1], place.h_peer(step))
            )

    def finish(self):
        for copy in self.over_h:
            copy.wait_recv()
        terms = [self.own.at[1, self.place.h]]
        terms += [self.from_h.at[step] for step in range(self.place.high - 1)]
        add_rows(self.out, terms, self.out.shape[0], 32)


def scatter_all_kernel(sizes, *refs):
    grad_qkv, grad_wo, grad_g, grad_u, grad_d, down = refs[:6]
    out_qkv, out_wo, out_g, out_u, out_d, out_down = refs[6:12]
    send_sems, recv_sems, local_sems = refs[-3:]
    scratch = list(refs[12:-3])

    def take(count):
        taken = scratch[:count]
        del scratch[:count]
        return taken

    place = Place(*sizes)
    mover = Mover(send_sems, recv_sems, local_sems)
    greet(dp_peers(place) + [place.x_peer, place.c_peer])
    wo = ScatterDp(place, mover, grad_wo, out_wo, *take(4))
    qkv = ScatterDp(place, mover, grad_qkv, out_qkv, *take(4))
    mlp = [
        ScatterColumns(place, mover, grad, out, *take(5))
        for grad, out in ((grad_d, out_d), (grad_g, out_g), (grad_u, out_u))
    ]
    row = ScatterGroup(place, mover, down, out_down, *take(3))
    mlp[0].forward_x()
    wo.forward_y()
    qkv.forward_y()
    mlp[1].forward_x()
    mlp[0].forward_high()
    wo.forward_l()
    mlp[2].forward_x()
    qkv.forward_l()
    mlp[1].forward_high()
    row.forward()
    mlp[2].forward_high()
    for part in (mlp[0], wo, mlp[1], qkv, row, mlp[2]):
        part.finish()
    mover.finish()


def scatter_all(sizes, collective_id, grad_qkv, grad_wo, grad_g, grad_u, grad_d, down):
    dp_size, _ = sizes
    high = dp_size // GROUP
    rows = grad_g.shape[0] // dp_size
    quarter = grad_g.shape[1] // 2
    shapes = [
        (rows, grad_qkv.shape[1]),
        (rows, grad_wo.shape[1]),
        (rows, GROUP * quarter),
        (rows, GROUP * quarter),
        (rows, GROUP * quarter),
        down.shape[2:],
    ]
    split = (high, 2, 2, rows)
    args = (
        grad_qkv.reshape(split + (-1,)),
        grad_wo.reshape(split + (-1,)),
        grad_g,
        grad_u,
        grad_d,
        down,
    )
    scratch = ScatterDp.scratch(high, rows, grad_wo.shape[1])
    scratch += ScatterDp.scratch(high, rows, grad_qkv.shape[1])
    for _ in range(3):
        scratch += ScatterColumns.scratch(high, rows, quarter)
    scratch += ScatterGroup.scratch(*down.shape[2:])
    sends = 2 * (2 + high) + 3 * (high + 3) + ScatterGroup.sends
    return pl.pallas_call(
        functools.partial(scatter_all_kernel, sizes),
        out_shape=[jax.ShapeDtypeStruct(shape, F32) for shape in shapes],
        in_specs=[HBM] * 6,
        out_specs=[VMEM] * 6,
        scratch_shapes=scratch + sems(sends, 4 + 3 + ScatterGroup.locals),
        compiler_params=comm_params(collective_id),
        name="scatter_grads",
    )(*args)


def per_device(
    sizes,
    hidden_in,
    valid_len,
    doc_lengths,
    doc_perm,
    attn_norm,
    w_query,
    key_weight,
    value_weight,
    w_out,
    query_norm,
    key_norm_gain,
    mlp_norm,
    w_gate,
    w_up,
    w_down,
    out_grad,
):
    shard_len = hidden_in.shape[0]
    model_width = hidden_in.shape[1]
    seq_count = doc_lengths.shape[0]
    row_count = doc_lengths.shape[1]
    shorts = doc_lengths.shape[2]
    row_len = shard_len * seq_count
    cap_len = MAXSHORT
    body_len = shard_len - shorts * cap_len
    my_row = lax.axis_index("dp")
    my_part = lax.axis_index("seq")
    valid_here = valid_len[my_row]
    all_starts, all_kept, all_new, all_dest = jax.vmap(
        lambda lengths_part, perm_part: layout(lengths_part, perm_part, body_len)
    )(doc_lengths, doc_perm)
    part_ids = jnp.arange(seq_count, dtype=jnp.int32)
    seg_parts, pos_parts, long_parts, short_parts = jax.vmap(
        lambda kept_p, new_p, dest_p, part: slot_labels(
            kept_p, new_p, dest_p, part, my_row, valid_here, body_len, shard_len, row_len, row_count
        )
    )(all_kept, all_new, all_dest, part_ids)
    segment = seg_parts.reshape(row_len)
    position = pos_parts.reshape(row_len)
    seg_local = lax.dynamic_index_in_dim(seg_parts, my_part, 0, keepdims=False)
    pos_local = lax.dynamic_index_in_dim(pos_parts, my_part, 0, keepdims=False)
    keep_long = lax.dynamic_index_in_dim(long_parts, my_part, 0, keepdims=False)
    live_local = keep_long | lax.dynamic_index_in_dim(short_parts, my_part, 0, keepdims=False)
    starts = lax.dynamic_index_in_dim(all_starts, my_part, 0, keepdims=False)
    kept_flat = lax.dynamic_index_in_dim(all_kept, my_part, 0, keepdims=False)
    new_start = lax.dynamic_index_in_dim(all_new, my_part, 0, keepdims=False)
    dest_row = lax.dynamic_index_in_dim(all_dest, my_part, 0, keepdims=False)
    row_ids = jnp.arange(row_count, dtype=jnp.int32)
    local_slots = jnp.arange(shard_len, dtype=jnp.int32)
    cap_ids = jnp.arange(cap_len, dtype=jnp.int32)
    my_dest = lax.dynamic_slice_in_dim(dest_row, my_row * shorts, shorts)
    my_starts = lax.dynamic_slice_in_dim(starts, my_row * shorts, shorts)
    my_kept = lax.dynamic_slice_in_dim(kept_flat, my_row * shorts, shorts)
    going = my_dest[None, :] == row_ids[:, None]
    send_start = jnp.sum(jnp.where(going, my_starts[None, :], 0), axis=1)
    send_len = jnp.sum(jnp.where(going, my_kept[None, :], 0), axis=1)
    send_map = (
        (
            (cap_ids[None, :, None] < send_len[:, None, None])
            & (local_slots[None, None, :] == send_start[:, None, None] + cap_ids[None, :, None])
        )
        .reshape(row_count * cap_len, shard_len)
        .astype(jnp.bfloat16)
    )
    coming = (dest_row == my_row).reshape(row_count, shorts)
    recv_start = jnp.sum(jnp.where(coming, new_start.reshape(row_count, shorts), 0), axis=1)
    recv_len = jnp.sum(jnp.where(coming, kept_flat.reshape(row_count, shorts), 0), axis=1)
    recv_map = (
        (
            (cap_ids[None, None, :] < recv_len[None, :, None])
            & (local_slots[:, None, None] == recv_start[None, :, None] + cap_ids[None, None, :])
        )
        .reshape(shard_len, row_count * cap_len)
        .astype(jnp.bfloat16)
    )
    high_dims = (row_count * cap_len, model_width)
    outgoing = jnp.dot(send_map, hidden_in, preferred_element_type=F32).astype(BF16)
    flat_blocks = (row_count, 16, cap_len * model_width // 16)

    def spread(piece, total):
        return lax.dynamic_update_slice(
            jnp.zeros((total,), F32), piece.astype(F32), (my_row * piece.shape[0],)
        )

    head_size = query_norm.shape[0] * row_count
    gain_row = jnp.concatenate(
        [
            spread(attn_norm, model_width),
            spread(mlp_norm, model_width),
            spread(query_norm, head_size),
            spread(key_norm_gain, head_size),
        ]
    )[None, :]
    incoming, gain_rows = exchange(sizes, 0, outgoing.reshape(flat_blocks), gain_row)
    gains = jnp.sum(gain_rows, axis=0)[0]
    cuts = (model_width, 2 * model_width, 2 * model_width + head_size)
    gain_attn, gain_mlp, gain_query, gain_key = jnp.split(gains, cuts)
    moved = jnp.where(keep_long[:, None], hidden_in.astype(F32), 0.0) + jnp.dot(
        recv_map, incoming.reshape(high_dims), preferred_element_type=F32
    )
    live_scale = live_local.astype(F32)[:, None]
    grad_y_low = (out_grad.astype(F32) * live_scale).astype(BF16)
    normed_own = root_mean_norm(moved, gain_attn).astype(BF16)
    qkv_own = jnp.concatenate([w_query, key_weight, value_weight], axis=1)
    qkv_mat, out_mat, gate_mat, up_mat, down_mat, grad_y_all, normed = gather_all(
        sizes, 1, qkv_own, w_out.T, w_gate, w_up, w_down.T, grad_y_low, normed_own
    )
    qkv_mat = qkv_mat.reshape(model_width, -1)
    out_mat = out_mat.reshape(model_width, -1)
    gate_mat = gate_mat.reshape(model_width, -1)
    up_mat = up_mat.reshape(model_width, -1)
    down_mat = down_mat.reshape(model_width, -1)
    group_rows = GROUP * (seq_count // 2) * shard_len
    grad_y_all = grad_y_all.reshape(group_rows, model_width)
    normed = normed.reshape(row_len, model_width)
    query_width = w_query.shape[1]
    key_width = key_weight.shape[1]
    qkv_cuts = (query_width, query_width + key_width)
    qkv_lin = jnp.dot(normed, qkv_mat, preferred_element_type=F32)
    query_lin, key_linear, value_linear = jnp.split(qkv_lin, qkv_cuts, axis=1)
    query_rows = head_prep(query_lin, gain_query, position).astype(BF16)
    rotated_keys = head_prep(key_linear, gain_key, position).astype(BF16)
    value_heads = value_linear.astype(BF16).reshape(row_len, -1, head_size)
    attended, log_total = attend_forward(
        query_rows, rotated_keys, value_heads, segment, position, segment, position
    )
    projected = product(attended, out_mat, CONTRACT_COLS).astype(BF16)
    resid_rows = moved + scatter_seq(
        sizes, 2, projected.reshape(seq_count, shard_len, model_width)
    )
    normed_mlp_own = root_mean_norm(resid_rows, gain_mlp).astype(BF16)
    normed_mlp = gather_group(sizes, 3, normed_mlp_own).reshape(group_rows, model_width)
    gate = jnp.dot(normed_mlp, gate_mat, preferred_element_type=F32)
    upper = jnp.dot(normed_mlp, up_mat, preferred_element_type=F32)
    hidden = (jax.nn.silu(gate) * upper).astype(BF16)
    down_part = product(hidden, down_mat, CONTRACT_COLS).astype(BF16)
    grad_mid = jnp.dot(grad_y_all, down_mat, preferred_element_type=F32)
    silu_pull = jax.vjp(lambda gate_in, up_in: jax.nn.silu(gate_in) * up_in, gate, upper)[1]
    grad_gate_lin, grad_up_lin = silu_pull(grad_mid)
    grad_gate_low = grad_gate_lin.astype(BF16)
    grad_up_low = grad_up_lin.astype(BF16)
    grad_nmlp_part = (
        product(grad_gate_low, gate_mat, CONTRACT_COLS)
        + product(grad_up_low, up_mat, CONTRACT_COLS)
    ).astype(BF16)
    group_shape = (GROUP, seq_count // 2, shard_len, model_width)
    grad_nmlp = scatter_group(sizes, 4, grad_nmlp_part.reshape(group_shape))
    grad_down = product(grad_y_all, hidden, CONTRACT_ROWS).astype(BF16)
    grad_gate = product(normed_mlp, grad_gate_low, CONTRACT_ROWS).astype(BF16)
    grad_up = product(normed_mlp, grad_up_low, CONTRACT_ROWS).astype(BF16)
    mlp_pull = jax.vjp(root_mean_norm, resid_rows, gain_mlp)[1]
    grad_resid_part, grad_gain_mlp = mlp_pull(grad_nmlp)
    grad_resid = grad_y_low.astype(F32) + grad_resid_part
    grad_proj = gather_seq(sizes, 5, grad_resid.astype(BF16)).reshape(row_len, model_width)
    grad_w_out = product(grad_proj, attended, CONTRACT_ROWS).astype(BF16)
    grad_att = jnp.dot(grad_proj, out_mat, preferred_element_type=F32).astype(BF16)
    grad_queries, grad_keys, grad_values = attend_backward(
        query_rows,
        rotated_keys,
        value_heads,
        grad_att,
        log_total,
        segment,
        position,
        segment,
        position,
    )
    query_pull = jax.vjp(
        lambda flat, gain_in: head_prep(flat, gain_in, position), query_lin, gain_query
    )[1]
    grad_query_lin, grad_gain_query = query_pull(grad_queries)
    key_pull = jax.vjp(
        lambda flat, gain_in: head_prep(flat, gain_in, position), key_linear, gain_key
    )[1]
    grad_key_lin, grad_gain_key = key_pull(grad_keys)
    grad_qkv_low = jnp.concatenate(
        [
            grad_query_lin.astype(BF16),
            grad_key_lin.astype(BF16),
            grad_values.reshape(row_len, -1).astype(BF16),
        ],
        axis=1,
    )
    grad_normed_part = product(grad_qkv_low, qkv_mat, CONTRACT_COLS).astype(BF16)
    grad_normed = scatter_seq(
        sizes, 6, grad_normed_part.reshape(seq_count, shard_len, model_width)
    )
    grad_qkv = product(normed, grad_qkv_low, CONTRACT_ROWS).astype(BF16)
    attn_pull = jax.vjp(root_mean_norm, moved, gain_attn)[1]
    grad_moved_part, grad_gain_attn = attn_pull(grad_normed)
    grad_moved = (grad_resid + grad_moved_part).astype(BF16)
    gain_grads = lax.psum(
        jnp.concatenate([grad_gain_attn, grad_gain_mlp, grad_gain_query, grad_gain_key]),
        ("dp", "seq"),
    )
    back_out = product(recv_map, grad_moved, CONTRACT_ROWS).astype(BF16)
    (returned,) = exchange(sizes, 7, back_out.reshape(flat_blocks))
    grad_hidden = (
        jnp.where(keep_long[:, None], grad_moved.astype(F32), 0.0)
        + product(send_map, returned.reshape(high_dims), CONTRACT_ROWS)
    ).astype(BF16)
    out_qkv, out_wo, out_gate, out_up, out_down, down_sum = scatter_all(
        sizes, 8, grad_qkv, grad_w_out, grad_gate, grad_up, grad_down,
        down_part.reshape(group_shape),
    )
    mixed = ((resid_rows + down_sum) * live_scale).astype(BF16)
    out_query, out_key, out_value = jnp.split(out_qkv, qkv_cuts, axis=1)
    device = my_row * seq_count + my_part

    def own_piece(vector):
        size = vector.shape[0] // (row_count * seq_count)
        return lax.dynamic_slice_in_dim(vector, device * size, size)

    sum_attn, sum_mlp, sum_query, sum_key = [own_piece(v) for v in jnp.split(gain_grads, cuts)]
    return (
        mixed,
        grad_hidden,
        sum_attn,
        out_query,
        out_key,
        out_value,
        out_wo.T,
        sum_query,
        sum_key,
        sum_mlp,
        out_gate,
        out_up,
        out_down.T,
    )


def solution(mesh):
    in_specs = (
        P(("dp", "seq"), None),
        P(),
        P(),
        P(),
        P("dp"),
        P("dp", "seq"),
        P("dp", "seq"),
        P("dp", "seq"),
        P("seq", "dp"),
        P("dp"),
        P("dp"),
        P("dp"),
        P("dp", "seq"),
        P("dp", "seq"),
        P("seq", "dp"),
        P(("dp", "seq"), None),
    )
    out_specs = (
        P(("dp", "seq"), None),
        P(("dp", "seq"), None),
        P(("dp", "seq")),
        P("dp", "seq"),
        P("dp", "seq"),
        P("dp", "seq"),
        P("seq", "dp"),
        P(("dp", "seq")),
        P(("dp", "seq")),
        P(("dp", "seq")),
        P("dp", "seq"),
        P("dp", "seq"),
        P("seq", "dp"),
    )
    return jax.shard_map(
        functools.partial(per_device, (mesh.shape["dp"], mesh.shape["seq"])), mesh=mesh, in_specs=in_specs, out_specs=out_specs, check_vma=False
    )
```

```python
import functools
import math

import jax
import jax.numpy as jnp
from jax import lax
from jax.experimental import pallas as pl
from jax.experimental.pallas import tpu as pltpu
from jax.sharding import PartitionSpec as P

MAXSHORT = 4
GROUP = 4
MESH = pl.DeviceIdType.MESH
HBM = pl.BlockSpec(memory_space=pltpu.HBM)
VMEM = pl.BlockSpec(memory_space=pltpu.VMEM)
BF16 = jnp.bfloat16
F32 = jnp.float32


NORM_EPS = 1e-06
ROPE_BASE = 1000000.0
MASKED = -1e30
CONTRACT_ROWS = (((0,), (0,)), ((), ()))
CONTRACT_COLS = (((1,), (1,)), ((), ()))


def product(left, right, dims):
    return lax.dot_general(left, right, dims, preferred_element_type=jnp.float32)


def layout(lengths_part, perm_part, body_len):
    row_count, shorts = lengths_part.shape
    doc_total = row_count * shorts
    starts = body_len + jnp.cumsum(lengths_part, axis=1) - lengths_part
    kept_flat = lengths_part.reshape(doc_total)
    matched = perm_part[:, None] == jnp.arange(doc_total, dtype=jnp.int32)[None, :]
    placed = jnp.sum(jnp.where(matched, kept_flat[:, None], 0), axis=0).reshape(row_count, shorts)
    new_at = body_len + jnp.cumsum(placed, axis=1) - placed
    new_start = jnp.sum(jnp.where(matched, new_at.reshape(doc_total)[None, :], 0), axis=1)
    return (starts.reshape(doc_total), kept_flat, new_start, perm_part // shorts)


def slot_labels(
    kept_flat,
    new_start,
    dest_row,
    part,
    my_row,
    valid_here,
    body_len,
    shard_len,
    row_len,
    row_count,
):
    doc_total = kept_flat.shape[0]
    local = jnp.arange(shard_len, dtype=jnp.int32)
    doc_ids = jnp.arange(doc_total, dtype=jnp.int32)
    inside = (
        (dest_row == my_row)[None, :]
        & (local[:, None] >= new_start[None, :])
        & (local[:, None] < (new_start + kept_flat)[None, :])
    )
    offset = local[:, None] - new_start[None, :]
    in_short = jnp.any(inside, axis=1)
    short_seg = jnp.sum(
        jnp.where(inside, row_count + part * doc_total + doc_ids[None, :], 0), axis=1
    )
    short_pos = jnp.sum(jnp.where(inside, offset, 0), axis=1)
    long_pos = part * body_len + local
    in_long = (local < body_len) & (long_pos < valid_here)
    flat_slot = my_row * row_len + part * shard_len + local
    segment = jnp.where(in_long, my_row, jnp.where(in_short, short_seg, -1 - flat_slot))
    position = jnp.where(in_long, long_pos, short_pos)
    return (segment, position, in_long, in_short)


class Place:
    def __init__(self, dp_size, seq_size):
        self.dp_size = dp_size
        self.seq_size = seq_size
        self.high = dp_size // GROUP
        self.cores = seq_size // 2
        self.d = lax.axis_index("dp")
        self.s = lax.axis_index("seq")
        self.g = lax.rem(self.d, GROUP)
        self.h = lax.div(self.d, GROUP)
        self.x = lax.div(self.s, self.cores)
        self.c = lax.rem(self.s, self.cores)
        self.y = lax.rem(self.g, 2)
        self.l = lax.div(self.g, 2)
        self.gy = self.g + 1 - 2 * self.y
        self.gl = lax.rem(self.g + 2, GROUP)
        self.gd = 3 - self.g
        self.y_peer = (self.h * GROUP + self.gy, self.s)
        self.l_peer = (self.h * GROUP + self.gl, self.s)
        self.d_peer = (self.h * GROUP + self.gd, self.s)
        self.x_peer = (self.d, (1 - self.x) * self.cores + self.c)
        self.c_peer = (self.d, self.x * self.cores + 1 - self.c)

    def h_peer(self, step):
        return (lax.rem(self.h + step, self.high) * GROUP + self.g, self.s)

    def h_from(self, step):
        return lax.rem(self.h + self.high - step, self.high)

    def g_peer(self, step):
        return (self.h * GROUP + lax.rem(self.g + step, GROUP), self.s)


class Mover:
    def __init__(self, send_sems, recv_sems, local_sems):
        self.send_sems = send_sems
        self.recv_sems = recv_sems
        self.local_sems = local_sems
        self.count = 0
        self.local_count = 0
        self.sent = []

    def send(self, source, target, device):
        index = self.count
        self.count += 1
        copy = pltpu.make_async_remote_copy(
            src_ref=source,
            dst_ref=target,
            send_sem=self.send_sems.at[index],
            recv_sem=self.recv_sems.at[index],
            device_id=device,
            device_id_type=MESH,
        )
        copy.start()
        self.sent.append(copy)
        return copy

    def local(self, source, target):
        index = self.local_count
        self.local_count += 1
        copy = pltpu.make_async_copy(source, target, self.local_sems.at[index])
        copy.start()
        return copy

    def drain(self, copy):
        copy.wait_send()
        self.sent = [other for other in self.sent if other is not copy]

    def finish(self):
        for copy in self.sent:
            copy.wait_send()


def greet(peers):
    barrier = pltpu.get_barrier_semaphore()
    for peer in peers:
        pl.semaphore_signal(barrier, inc=1, device_id=peer, device_id_type=MESH)
    pl.semaphore_wait(barrier, len(peers))


def dp_peers(place):
    return [
        (lax.rem(place.d + step, place.dp_size), place.s) for step in range(1, place.dp_size)
    ]


def sems(count, local):
    return [
        pltpu.SemaphoreType.DMA((count,)),
        pltpu.SemaphoreType.DMA((count,)),
        pltpu.SemaphoreType.DMA((max(local, 1),)),
    ]


def comm_params(collective_id, vmem=None):
    return pltpu.CompilerParams(
        collective_id=collective_id,
        has_side_effects=True,
        vmem_limit_bytes=vmem if vmem is not None else 60 * 1024 * 1024,
    )


def add_rows(target, terms, rows, chunk):
    def step(index, carry):
        part = pl.ds(pl.multiple_of(index * chunk, chunk), chunk)
        total = terms[0][part, :].astype(F32)
        for term in terms[1:]:
            total = total + term[part, :].astype(F32)
        target[part, :] = total.astype(target.dtype)
        return carry

    lax.fori_loop(0, rows // chunk, step, 0)


class GatherSeq:
    sends = 3

    def __init__(self, place, mover, own, full):
        self.place, self.mover, self.full = place, mover, full
        self.local = mover.local(own, full.at[place.s])
        self.over_x = mover.send(own, full.at[place.s], place.x_peer)
        self.over_c = mover.send(own, full.at[place.s], place.c_peer)

    def forward(self):
        self.over_x.wait_recv()
        block = self.full.at[self.place.x_peer[1]]
        self.passed = self.mover.send(block, block, self.place.c_peer)

    def finish(self):
        self.local.wait()
        self.over_c.wait_recv()
        self.passed.wait_recv()


class GatherGroup:
    sends = 10

    def __init__(self, place, mover, own, full):
        self.place, self.mover, self.full = place, mover, full
        half = own.shape[0] // 2
        self.low, self.top = pl.ds(0, half), pl.ds(half, half)
        self.local = mover.local(own, full.at[place.g, place.c])
        spot = full.at[place.g, place.c]
        self.y_low = mover.send(own.at[self.low], spot.at[self.low], place.y_peer)
        self.l_top = mover.send(own.at[self.top], spot.at[self.top], place.l_peer)
        self.y_top = mover.send(own.at[self.top], spot.at[self.top], place.y_peer)
        self.l_low = mover.send(own.at[self.low], spot.at[self.low], place.l_peer)
        self.core = [mover.send(own, spot, place.c_peer)]

    def forward(self):
        place, mover, full = self.place, self.mover, self.full
        self.y_low.wait_recv()
        part = full.at[place.gy, place.c, self.low]
        self.d_low = mover.send(part, part, place.l_peer)
        self.l_top.wait_recv()
        part = full.at[place.gl, place.c, self.top]
        self.d_top = mover.send(part, part, place.y_peer)
        self.y_top.wait_recv()
        part = full.at[place.gy, place.c]
        self.core.append(mover.send(part, part, place.c_peer))
        self.l_low.wait_recv()
        part = full.at[place.gl, place.c]
        self.core.append(mover.send(part, part, place.c_peer))

    def finish_ici(self):
        place = self.place
        self.d_low.wait_recv()
        self.d_top.wait_recv()
        part = self.full.at[place.gd, place.c]
        self.core.append(self.mover.send(part, part, place.c_peer))

    def finish(self):
        self.local.wait()
        for copy in self.core:
            copy.wait_recv()


class GatherDp:
    def __init__(self, place, mover, pieces, full):
        self.place, self.mover, self.full = place, mover, full
        first, last = pieces[0], pieces[-1]
        self.window = pl.ds(first[1], last[1] + last[2] - first[1])
        self.rows = full.shape[0] // place.dp_size
        self.local, self.over_h, self.over_l, self.over_y = [], [], [], []
        own_rows = self.block(place.d)
        high_sends = [[] for _ in range(1, place.high)]
        l_own, y_own = [], []
        for own, start, size in pieces:
            spot = full.at[own_rows, pl.ds(start, size)]
            for step in range(1, place.high):
                high_sends[step - 1].append(mover.send(own, spot, place.h_peer(step)))
            l_own.append(mover.send(own, spot, place.l_peer))
            y_own.append(mover.send(own, spot, place.y_peer))
            self.local.append(mover.local(own, spot))
        self.over_h = high_sends
        self.over_l = [l_own]
        self.over_y = y_own

    def block(self, index):
        return pl.ds(pl.multiple_of(index * self.rows, self.rows), self.rows)

    def forward_high(self):
        place = self.place
        for step, copies in enumerate(self.over_h, 1):
            for copy in copies:
                copy.wait_recv()
            part = self.full.at[self.block(place.h_from(step) * GROUP + place.g), self.window]
            self.over_l.append([self.mover.send(part, part, place.l_peer)])
            self.over_y.append(self.mover.send(part, part, place.y_peer))

    def forward_l(self):
        place = self.place
        for step, copies in enumerate(self.over_l):
            for copy in copies:
                copy.wait_recv()
            high = place.h if step == 0 else place.h_from(step)
            part = self.full.at[self.block(high * GROUP + place.gl), self.window]
            self.over_y.append(self.mover.send(part, part, place.y_peer))

    def finish(self):
        for copy in self.local:
            copy.wait()
        for copy in self.over_y:
            copy.wait_recv()


class GatherColumns:
    def __init__(self, place, mover, own, full):
        self.place, self.mover, self.full = place, mover, full
        self.quarter = own.shape[1] // GROUP
        self.near = pl.ds(0, self.quarter)
        self.far = pl.ds(self.quarter, self.quarter)
        self.over_g = []
        spot = full.at[place.h, place.g, :, self.near]
        for step in (3, 1, 2):
            to = lax.rem(place.g + step, GROUP)
            columns = pl.ds(pl.multiple_of(to * self.quarter, self.quarter), self.quarter)
            self.over_g.append(mover.send(own.at[:, columns], spot, place.g_peer(step)))
        columns = pl.ds(pl.multiple_of(place.g * self.quarter, self.quarter), self.quarter)
        self.local = mover.local(own.at[:, columns], spot)

    def forward_g(self):
        place = self.place
        self.local.wait()
        for copy in self.over_g:
            copy.wait_recv()
        near = self.full.at[place.h, :, :, self.near]
        far = self.full.at[place.h, :, :, self.far]
        self.over_h = [
            self.mover.send(near, near, place.h_peer(step)) for step in range(1, place.high)
        ]
        self.over_x = [self.mover.send(near, far, place.x_peer)]

    def forward_high(self):
        place = self.place
        for step, copy in enumerate(self.over_h, 1):
            copy.wait_recv()
            high = place.h_from(step)
            self.over_x.append(
                self.mover.send(
                    self.full.at[high, :, :, self.near],
                    self.full.at[high, :, :, self.far],
                    place.x_peer,
                )
            )

    def finish(self):
        for copy in self.over_x:
            copy.wait_recv()


def lane_swap(values):
    half = values.shape[-1] // 2
    return jnp.concatenate([values[:, half:], values[:, :half]], axis=-1)


def norm_rows(values, gain):
    scale = lax.rsqrt(jnp.mean(values * values, axis=-1, keepdims=True) + NORM_EPS)
    return values * scale * gain


def forward_kernel(sizes, *refs):
    (hidden, keep, send_maps, recv_maps, gain_row, cosine, sine, seg_col, pos_col, seg_row,
     pos_row, out_grad, live, wq, wk, wv, wo, wg, wu, wd) = refs[:20]
    (moved, gains, normed, full_qkv, full_wo, full_g, full_u, full_d, grad_y, lin, rot, attended,
     log_total, resid, full_nm) = refs[20:35]
    (blocks_out, blocks_in, rows_in, normed_own, bias, part_own, from_c, from_x, to_c,
     nm_own, send_sems, recv_sems, local_sems) = refs[35:]
    place = Place(*sizes)
    mover = Mover(send_sems, recv_sems, local_sems)
    tokens, width = hidden.shape
    head = cosine.shape[1]
    query_width, key_width = wq.shape[1], wk.shape[1]
    columns = width // GROUP
    parts = sizes[1]
    repeat = query_width // key_width

    for q in range(GROUP):
        lanes = pl.ds(q * columns, columns)
        piece = jnp.dot(send_maps[q], hidden[:, lanes], preferred_element_type=F32)
        if q == 0:
            total = piece
        else:
            total = total + piece
    blocks_out[...] = total.astype(BF16).reshape(blocks_out.shape)
    greet(dp_peers(place) + [place.x_peer, place.c_peer])
    copies = []
    for step in range(1, place.dp_size):
        other = lax.rem(place.d + step, place.dp_size)
        copies.append(mover.send(blocks_out.at[other], blocks_in.at[place.d], (other, place.s)))
        copies.append(mover.send(gain_row, rows_in.at[place.d], (other, place.s)))
    key_parts = [(wk, query_width, key_width), (wv, query_width + key_width, key_width)]
    attn = [
        GatherDp(place, mover, [(wq, 0, query_width)], full_qkv),
        GatherDp(place, mover, key_parts, full_qkv),
    ]
    mlp = [GatherColumns(place, mover, wg, full_g)]
    attn.append(GatherDp(place, mover, [(wo, 0, wo.shape[1])], full_wo))
    mlp.append(GatherColumns(place, mover, wu, full_u))
    mlp.append(GatherColumns(place, mover, wd, full_d))
    blocks_in[place.d] = blocks_out[place.d]
    rows_in[place.d] = gain_row[...]
    for copy in copies:
        copy.wait_recv()
    all_gains = rows_in[0]
    for index in range(1, place.dp_size):
        all_gains = all_gains + rows_in[index]
    gains[...] = all_gains
    incoming = blocks_in[...].reshape(place.dp_size * 16, columns)
    for q in range(GROUP):
        lanes = pl.ds(q * columns, columns)
        here = jnp.dot(recv_maps[q], incoming, preferred_element_type=F32)
        here = here + jnp.where(keep[...] > 0.0, hidden[:, lanes].astype(F32), 0.0)
        moved[:, lanes] = here.astype(BF16)

    def norm_moved(index, carry):
        rows = pl.ds(pl.multiple_of(index * 32, 32), 32)
        normed_own[rows, :] = norm_rows(moved[rows, :].astype(F32), gains[:, :width]).astype(BF16)
        grad_y[rows, :] = (out_grad[rows, :].astype(F32) * live[rows, :]).astype(BF16)
        return carry

    lax.fori_loop(0, tokens // 32, norm_moved, 0)
    row = GatherSeq(place, mover, normed_own, normed)
    attn[0].forward_high()
    mlp[0].forward_g()
    attn[1].forward_high()
    attn[0].forward_l()
    row.forward()
    attn[1].forward_l()
    mlp[1].forward_g()
    attn[2].forward_high()
    mlp[2].forward_g()
    attn[2].forward_l()
    row.finish()
    attn[0].finish()
    attn[1].finish()

    gain_query = gains[:, 2 * width : 2 * width + head]
    gain_key = gains[:, 2 * width + head : 2 * width + 2 * head]
    rotated = query_width + key_width
    tile = 2 * head

    def project(part, carry):
        spots = pl.ds(pl.multiple_of(part * tokens, tokens), tokens)
        source = normed[part]
        cos_part, sin_part = cosine[spots, :], sine[spots, :]
        for start in range(0, rotated + key_width, tile):
            result = jnp.dot(source, full_qkv[:, start : start + tile], preferred_element_type=F32)
            if start < rotated:
                lin[spots, start : start + tile] = result.astype(BF16)
                gain = gain_query if start < query_width else gain_key
                for inner in (0, head):
                    unit = norm_rows(result[:, inner : inner + head], gain)
                    turned = unit * cos_part + lane_swap(unit) * sin_part
                    rot[spots, start + inner : start + inner + head] = turned.astype(BF16)
            else:
                rot[spots, start : start + tile] = result.astype(BF16)
        return carry

    lax.fori_loop(0, parts, project, 0)
    mlp[0].forward_high()
    scale = head ** (-0.5)
    for part in range(parts):
        keys = (part + 1) * tokens
        spots = pl.ds(part * tokens, tokens)
        allowed = (seg_col[spots, :] == seg_row[:, :keys]) & (pos_row[:, :keys] <= pos_col[spots, :])
        some = jnp.where(allowed, 0.0, MASKED)
        for copy in range(repeat):
            bias[copy * tokens : (copy + 1) * tokens, :keys] = some

        def attend(pair, carry):
            key_lanes = pl.ds(pl.multiple_of(query_width + pair * head, head), head)
            value_lanes = pl.ds(pl.multiple_of(rotated + pair * head, head), head)
            query_lanes = [
                pl.ds(pl.multiple_of((pair * repeat + copy) * head, head), head)
                for copy in range(repeat)
            ]
            queries = jnp.concatenate([rot[spots, lanes] for lanes in query_lanes], axis=0)
            scores = product(queries, rot[:keys, key_lanes], CONTRACT_COLS) * scale
            scores = scores + bias[:, :keys]
            peak = jnp.max(scores, axis=-1, keepdims=True)
            expd = jnp.exp(scores - peak)
            weight = jnp.sum(expd, axis=-1, keepdims=True)
            probs = (expd / weight).astype(BF16)
            log_total[pair, part] = peak + jnp.log(weight)
            context = jnp.dot(probs, rot[:keys, value_lanes], preferred_element_type=F32)
            for copy in range(repeat):
                attended[spots, query_lanes[copy]] = context[
                    copy * tokens : (copy + 1) * tokens
                ].astype(BF16)
            return carry

        lax.fori_loop(0, key_width // head, attend, 0)
    mlp[1].forward_high()
    attn[2].finish()

    def project_out(part, target):
        source = attended[pl.ds(pl.multiple_of(part * tokens, tokens), tokens), :]

        def step(index, carry):
            block = pl.ds(pl.multiple_of(index * 256, 256), 256)
            target[:, block] = product(source, full_wo[block, :], CONTRACT_COLS).astype(BF16)
            return carry

        lax.fori_loop(0, width // 256, step, 0)

    cores = place.cores
    places = ((1 - place.x) * cores, place.x * cores)
    project_out(places[0] + 1 - place.c, to_c.at[0])
    over_c = [mover.send(to_c.at[0], from_c.at[0], place.c_peer)]
    project_out(places[0] + place.c, part_own.at[0])
    over_c[0].wait_recv()
    add_rows(part_own.at[0], [part_own.at[0], from_c.at[0]], tokens, 32)
    over_x = mover.send(part_own.at[0], from_x, place.x_peer)
    project_out(places[1] + 1 - place.c, to_c.at[1])
    over_c.append(mover.send(to_c.at[1], from_c.at[1], place.c_peer))
    project_out(places[1] + place.c, part_own.at[1])
    mlp[2].forward_high()
    over_c[1].wait_recv()
    over_x.wait_recv()

    def norm_resid(index, carry):
        rows = pl.ds(pl.multiple_of(index * 32, 32), 32)
        total = moved[rows, :].astype(F32) + part_own[1, rows, :].astype(F32)
        total = total + from_c[1, rows, :].astype(F32) + from_x[rows, :].astype(F32)
        resid[rows, :] = total
        nm_own[rows, :] = norm_rows(total, gains[:, width : 2 * width]).astype(BF16)
        return carry

    lax.fori_loop(0, tokens // 32, norm_resid, 0)
    group = GatherGroup(place, mover, nm_own, full_nm)
    group.forward()
    group.finish_ici()
    for part in [group] + mlp:
        part.finish()
    mover.finish()


def forward(sizes, collective_id, head_size, args):
    dp_size, seq_size = sizes
    hidden, wq, wk, wo, wg = args[0], args[13], args[14], args[16], args[17]
    tokens, width = hidden.shape
    high = dp_size // GROUP
    rows = wq.shape[0]
    row_len = seq_size * tokens
    rotated = wq.shape[1] + wk.shape[1]
    wide = (high, GROUP, rows, wg.shape[1] // 2)
    group = (GROUP, seq_size // 2, tokens, width)
    heads = wq.shape[1] // head_size
    gain_width = args[4].shape[1]
    outs = [
        ((tokens, width), BF16, VMEM),
        ((1, gain_width), F32, VMEM),
        ((seq_size, tokens, width), BF16, VMEM),
        ((width, rotated + wk.shape[1]), BF16, VMEM),
        ((width, wo.shape[1]), BF16, VMEM),
        (wide, BF16, HBM),
        (wide, BF16, HBM),
        (wide, BF16, HBM),
        ((tokens, width), BF16, VMEM),
        ((row_len, rotated), BF16, VMEM),
        ((row_len, rotated + wk.shape[1]), BF16, VMEM),
        ((row_len, wq.shape[1]), BF16, VMEM),
        ((wk.shape[1] // head_size, seq_size, heads * head_size // wk.shape[1] * tokens, 1), F32, VMEM),
        ((tokens, width), F32, VMEM),
        (group, BF16, HBM),
    ]
    scratch = [
        pltpu.VMEM((dp_size, 16, width // GROUP), BF16),
        pltpu.VMEM((dp_size, 16, width // GROUP), BF16),
        pltpu.VMEM((dp_size, 1, gain_width), F32),
        pltpu.VMEM((tokens, width), BF16),
        pltpu.VMEM((wq.shape[1] // wk.shape[1] * tokens, row_len), F32),
        pltpu.VMEM((2, tokens, width), BF16),
        pltpu.VMEM((2, tokens, width), BF16),
        pltpu.VMEM((tokens, width), BF16),
        pltpu.VMEM((2, tokens, width), BF16),
        pltpu.VMEM((tokens, width), BF16),
    ]
    sends = 2 * (dp_size - 1) + 4 * (high + 1) + 9 * high
    sends += 3 * (3 + 2 * high) + 2 * GatherGroup.sends + GatherSeq.sends + 3
    return pl.pallas_call(
        functools.partial(forward_kernel, sizes),
        out_shape=[jax.ShapeDtypeStruct(shape, dtype) for shape, dtype, _ in outs],
        in_specs=[VMEM] * 13 + [HBM] * 7,
        out_specs=[spec for _, _, spec in outs],
        scratch_shapes=scratch + sems(sends, 16),
        compiler_params=comm_params(collective_id),
        name="forward_attention",
    )(*args)


class ScatterColumns:
    sends = GROUP
    pieces = 4

    @staticmethod
    def scratch(high, rows, quarter):
        group_rows = GROUP * rows
        return [
            pltpu.VMEM((high * group_rows, quarter), BF16),
            pltpu.VMEM((max(high - 1, 1), group_rows, quarter), BF16),
            pltpu.VMEM((GROUP - 1, rows, quarter), BF16),
        ]

    def __init__(self, place, mover, parts, from_x, from_h, from_g):
        self.place, self.mover, self.parts = place, mover, parts
        self.from_x, self.from_h, self.from_g = from_x, from_h, from_g
        self.group_rows = from_h.shape[1]
        self.quarter = from_x.shape[1]

    def start(self):
        quarter = self.quarter
        far = self.parts.at[:, pl.ds(quarter, quarter)]
        self.over_x = self.mover.send(far, self.from_x, self.place.x_peer)

    def forward_x(self, stage):
        place, mover, total = self.place, self.mover, self.from_x
        rows = total.shape[0] // self.pieces
        near = pl.ds(0, self.quarter)

        def load(index):
            block = pl.ds(index * rows, rows)
            return mover.local(self.parts.at[block, near], stage.at[index % 2])

        copies = [load(0)]
        self.over_x.wait_recv()
        for index in range(self.pieces):
            if index + 1 < self.pieces:
                copies.append(load(index + 1))
            copies[index].wait()
            part = total.at[pl.ds(index * rows, rows)]
            add_rows(part, [part, stage.at[index % 2]], rows, 64)
        self.over_h = []
        for step in range(1, place.high):
            high = lax.rem(place.h + step, place.high)
            block = pl.ds(pl.multiple_of(high * self.group_rows, self.group_rows), self.group_rows)
            self.over_h.append(
                mover.send(total.at[block], self.from_h.at[step - 1], place.h_peer(step))
            )

    def block(self, index):
        rows = self.group_rows // GROUP
        return pl.ds(
            pl.multiple_of(self.place.h * self.group_rows + index * rows, rows), rows
        )

    def forward_high(self):
        place = self.place
        own_rows = pl.ds(
            pl.multiple_of(place.h * self.group_rows, self.group_rows), self.group_rows
        )
        for copy in self.over_h:
            copy.wait_recv()
        mine = self.from_x.at[own_rows]
        terms = [mine] + [self.from_h.at[step] for step in range(place.high - 1)]
        add_rows(mine, terms, self.group_rows, 64)
        self.over_g = []
        for step in (3, 1, 2):
            block = self.block(lax.rem(place.g + step, GROUP))
            self.over_g.append(
                (
                    step,
                    self.mover.send(
                        self.from_x.at[block], self.from_g.at[step - 1], place.g_peer(step)
                    ),
                )
            )

    def finish(self, stage, out):
        place, quarter = self.place, self.quarter
        columns = pl.ds(pl.multiple_of(place.g * quarter, quarter), quarter)
        stage[:, columns] = self.from_x[self.block(place.g), :].astype(F32)
        for step, copy in self.over_g:
            copy.wait_recv()
            source = lax.rem(place.g + GROUP - step, GROUP)
            columns = pl.ds(pl.multiple_of(source * quarter, quarter), quarter)
            stage[:, columns] = self.from_g[step - 1].astype(F32)
        self.mover.local(stage, out).wait()


class ScatterDp:
    @staticmethod
    def sends(high):
        return 2 * high + high + high - 1

    @staticmethod
    def scratch(high, rows, width):
        return [
            pltpu.VMEM((2, high, rows, width), BF16),
            pltpu.VMEM((high, rows, width), BF16),
            pltpu.VMEM((max(high - 1, 1), rows, width), BF16),
        ]

    def __init__(self, place, mover, parts, out, from_y, from_l, from_h):
        self.place, self.mover, self.parts, self.out = place, mover, parts, out
        self.from_y, self.from_l, self.from_h = from_y, from_l, from_h
        self.rows = out.shape[0]

    def block(self, high, l_index, y_index):
        index = high * GROUP + l_index * 2 + y_index
        return self.parts.at[pl.ds(pl.multiple_of(index * self.rows, self.rows), self.rows)]

    def start(self):
        place = self.place
        self.owners = (1 - place.l, place.l)
        self.over_y = []
        for index, l_owner in enumerate(self.owners):
            for high in range(place.high):
                source = self.block(high, l_owner, 1 - place.y)
                self.over_y.append(
                    self.mover.send(source, self.from_y.at[index, high], place.y_peer)
                )

    def ready(self, index, extra=None):
        place = self.place
        for high in range(place.high):
            self.over_y[index * place.high + high].wait_recv()
            mine = self.block(high, self.owners[index], place.y)
            terms = [mine, self.from_y.at[index, high]]
            if extra is not None:
                extra[high].wait_recv()
                terms.append(self.from_l.at[high])
            add_rows(mine, terms, self.rows, 32)

    def forward_y(self):
        place = self.place
        self.ready(0)
        self.over_l = []
        for high in range(place.high):
            source = self.block(high, 1 - place.l, place.y)
            self.over_l.append(self.mover.send(source, self.from_l.at[high], place.l_peer))

    def forward_l(self):
        place = self.place
        self.ready(1, self.over_l)
        self.over_h = []
        for step in range(1, place.high):
            source = self.block(lax.rem(place.h + step, place.high), place.l, place.y)
            self.over_h.append(
                self.mover.send(source, self.from_h.at[step - 1], place.h_peer(step))
            )

    def finish(self):
        place = self.place
        for copy in self.over_h:
            copy.wait_recv()
        terms = [self.block(place.h, place.l, place.y)]
        terms += [self.from_h.at[step] for step in range(place.high - 1)]
        add_rows(self.out, terms, self.rows, 32)


class ScatterGroup:
    sends = 10

    @staticmethod
    def scratch(rows, width):
        return [
            pltpu.VMEM((GROUP, rows, width), BF16),
            pltpu.VMEM((6, rows // 2, width), BF16),
        ]

    def __init__(self, place, mover, parts, from_c, landed):
        self.place, self.mover, self.parts = place, mover, parts
        self.from_c, self.landed = from_c, landed
        self.owners = (place.gd, place.gy, place.gl, place.g)
        self.over_c = []
        half = from_c.shape[1] // 2
        self.low, self.top = pl.ds(0, half), pl.ds(half, half)

    def start(self, index):
        place = self.place
        source = self.parts.at[self.owners[index], 1 - place.c]
        self.over_c.append(self.mover.send(source, self.from_c.at[index], place.c_peer))

    def forward(self, index):
        place, mover, sums, landed = self.place, self.mover, self.from_c, self.landed
        low, top = self.low, self.top
        self.over_c[index].wait_recv()
        total = sums.at[index]
        own = self.parts.at[self.owners[index], place.c]
        add_rows(total, [total, own], total.shape[0], 32)
        if index == 0:
            self.y_diag = mover.send(sums.at[0, low], landed.at[0], place.y_peer)
            self.l_diag = mover.send(sums.at[0, top], landed.at[1], place.l_peer)
        if index == 1:
            self.y_own = mover.send(sums.at[1, low], landed.at[2], place.y_peer)
        if index == 2:
            self.l_own = mover.send(sums.at[2, top], landed.at[3], place.l_peer)

    def forward_diag(self):
        place, mover, sums, landed = self.place, self.mover, self.from_c, self.landed
        half = sums.shape[1] // 2
        low, top = self.low, self.top
        self.y_diag.wait_recv()
        add_rows(sums.at[2, low], [sums.at[2, low], landed.at[0]], half, 32)
        self.l_last = mover.send(sums.at[2, low], landed.at[4], place.l_peer)
        self.l_diag.wait_recv()
        add_rows(sums.at[1, top], [sums.at[1, top], landed.at[1]], half, 32)
        self.y_last = mover.send(sums.at[1, top], landed.at[5], place.y_peer)

    def finish(self, take):
        half = self.from_c.shape[1] // 2
        chunk = 32
        self.y_own.wait_recv()
        self.l_last.wait_recv()
        self.l_own.wait_recv()
        self.y_last.wait_recv()
        for base, first, second in ((0, 2, 4), (half, 3, 5)):

            def step(index, carry):
                rows = pl.ds(pl.multiple_of(base + index * chunk, chunk), chunk)
                inner = pl.ds(pl.multiple_of(index * chunk, chunk), chunk)
                total = self.from_c[3, rows, :].astype(F32)
                total = total + self.landed[first, inner, :].astype(F32)
                take(rows, total + self.landed[second, inner, :].astype(F32))
                return carry

            lax.fori_loop(0, half // chunk, step, 0)


def norm_back(values, gain, cotangent):
    scale = lax.rsqrt(jnp.mean(values * values, axis=-1, keepdims=True) + NORM_EPS)
    weighted = cotangent * gain
    inner = jnp.mean(weighted * values, axis=-1, keepdims=True)
    unit = values * scale
    return scale * (weighted - unit * (scale * inner)), cotangent * unit


def feed_forward_kernel(sizes, *refs):
    nm_hbm, wg_hbm, wu_hbm, wd_hbm, grad_y, resid, live, gains = refs[:8]
    mixed, grad_resid, full_proj, gain_sum, out_gd, out_gg, out_gu = refs[8:15]
    (nm, gy, wg, wu, wd, hidden, gate_grad, up_grad, part_nmlp, part_down, nmlp_c, nmlp_landed,
     down_c, down_landed, grad_proj, stage) = refs[15:31]
    send_sems, recv_sems, local_sems = refs[31:]
    place = Place(*sizes)
    mover = Mover(send_sems, recv_sems, local_sems)
    tokens, width = resid.shape
    cores = place.cores
    block = cores * tokens
    inner = wg.shape[1]
    tile = 256
    loads = [mover.local(wg_hbm, wg), mover.local(wu_hbm, wu)]
    nm_loads = [mover.local(nm_hbm.at[index], nm.at[index]) for index in range(GROUP)]
    wd_load = mover.local(wd_hbm, wd)
    greet([place.y_peer, place.l_peer, place.c_peer, place.x_peer])
    gather = GatherGroup(place, mover, grad_y, gy)
    gain_sum[...] = jnp.zeros_like(gain_sum)
    for copy in loads:
        copy.wait()

    def gate_up(index, carry):
        source = nm[index].reshape(block, width)
        rows = pl.ds(pl.multiple_of(index * block, block), block)
        for start in range(0, inner, tile):
            lanes = slice(start, start + tile)
            gate = jnp.dot(source, wg[:, lanes], preferred_element_type=F32)
            upper = jnp.dot(source, wu[:, lanes], preferred_element_type=F32)
            gain = 1.0 / (1.0 + jnp.exp(-gate))
            silu = gate * gain
            hidden[rows, lanes] = (silu * upper).astype(BF16)
            up_grad[rows, lanes] = silu.astype(BF16)
            gate_grad[rows, lanes] = (upper * (gain + silu * (1.0 - gain))).astype(BF16)
        return carry

    nm_loads[0].wait()
    nm_loads[1].wait()
    lax.fori_loop(0, 2, gate_up, 0)
    gather.forward()
    nm_loads[2].wait()
    nm_loads[3].wait()
    lax.fori_loop(2, GROUP, gate_up, 0)
    gather.finish_ici()
    wd_load.wait()

    def down_block(owner):
        rows = pl.ds(pl.multiple_of(owner * block, block), block)

        def step(index, carry):
            lanes = pl.ds(pl.multiple_of(index * tile, tile), tile)
            result = product(hidden[rows, :], wd[lanes, :], CONTRACT_COLS).astype(BF16)
            part_down[owner, :, :, lanes] = result.reshape(cores, tokens, tile)
            return carry

        lax.fori_loop(0, width // tile, step, 0)

    down = ScatterGroup(place, mover, part_down, down_c, down_landed)
    down_block(down.owners[0])
    down_block(down.owners[1])
    gather.finish()

    def back_block(owner):
        rows = pl.ds(pl.multiple_of(owner * block, block), block)
        source = gy[owner].reshape(block, width)
        for start in range(0, inner, tile):
            lanes = slice(start, start + tile)
            grad_mid = jnp.dot(source, wd[:, lanes], preferred_element_type=F32)
            gate_grad[rows, lanes] = (grad_mid * gate_grad[rows, lanes].astype(F32)).astype(BF16)
            up_grad[rows, lanes] = (grad_mid * up_grad[rows, lanes].astype(F32)).astype(BF16)

        def step(index, carry):
            lanes = pl.ds(pl.multiple_of(index * tile, tile), tile)
            result = product(gate_grad[rows, :], wg[lanes, :], CONTRACT_COLS)
            result = result + product(up_grad[rows, :], wu[lanes, :], CONTRACT_COLS)
            part_nmlp[owner, :, :, lanes] = result.astype(BF16).reshape(cores, tokens, tile)
            return carry

        lax.fori_loop(0, width // tile, step, 0)

    nmlp = ScatterGroup(place, mover, part_nmlp, nmlp_c, nmlp_landed)
    back_block(nmlp.owners[0])
    nmlp.start(0)
    back_block(nmlp.owners[1])
    nmlp.start(1)
    nmlp.forward(0)
    back_block(nmlp.owners[2])
    nmlp.start(2)
    nmlp.forward(1)
    back_block(nmlp.owners[3])
    nmlp.start(3)
    nmlp.forward(2)
    down_block(down.owners[2])
    nmlp.forward(3)
    nmlp.forward_diag()
    down_block(down.owners[3])
    for index in range(GROUP):
        down.start(index)

    def weight_grad(grad, source, target):
        copies = []
        tiles = width // tile
        for index in range(tiles):
            lanes = pl.ds(index * tile, tile)
            left = source[:, :, :, lanes].reshape(GROUP * block, tile)
            if index >= 2:
                copies[index - 2].wait()
            stage[index % 2] = product(left, grad[...], CONTRACT_ROWS).astype(BF16)
            copies.append(mover.local(stage.at[index % 2], target.at[lanes]))
        copies[-2].wait()
        copies[-1].wait()

    def back_mlp(rows, total):
        grad, terms = norm_back(resid[rows, :], gains[:, width : 2 * width], total)
        grad = grad + grad_y[rows, :].astype(F32)
        grad_resid[rows, :] = grad
        grad_proj[rows, :] = grad.astype(BF16)
        gain_sum[...] += jnp.sum(terms, axis=0, keepdims=True)

    def mix(rows, total):
        mixed[rows, :] = ((resid[rows, :] + total) * live[rows, :]).astype(BF16)

    weight_grad(hidden, gy, out_gd)
    nmlp.finish(back_mlp)
    row = GatherSeq(place, mover, grad_proj, full_proj)
    for index in range(GROUP):
        down.forward(index)
    weight_grad(gate_grad, nm, out_gg)
    down.forward_diag()
    row.forward()
    weight_grad(up_grad, nm, out_gu)
    down.finish(mix)
    row.finish()
    mover.finish()


def feed_forward(sizes, collective_id, args):
    dp_size, seq_size = sizes
    nm, wg, resid, gains = args[0], args[1], args[5], args[7]
    tokens, width = resid.shape
    inner = wg.shape[1]
    rows = GROUP * (seq_size // 2) * tokens
    outs = [
        ((tokens, width), BF16, VMEM),
        ((tokens, width), F32, VMEM),
        ((seq_size, tokens, width), BF16, HBM),
        ((1, width), F32, VMEM),
        ((width, inner), BF16, HBM),
        ((width, inner), BF16, HBM),
        ((width, inner), BF16, HBM),
    ]
    scratch = [pltpu.VMEM(nm.shape, BF16)] * 2
    scratch += [pltpu.VMEM((width, inner), BF16)] * 3
    scratch += [pltpu.VMEM((rows, inner), BF16)] * 3
    scratch += [pltpu.VMEM(nm.shape, BF16)] * 2
    scratch += ScatterGroup.scratch(tokens, width) * 2
    scratch += [pltpu.VMEM((tokens, width), BF16), pltpu.VMEM((2, 256, inner), BF16)]
    sends = 3 * 10 + GatherSeq.sends
    local = 9 + 3 * (width // 256)
    return pl.pallas_call(
        functools.partial(feed_forward_kernel, sizes),
        out_shape=[jax.ShapeDtypeStruct(shape, dtype) for shape, dtype, _ in outs],
        in_specs=[HBM] * 4 + [VMEM] * 4,
        out_specs=[spec for _, _, spec in outs],
        scratch_shapes=scratch + sems(sends, local),
        compiler_params=comm_params(collective_id, 63 * 1024 * 1024),
        name="feed_forward",
    )(*args)


def backward_kernel(sizes, *refs):
    (part_gd, part_gg, part_gu, wo, grad_resid, full_proj, moved, keep, gain_mlp, gains, cosine,
     sine, seg_col, pos_col, seg_row, pos_row, log_row, normed, full_qkv, lin, rot, attended,
     recv_maps_t, send_maps_t) = refs[:24]
    grad_hidden, gain_sums, out_gd, out_gg, out_gu, out_qkv, out_wo = refs[24:31]
    send_sems, recv_sems, local_sems = refs[-3:]
    scratch = list(refs[31:-3])

    def take(count):
        taken = scratch[:count]
        del scratch[:count]
        return taken

    place = Place(*sizes)
    mover = Mover(send_sems, recv_sems, local_sems)
    tokens, width = moved.shape
    parts = sizes[1]
    head = cosine.shape[1]
    query_width = attended.shape[1]
    key_width = (rot.shape[1] - query_width) // 2
    rotated = query_width + key_width
    columns = width // GROUP
    repeat = query_width // key_width
    column_stage, out_stage = take(2)
    grad_wo, grad_key, grad_query = take(3)
    mlp = [
        ScatterColumns(place, mover, part, *take(3)) for part in (part_gd, part_gg, part_gu)
    ]
    wo_sum = ScatterDp(place, mover, grad_wo, out_wo, *take(3))
    key_sum = ScatterDp(place, mover, grad_key, out_qkv.at[:, pl.ds(query_width, 2 * key_width)], *take(3))
    query_sum = ScatterDp(place, mover, grad_query, out_qkv.at[:, pl.ds(0, query_width)], *take(3))
    grad_moved, to_c, from_c, from_x = take(4)
    grad_att, grad_keys, grad_values, grad_lin, bias = take(5)
    blocks_out, blocks_in, rows_in, row_c, row_x = take(5)

    greet(dp_peers(place) + [place.x_peer, place.c_peer])
    for part in mlp:
        part.start()
    gain_sums[...] = jnp.zeros_like(gain_sums)
    gain_sums[:, width : 2 * width] = gain_mlp[...]
    grad_keys[...] = jnp.zeros_like(grad_keys)
    grad_values[...] = jnp.zeros_like(grad_values)

    def attended_grad(part, carry):
        spots = pl.ds(pl.multiple_of(part * tokens, tokens), tokens)
        for start in range(0, query_width, 256):
            result = jnp.dot(full_proj[part], wo[:, start : start + 256], preferred_element_type=F32)
            grad_att[spots, start : start + 256] = result.astype(BF16)
        return carry

    lax.fori_loop(0, parts, attended_grad, 0)

    def out_weight_grad(index, carry):
        lanes = pl.ds(pl.multiple_of(index * 256, 256), 256)
        source = full_proj[:, :, lanes].reshape(parts * tokens, 256)
        grad_wo[lanes, :] = product(source, attended[...], CONTRACT_ROWS).astype(BF16)
        return carry

    lax.fori_loop(0, width // 256, out_weight_grad, 0)
    wo_sum.start()

    scale = head ** (-0.5)
    gain_query = gains[:, 2 * width : 2 * width + head]
    gain_key = gains[:, 2 * width + head : 2 * width + 2 * head]

    def unrotate(spots, lanes, grad, gain, gain_lanes):
        turned = grad * cosine[spots, :] - lane_swap(grad) * sine[spots, :]
        values, terms = norm_back(lin[spots, lanes].astype(F32), gain, turned)
        grad_lin[spots, lanes] = values.astype(BF16)
        gain_sums[:, gain_lanes] += jnp.sum(terms, axis=0, keepdims=True)

    for part in range(parts):
        keys = (part + 1) * tokens
        spots = pl.ds(part * tokens, tokens)
        allowed = (seg_col[:keys, :] == seg_row[:, spots]) & (pos_col[:keys, :] <= pos_row[:, spots])
        some = jnp.where(allowed, 0.0, MASKED)
        for copy in range(repeat):
            bias[:keys, copy * tokens : (copy + 1) * tokens] = some

        def attend(pair, carry):
            key_lanes = pl.ds(pl.multiple_of(query_width + pair * head, head), head)
            value_lanes = pl.ds(pl.multiple_of(rotated + pair * head, head), head)
            own_lanes = pl.ds(pl.multiple_of(pair * head, head), head)
            query_lanes = [
                pl.ds(pl.multiple_of((pair * repeat + copy) * head, head), head)
                for copy in range(repeat)
            ]
            queries = jnp.concatenate([rot[spots, lanes] for lanes in query_lanes], axis=0)
            grads = jnp.concatenate([grad_att[spots, lanes] for lanes in query_lanes], axis=0)
            key_rows, value_rows = rot[:keys, key_lanes], rot[:keys, value_lanes]
            scores = product(key_rows, queries, CONTRACT_COLS) * scale + bias[:keys, :]
            probs = jnp.exp(scores - log_row[pair, part])
            grad_values[:keys, own_lanes] += jnp.dot(
                probs.astype(BF16), grads, preferred_element_type=F32
            )
            grad_probs = product(value_rows, grads, CONTRACT_COLS)
            spread = jnp.sum(probs * grad_probs, axis=0, keepdims=True)
            grad_scores = (probs * (grad_probs - spread)).astype(BF16)
            grad_keys[:keys, own_lanes] += jnp.dot(
                grad_scores, queries, preferred_element_type=F32
            )
            grad_queries = product(grad_scores, key_rows, CONTRACT_ROWS) * scale
            for copy in range(repeat):
                unrotate(
                    spots,
                    query_lanes[copy],
                    grad_queries[copy * tokens : (copy + 1) * tokens],
                    gain_query,
                    pl.ds(2 * width, head),
                )
            return carry

        lax.fori_loop(0, key_width // head, attend, 0)
        if part == parts - 2:
            mlp[0].forward_x(column_stage)
            wo_sum.forward_y()
    for pair in range(key_width // head):

        def back_keys(part, carry):
            spots = pl.ds(pl.multiple_of(part * tokens, tokens), tokens)
            lanes = pl.ds(pair * head, head)
            unrotate(
                spots,
                pl.ds(query_width + pair * head, head),
                grad_keys[spots, lanes] * scale,
                gain_key,
                pl.ds(2 * width + head, head),
            )
            grad_lin[spots, pl.ds(rotated + pair * head, head)] = grad_values[spots, lanes].astype(
                BF16
            )
            return carry

        lax.fori_loop(0, parts, back_keys, 0)

    def weight_grad(target, start, size):
        def step(index, carry):
            lanes = pl.ds(pl.multiple_of(index * 256, 256), 256)
            source = normed[:, :, lanes].reshape(parts * tokens, 256)
            target[lanes, :] = product(
                source, grad_lin[:, start : start + size], CONTRACT_ROWS
            ).astype(BF16)
            return carry

        lax.fori_loop(0, width // 256, step, 0)

    weight_grad(grad_key, query_width, 2 * key_width)
    key_sum.start()
    weight_grad(grad_query, 0, query_width)
    query_sum.start()

    def normed_grad(part, target):
        source = grad_lin[pl.ds(pl.multiple_of(part * tokens, tokens), tokens), :]

        def step(index, carry):
            block = pl.ds(pl.multiple_of(index * 256, 256), 256)
            target[:, block] = product(source, full_qkv[block, :], CONTRACT_COLS).astype(BF16)
            return carry

        lax.fori_loop(0, width // 256, step, 0)

    cores = place.cores
    places = ((1 - place.x) * cores, place.x * cores)
    normed_grad(places[0] + 1 - place.c, to_c.at[0])
    over_c = [mover.send(to_c.at[0], from_c.at[0], place.c_peer)]
    normed_grad(places[0] + place.c, to_c.at[1])
    over_c[0].wait_recv()
    add_rows(to_c.at[1], [to_c.at[1], from_c.at[0]], tokens, 32)
    over_x = mover.send(to_c.at[1], from_x, place.x_peer)
    normed_grad(places[1] + 1 - place.c, to_c.at[2])
    over_c.append(mover.send(to_c.at[2], from_c.at[1], place.c_peer))
    normed_grad(places[1] + place.c, to_c.at[3])
    mlp[1].forward_x(column_stage)
    mlp[0].forward_high()
    wo_sum.forward_l()
    key_sum.forward_y()
    over_c[1].wait_recv()
    over_x.wait_recv()

    def back_normed(index, carry):
        rows = pl.ds(pl.multiple_of(index * 32, 32), 32)
        total = to_c[3, rows, :].astype(F32) + from_c[1, rows, :].astype(F32)
        total = total + from_x[rows, :].astype(F32)
        grad, terms = norm_back(moved[rows, :].astype(F32), gains[:, :width], total)
        grad_moved[rows, :] = (grad_resid[rows, :] + grad).astype(BF16)
        gain_sums[:, :width] += jnp.sum(terms, axis=0, keepdims=True)
        return carry

    lax.fori_loop(0, tokens // 32, back_normed, 0)
    for q in range(GROUP):
        lanes = pl.ds(q * columns, columns)
        piece = jnp.dot(recv_maps_t[q], grad_moved[:, lanes], preferred_element_type=F32)
        total = piece if q == 0 else total + piece
    blocks_out[...] = total.astype(BF16).reshape(blocks_out.shape)
    copies = []
    for step in range(1, place.dp_size):
        other = lax.rem(place.d + step, place.dp_size)
        copies.append(mover.send(blocks_out.at[other], blocks_in.at[place.d], (other, place.s)))
        copies.append(mover.send(gain_sums, rows_in.at[place.d], (other, place.s)))
    blocks_in[place.d] = blocks_out[place.d]
    rows_in[place.d] = gain_sums[...]
    query_sum.forward_y()
    key_sum.forward_l()
    mlp[2].forward_x(column_stage)
    for copy in copies:
        copy.wait_recv()
    row_total = rows_in[0]
    for index in range(1, place.dp_size):
        row_total = row_total + rows_in[index]
    row_c[0] = row_total
    pass_c = mover.send(row_c.at[0], row_c.at[1], place.c_peer)
    returned = blocks_in[...].reshape(place.dp_size * 16, columns)
    for q in range(GROUP):
        lanes = pl.ds(q * columns, columns)
        here = jnp.dot(send_maps_t[q], returned, preferred_element_type=F32)
        here = here + jnp.where(keep[...] > 0.0, grad_moved[:, lanes].astype(F32), 0.0)
        grad_hidden[:, lanes] = here.astype(BF16)
    query_sum.forward_l()
    pass_c.wait_recv()
    row_x[0] = row_c[0] + row_c[1]
    pass_x = mover.send(row_x.at[0], row_x.at[1], place.x_peer)
    mlp[1].forward_high()
    mlp[2].forward_high()
    mlp[0].finish(out_stage, out_gd)
    wo_sum.finish()
    mlp[1].finish(out_stage, out_gg)
    key_sum.finish()
    query_sum.finish()
    pass_x.wait_recv()
    mlp[2].finish(out_stage, out_gu)
    mover.finish()
    gain_sums[...] = row_x[0] + row_x[1]


def backward(sizes, collective_id, args):
    dp_size, seq_size = sizes
    part_gd, wo, moved, gains = args[0], args[3], args[6], args[9]
    rot, attended = args[20], args[21]
    tokens, width = moved.shape
    high = dp_size // GROUP
    rows = width // dp_size
    quarter = part_gd.shape[1] // 2
    row_len = seq_size * tokens
    query_width = attended.shape[1]
    key_width = (rot.shape[1] - query_width) // 2
    repeat = query_width // key_width
    outs = [
        ((tokens, width), BF16, VMEM),
        (gains.shape, F32, VMEM),
        ((rows, GROUP * quarter), F32, HBM),
        ((rows, GROUP * quarter), F32, HBM),
        ((rows, GROUP * quarter), F32, HBM),
        ((rows, rot.shape[1]), F32, VMEM),
        ((rows, query_width), F32, VMEM),
    ]
    piece = high * GROUP * rows // ScatterColumns.pieces
    scratch = [
        pltpu.VMEM((2, piece, quarter), BF16),
        pltpu.VMEM((rows, GROUP * quarter), F32),
    ]
    scratch += [
        pltpu.VMEM(wo.shape, BF16),
        pltpu.VMEM((width, 2 * key_width), BF16),
        pltpu.VMEM((width, query_width), BF16),
    ]
    for _ in range(3):
        scratch += ScatterColumns.scratch(high, rows, quarter)
    scratch += ScatterDp.scratch(high, rows, query_width)
    scratch += ScatterDp.scratch(high, rows, 2 * key_width)
    scratch += ScatterDp.scratch(high, rows, query_width)
    scratch += [
        pltpu.VMEM((tokens, width), BF16),
        pltpu.VMEM((seq_size, tokens, width), BF16),
        pltpu.VMEM((2, tokens, width), BF16),
        pltpu.VMEM((tokens, width), BF16),
        pltpu.VMEM((row_len, query_width), BF16),
        pltpu.VMEM((row_len, key_width), F32),
        pltpu.VMEM((row_len, key_width), F32),
        pltpu.VMEM((row_len, rot.shape[1]), BF16),
        pltpu.VMEM((row_len, repeat * tokens), F32),
        pltpu.VMEM((dp_size, 16, width // GROUP), BF16),
        pltpu.VMEM((dp_size, 16, width // GROUP), BF16),
        pltpu.VMEM((dp_size,) + gains.shape, F32),
        pltpu.VMEM((2,) + gains.shape, F32),
        pltpu.VMEM((2,) + gains.shape, F32),
    ]
    sends = 3 * (high + 3) + 3 * ScatterDp.sends(high)
    sends += 3 + 2 * (dp_size - 1) + 2
    local = 3 * (ScatterColumns.pieces + 1) + 1
    return pl.pallas_call(
        functools.partial(backward_kernel, sizes),
        out_shape=[jax.ShapeDtypeStruct(shape, dtype) for shape, dtype, _ in outs],
        in_specs=[HBM] * 3 + [VMEM] * 21,
        out_specs=[spec for _, _, spec in outs],
        scratch_shapes=scratch + sems(sends, local),
        compiler_params=comm_params(collective_id, 63 * 1024 * 1024),
        name="backward_attention",
    )(*args)


def per_device(
    sizes,
    hidden_in,
    valid_len,
    doc_lengths,
    doc_perm,
    attn_norm,
    w_query,
    key_weight,
    value_weight,
    w_out,
    query_norm,
    key_norm_gain,
    mlp_norm,
    w_gate,
    w_up,
    w_down,
    out_grad,
):
    shard_len = hidden_in.shape[0]
    model_width = hidden_in.shape[1]
    seq_count = doc_lengths.shape[0]
    row_count = doc_lengths.shape[1]
    shorts = doc_lengths.shape[2]
    row_len = shard_len * seq_count
    cap_len = MAXSHORT
    body_len = shard_len - shorts * cap_len
    my_row = lax.axis_index("dp")
    my_part = lax.axis_index("seq")
    valid_here = valid_len[my_row]
    all_starts, all_kept, all_new, all_dest = jax.vmap(
        lambda lengths_part, perm_part: layout(lengths_part, perm_part, body_len)
    )(doc_lengths, doc_perm)
    part_ids = jnp.arange(seq_count, dtype=jnp.int32)
    seg_parts, pos_parts, long_parts, short_parts = jax.vmap(
        lambda kept_p, new_p, dest_p, part: slot_labels(
            kept_p, new_p, dest_p, part, my_row, valid_here, body_len, shard_len, row_len, row_count
        )
    )(all_kept, all_new, all_dest, part_ids)
    segment = seg_parts.reshape(row_len)
    position = pos_parts.reshape(row_len)
    seg_local = lax.dynamic_index_in_dim(seg_parts, my_part, 0, keepdims=False)
    pos_local = lax.dynamic_index_in_dim(pos_parts, my_part, 0, keepdims=False)
    keep_long = lax.dynamic_index_in_dim(long_parts, my_part, 0, keepdims=False)
    live_local = keep_long | lax.dynamic_index_in_dim(short_parts, my_part, 0, keepdims=False)
    starts = lax.dynamic_index_in_dim(all_starts, my_part, 0, keepdims=False)
    kept_flat = lax.dynamic_index_in_dim(all_kept, my_part, 0, keepdims=False)
    new_start = lax.dynamic_index_in_dim(all_new, my_part, 0, keepdims=False)
    dest_row = lax.dynamic_index_in_dim(all_dest, my_part, 0, keepdims=False)
    row_ids = jnp.arange(row_count, dtype=jnp.int32)
    local_slots = jnp.arange(shard_len, dtype=jnp.int32)
    cap_ids = jnp.arange(cap_len, dtype=jnp.int32)
    my_dest = lax.dynamic_slice_in_dim(dest_row, my_row * shorts, shorts)
    my_starts = lax.dynamic_slice_in_dim(starts, my_row * shorts, shorts)
    my_kept = lax.dynamic_slice_in_dim(kept_flat, my_row * shorts, shorts)
    going = my_dest[None, :] == row_ids[:, None]
    send_start = jnp.sum(jnp.where(going, my_starts[None, :], 0), axis=1)
    send_len = jnp.sum(jnp.where(going, my_kept[None, :], 0), axis=1)
    send_map = (
        (
            (cap_ids[None, :, None] < send_len[:, None, None])
            & (local_slots[None, None, :] == send_start[:, None, None] + cap_ids[None, :, None])
        )
        .reshape(row_count * cap_len, shard_len)
        .astype(jnp.bfloat16)
    )
    coming = (dest_row == my_row).reshape(row_count, shorts)
    recv_start = jnp.sum(jnp.where(coming, new_start.reshape(row_count, shorts), 0), axis=1)
    recv_len = jnp.sum(jnp.where(coming, kept_flat.reshape(row_count, shorts), 0), axis=1)
    recv_map = (
        (
            (cap_ids[None, None, :] < recv_len[None, :, None])
            & (local_slots[:, None, None] == recv_start[None, :, None] + cap_ids[None, None, :])
        )
        .reshape(shard_len, row_count * cap_len)
        .astype(jnp.bfloat16)
    )
    same_piece = jnp.eye(GROUP, dtype=BF16)

    def spread(piece, total):
        return lax.dynamic_update_slice(
            jnp.zeros((total,), F32), piece.astype(F32), (my_row * piece.shape[0],)
        )

    head_size = query_norm.shape[0] * row_count
    gain_row = jnp.concatenate(
        [
            spread(attn_norm, model_width),
            spread(mlp_norm, model_width),
            spread(query_norm, head_size),
            spread(key_norm_gain, head_size),
        ]
    )[None, :]
    send_maps = (same_piece[:, None, :, None] * send_map[None, :, None, :]).reshape(
        GROUP, -1, shard_len
    )
    recv_maps = (recv_map[None, :, :, None] * same_piece[:, None, None, :]).reshape(
        GROUP, shard_len, -1
    )
    half_width = head_size // 2
    freq_index = jnp.arange(half_width, dtype=F32)
    inverse = jnp.exp(freq_index * (-2.0 * math.log(ROPE_BASE) / head_size))
    angles = position.astype(F32)[:, None] * inverse[None, :]
    cosine = jnp.concatenate([jnp.cos(angles)] * 2, axis=1)
    sine = jnp.concatenate([-jnp.sin(angles), jnp.sin(angles)], axis=1)
    live_scale = live_local.astype(F32)[:, None]
    keep_scale = keep_long.astype(F32)[:, None]
    (
        moved_low,
        gains,
        normed,
        qkv_mat,
        out_mat,
        gate_mat,
        up_mat,
        down_mat,
        grad_y_own,
        rotated_lin,
        rotated_all,
        attended,
        log_total,
        resid_rows,
        normed_mlp,
    ) = forward(
        sizes,
        1,
        head_size,
        (
            hidden_in,
            keep_scale,
            send_maps,
            recv_maps,
            gain_row,
            cosine,
            sine,
            segment[:, None],
            position[:, None],
            segment[None, :],
            position[None, :],
            out_grad,
            live_scale,
            w_query,
            key_weight,
            value_weight,
            w_out.T,
            w_gate,
            w_up,
            w_down.T,
        ),
    )
    cuts = (model_width, 2 * model_width, 2 * model_width + head_size)
    gate_mat = gate_mat.reshape(model_width, -1)
    up_mat = up_mat.reshape(model_width, -1)
    down_mat = down_mat.reshape(model_width, -1)
    query_width = w_query.shape[1]
    key_width = key_weight.shape[1]
    qkv_cuts = (query_width, query_width + key_width)
    mixed, grad_resid, grad_proj, gain_mlp_sum, grad_down, grad_gate, grad_up = feed_forward(
        sizes,
        2,
        (normed_mlp, gate_mat, up_mat, down_mat, grad_y_own, resid_rows, live_scale, gains),
    )
    grad_hidden, gain_sums, out_down, out_gate, out_up, out_qkv, out_wo = backward(
        sizes,
        3,
        (
            grad_down,
            grad_gate,
            grad_up,
            out_mat,
            grad_resid,
            grad_proj,
            moved_low,
            keep_scale,
            gain_mlp_sum,
            gains,
            cosine,
            sine,
            segment[:, None],
            position[:, None],
            segment[None, :],
            position[None, :],
            jnp.swapaxes(log_total, 2, 3),
            normed,
            qkv_mat,
            rotated_lin,
            rotated_all,
            attended,
            jnp.swapaxes(recv_maps, 1, 2),
            jnp.swapaxes(send_maps, 1, 2),
        ),
    )
    out_query, out_key, out_value = jnp.split(out_qkv, qkv_cuts, axis=1)
    device = my_row * seq_count + my_part

    def own_piece(vector):
        size = vector.shape[0] // (row_count * seq_count)
        return lax.dynamic_slice_in_dim(vector, device * size, size)

    sum_attn, sum_mlp, sum_query, sum_key = [own_piece(v) for v in jnp.split(gain_sums[0], cuts)]
    return (
        mixed,
        grad_hidden,
        sum_attn,
        out_query,
        out_key,
        out_value,
        out_wo.T,
        sum_query,
        sum_key,
        sum_mlp,
        out_gate,
        out_up,
        out_down.T,
    )


def solution(mesh):
    in_specs = (
        P(("dp", "seq"), None),
        P(),
        P(),
        P(),
        P("dp"),
        P("dp", "seq"),
        P("dp", "seq"),
        P("dp", "seq"),
        P("seq", "dp"),
        P("dp"),
        P("dp"),
        P("dp"),
        P("dp", "seq"),
        P("dp", "seq"),
        P("seq", "dp"),
        P(("dp", "seq"), None),
    )
    out_specs = (
        P(("dp", "seq"), None),
        P(("dp", "seq"), None),
        P(("dp", "seq")),
        P("dp", "seq"),
        P("dp", "seq"),
        P("dp", "seq"),
        P("seq", "dp"),
        P(("dp", "seq")),
        P(("dp", "seq")),
        P(("dp", "seq")),
        P("dp", "seq"),
        P("dp", "seq"),
        P("seq", "dp"),
    )
    return jax.shard_map(
        functools.partial(per_device, (mesh.shape["dp"], mesh.shape["seq"])), mesh=mesh, in_specs=in_specs, out_specs=out_specs, check_vma=False
    )
```

```python
import functools
import math

import jax
import jax.numpy as jnp
from jax import lax
from jax.experimental import pallas as pl
from jax.experimental.pallas import tpu as pltpu
from jax.sharding import PartitionSpec as P

MAXSHORT = 4
GROUP = 4
MESH = pl.DeviceIdType.MESH
HBM = pl.BlockSpec(memory_space=pltpu.HBM)
VMEM = pl.BlockSpec(memory_space=pltpu.VMEM)
BF16 = jnp.bfloat16
F32 = jnp.float32


NORM_EPS = 1e-06
ROPE_BASE = 1000000.0
MASKED = -1e30
CONTRACT_ROWS = (((0,), (0,)), ((), ()))
CONTRACT_COLS = (((1,), (1,)), ((), ()))


def product(left, right, dims):
    return lax.dot_general(left, right, dims, preferred_element_type=jnp.float32)


class Place:
    def __init__(self, dp_size, seq_size):
        self.dp_size = dp_size
        self.seq_size = seq_size
        self.high = dp_size // GROUP
        self.cores = seq_size // 2
        self.d = lax.axis_index("dp")
        self.s = lax.axis_index("seq")
        self.g = lax.rem(self.d, GROUP)
        self.h = lax.div(self.d, GROUP)
        self.x = lax.div(self.s, self.cores)
        self.c = lax.rem(self.s, self.cores)
        self.y = lax.rem(self.g, 2)
        self.l = lax.div(self.g, 2)
        self.gy = self.g + 1 - 2 * self.y
        self.gl = lax.rem(self.g + 2, GROUP)
        self.gd = 3 - self.g
        self.y_peer = (self.h * GROUP + self.gy, self.s)
        self.l_peer = (self.h * GROUP + self.gl, self.s)
        self.d_peer = (self.h * GROUP + self.gd, self.s)
        self.x_peer = (self.d, (1 - self.x) * self.cores + self.c)
        self.c_peer = (self.d, self.x * self.cores + 1 - self.c)

    def h_peer(self, step):
        return (lax.rem(self.h + step, self.high) * GROUP + self.g, self.s)

    def h_from(self, step):
        return lax.rem(self.h + self.high - step, self.high)

    def g_peer(self, step):
        return (self.h * GROUP + lax.rem(self.g + step, GROUP), self.s)


class Mover:
    def __init__(self, send_sems, recv_sems, local_sems):
        self.send_sems = send_sems
        self.recv_sems = recv_sems
        self.local_sems = local_sems
        self.count = 0
        self.local_count = 0
        self.sent = []

    def send(self, source, target, device):
        index = self.count
        self.count += 1
        copy = pltpu.make_async_remote_copy(
            src_ref=source,
            dst_ref=target,
            send_sem=self.send_sems.at[index],
            recv_sem=self.recv_sems.at[index],
            device_id=device,
            device_id_type=MESH,
        )
        copy.start()
        self.sent.append(copy)
        return copy

    def local(self, source, target):
        index = self.local_count
        self.local_count += 1
        copy = pltpu.make_async_copy(source, target, self.local_sems.at[index])
        copy.start()
        return copy

    def drain(self, copy):
        copy.wait_send()
        self.sent = [other for other in self.sent if other is not copy]

    def finish(self):
        for copy in self.sent:
            copy.wait_send()


def greet(peers):
    barrier = pltpu.get_barrier_semaphore()
    for peer in peers:
        pl.semaphore_signal(barrier, inc=1, device_id=peer, device_id_type=MESH)
    pl.semaphore_wait(barrier, len(peers))


def dp_peers(place):
    return [
        (lax.rem(place.d + step, place.dp_size), place.s) for step in range(1, place.dp_size)
    ]


def sems(count, local):
    return [
        pltpu.SemaphoreType.DMA((count,)),
        pltpu.SemaphoreType.DMA((count,)),
        pltpu.SemaphoreType.DMA((max(local, 1),)),
    ]


def comm_params(collective_id, vmem=None):
    return pltpu.CompilerParams(
        collective_id=collective_id,
        has_side_effects=True,
        vmem_limit_bytes=vmem if vmem is not None else 60 * 1024 * 1024,
    )


def add_rows(target, terms, rows, chunk):
    def step(index, carry):
        part = pl.ds(pl.multiple_of(index * chunk, chunk), chunk)
        total = terms[0][part, :].astype(F32)
        for term in terms[1:]:
            total = total + term[part, :].astype(F32)
        target[part, :] = total.astype(target.dtype)
        return carry

    lax.fori_loop(0, rows // chunk, step, 0)


class GatherSeq:
    sends = 3

    def __init__(self, place, mover, own, full):
        self.place, self.mover, self.full = place, mover, full
        self.local = mover.local(own, full.at[place.s])
        self.over_x = mover.send(own, full.at[place.s], place.x_peer)
        self.over_c = mover.send(own, full.at[place.s], place.c_peer)

    def forward(self):
        self.over_x.wait_recv()
        block = self.full.at[self.place.x_peer[1]]
        self.passed = self.mover.send(block, block, self.place.c_peer)

    def finish(self):
        self.local.wait()
        self.over_c.wait_recv()
        self.passed.wait_recv()


class GatherGroup:
    sends = 10

    def __init__(self, place, mover, own, full):
        self.place, self.mover, self.full = place, mover, full
        half = own.shape[0] // 2
        self.low, self.top = pl.ds(0, half), pl.ds(half, half)
        self.local = mover.local(own, full.at[place.g, place.c])
        spot = full.at[place.g, place.c]
        self.y_low = mover.send(own.at[self.low], spot.at[self.low], place.y_peer)
        self.l_top = mover.send(own.at[self.top], spot.at[self.top], place.l_peer)
        self.y_top = mover.send(own.at[self.top], spot.at[self.top], place.y_peer)
        self.l_low = mover.send(own.at[self.low], spot.at[self.low], place.l_peer)
        self.core = [mover.send(own, spot, place.c_peer)]

    def forward(self):
        place, mover, full = self.place, self.mover, self.full
        self.y_low.wait_recv()
        part = full.at[place.gy, place.c, self.low]
        self.d_low = mover.send(part, part, place.l_peer)
        self.l_top.wait_recv()
        part = full.at[place.gl, place.c, self.top]
        self.d_top = mover.send(part, part, place.y_peer)
        self.y_top.wait_recv()
        part = full.at[place.gy, place.c]
        self.core.append(mover.send(part, part, place.c_peer))
        self.l_low.wait_recv()
        part = full.at[place.gl, place.c]
        self.core.append(mover.send(part, part, place.c_peer))

    def finish_ici(self):
        place = self.place
        self.d_low.wait_recv()
        self.d_top.wait_recv()
        part = self.full.at[place.gd, place.c]
        self.core.append(self.mover.send(part, part, place.c_peer))

    def finish(self):
        self.local.wait()
        for copy in self.core:
            copy.wait_recv()


class GatherDp:
    def __init__(self, place, mover, pieces, full):
        self.place, self.mover, self.full, self.pieces = place, mover, full, pieces
        first, last = pieces[0], pieces[-1]
        self.window = pl.ds(first[1], last[1] + last[2] - first[1])
        self.rows = full.shape[0] // place.dp_size
        own_rows = self.block(place.d)
        self.spots = [full.at[own_rows, pl.ds(start, size)] for _, start, size in pieces]
        self.local = [
            mover.local(piece[0], spot) for piece, spot in zip(pieces, self.spots)
        ]
        self.over_y, self.passed_l = [], []

    def block(self, index):
        return pl.ds(pl.multiple_of(index * self.rows, self.rows), self.rows)

    def own_to(self, peer):
        return [
            self.mover.send(piece[0], spot, peer) for piece, spot in zip(self.pieces, self.spots)
        ]

    def send_h(self):
        place = self.place
        self.over_h = [self.own_to(place.h_peer(step)) for step in range(1, place.high)]

    def send_l(self):
        self.own_l = self.own_to(self.place.l_peer)

    def send_y(self):
        self.over_y += self.own_to(self.place.y_peer)

    def part(self, high, index):
        return self.full.at[self.block(high * GROUP + index), self.window]

    def pass_h_to_l(self):
        place = self.place
        for step, copies in enumerate(self.over_h, 1):
            for copy in copies:
                copy.wait_recv()
            part = self.part(place.h_from(step), place.g)
            self.passed_l.append(self.mover.send(part, part, place.l_peer))

    def pass_h_to_y(self):
        place = self.place
        for step in range(1, place.high):
            part = self.part(place.h_from(step), place.g)
            self.over_y.append(self.mover.send(part, part, place.y_peer))

    def pass_own_l_to_y(self):
        place = self.place
        for copy in self.own_l:
            copy.wait_recv()
        part = self.part(place.h, place.gl)
        self.over_y.append(self.mover.send(part, part, place.y_peer))

    def pass_l_to_y(self):
        place = self.place
        for step, copy in enumerate(self.passed_l, 1):
            copy.wait_recv()
            part = self.part(place.h_from(step), place.gl)
            self.over_y.append(self.mover.send(part, part, place.y_peer))

    def finish(self):
        for copy in self.local:
            copy.wait()
        for copy in self.over_y:
            copy.wait_recv()


class GatherColumns:
    def __init__(self, place, mover, own, full):
        self.place, self.mover, self.full, self.own = place, mover, full, own
        self.quarter = own.shape[1] // GROUP
        self.rows = own.shape[0]
        self.near = pl.ds(0, self.quarter)
        self.far = pl.ds(self.quarter, self.quarter)

    def block(self, high):
        rows = GROUP * self.rows
        return pl.ds(pl.multiple_of(high * rows, rows), rows)

    def send_g(self, spot=None):
        place, mover, own = self.place, self.mover, self.own
        if spot is None:
            spot = self.full.at[
                pl.ds(pl.multiple_of(place.d * self.rows, self.rows), self.rows), self.near
            ]
        self.over_g = []
        for step in (3, 1, 2):
            to = lax.rem(place.g + step, GROUP)
            columns = pl.ds(pl.multiple_of(to * self.quarter, self.quarter), self.quarter)
            self.over_g.append(mover.send(own.at[:, columns], spot, place.g_peer(step)))
        columns = pl.ds(pl.multiple_of(place.g * self.quarter, self.quarter), self.quarter)
        self.local = mover.local(own.at[:, columns], spot)

    def wait_g(self):
        self.local.wait()
        for copy in self.over_g:
            copy.wait_recv()

    def send_h(self, source=None):
        place = self.place
        near = self.full.at[self.block(place.h), self.near]
        source = near if source is None else source
        self.over_h = [
            self.mover.send(source, near, place.h_peer(step)) for step in range(1, place.high)
        ]

    def send_x(self, source=None):
        place = self.place
        rows = self.block(place.h)
        source = self.full.at[rows, self.near] if source is None else source
        self.over_x = [self.mover.send(source, self.full.at[rows, self.far], place.x_peer)]

    def pass_h_to_x(self):
        place = self.place
        for step, copy in enumerate(self.over_h, 1):
            copy.wait_recv()
            rows = self.block(place.h_from(step))
            self.over_x.append(
                self.mover.send(
                    self.full.at[rows, self.near], self.full.at[rows, self.far], place.x_peer
                )
            )

    def finish(self):
        for copy in self.over_x:
            copy.wait_recv()


def lane_swap(values):
    half = values.shape[-1] // 2
    return jnp.concatenate([values[:, half:], values[:, :half]], axis=-1)


def norm_rows(values, gain):
    scale = lax.rsqrt(jnp.mean(values * values, axis=-1, keepdims=True) + NORM_EPS)
    return values * scale * gain


def index_of(shape, dim):
    return lax.broadcasted_iota(jnp.int32, shape, dim)


def total_of(condition, values, axis):
    picked = jnp.where(condition, values.astype(F32), 0.0)
    return jnp.sum(picked, axis=axis, keepdims=True)


class Layout:
    def __init__(self, refs, part, row_count, body):
        len_row, perm_row, len_col, perm_col = refs
        docs = len_row.shape[-1]
        self.docs, self.body, self.row_count = docs, body, row_count
        self.bits = (docs // row_count).bit_length() - 1
        down, along = index_of((docs, docs), 0), index_of((docs, docs), 1)
        same_row = (down >> self.bits) == (along >> self.bits)
        before = jnp.where(same_row & (down < along), 1.0, 0.0).astype(BF16)
        self.lens = len_row[part].astype(F32)
        self.lens_col = len_col[part].astype(F32)
        perm, perm_of_col = perm_row[part], perm_col[part]
        matched = perm_of_col == along
        self.dest, self.dest_col = perm >> self.bits, perm_of_col >> self.bits
        self.starts = body + jnp.dot(self.lens.astype(BF16), before, preferred_element_type=F32)
        placed = total_of(matched, jnp.broadcast_to(self.lens_col, matched.shape), 0)
        new_at = body + jnp.dot(placed.astype(BF16), before, preferred_element_type=F32)
        self.new_col = total_of(matched, jnp.broadcast_to(new_at, matched.shape), 1)
        self.new = product(
            new_at.astype(BF16), jnp.where(matched, 1.0, 0.0).astype(BF16), CONTRACT_COLS
        )

    def labels(self, part, row, valid, tokens, row_len, column):
        shape = (tokens, self.docs) if column else (self.docs, tokens)
        axis = 1 if column else 0
        slot, doc = index_of(shape, 1 - axis).astype(F32), index_of(shape, axis)
        start, size, dest = (
            (self.new, self.lens, self.dest)
            if column
            else (self.new_col, self.lens_col, self.dest_col)
        )
        inside = (dest == row) & (slot >= start) & (slot < start + size)
        first = self.row_count + part * self.docs
        segment = total_of(inside, doc + first, axis).astype(jnp.int32)
        position = total_of(inside, slot - start, axis).astype(jnp.int32)
        here = total_of(inside, jnp.ones(shape, F32), axis) > 0.0
        local = index_of((tokens, 1) if column else (1, tokens), 1 - axis)
        long_position = part * self.body + local
        in_long = (local < self.body) & (long_position.astype(F32) < valid)
        empty = -1 - (row * row_len + part * tokens + local)
        segment = jnp.where(in_long, row, jnp.where(here, segment, empty))
        return segment, jnp.where(in_long, long_position, position), in_long, in_long | here

    def send_map(self, row, tokens):
        shape = (self.row_count * 16, self.docs)
        target, doc = index_of(shape, 0) >> 4, index_of(shape, 1)
        mine = ((doc >> self.bits) == row) & (self.dest == target)
        start = total_of(mine, jnp.broadcast_to(self.starts, shape), 1)
        size = total_of(mine, jnp.broadcast_to(self.lens, shape), 1)
        shape = (shape[0], tokens)
        token = ((index_of(shape, 0) >> 2) & 3).astype(F32)
        slot = index_of(shape, 1).astype(F32)
        return jnp.where((token < size) & (slot == start + token), 1.0, 0.0).astype(BF16)

    def recv_map(self, row, tokens):
        shape = (self.docs, self.row_count * 16)
        source, doc = index_of(shape, 1) >> 4, index_of(shape, 0)
        mine = ((doc >> self.bits) == source) & (self.dest_col == row)
        start = total_of(mine, jnp.broadcast_to(self.new_col, shape), 0)
        size = total_of(mine, jnp.broadcast_to(self.lens_col, shape), 0)
        shape = (tokens, shape[1])
        token = ((index_of(shape, 1) >> 2) & 3).astype(F32)
        slot = index_of(shape, 0).astype(F32)
        return jnp.where((token < size) & (slot == start + token), 1.0, 0.0).astype(BF16)


def spread_piece(piece, place, total):
    size = piece.shape[1]
    shape = (size, total)
    spot = index_of(shape, 1) == index_of(shape, 0) + place.d * size
    return jnp.dot(piece, jnp.where(spot, 1.0, 0.0).astype(BF16), preferred_element_type=F32)


def forward_kernel(sizes, *refs):
    (hidden, valid_row, len_row, perm_row, len_col, perm_col, attn_gain, mlp_gain, query_gain,
     key_gain, out_grad, wq, wk, wv, wo, wg, wu, wd) = refs[:18]
    (moved, gains, normed, full_qkv, full_wo, full_g, full_u, full_d, grad_y, lin, rot, attended,
     log_total, resid, full_nm, cosine, sine, seg_col, pos_col, seg_row, pos_row, keep, live,
     send_map, recv_map) = refs[18:43]
    (blocks_out, blocks_in, rows_in, gain_row, part_seg, part_pos, normed_own, bias, part_own,
     from_c, from_x, to_c, nm_own, send_sems, recv_sems, local_sems) = refs[43:]
    place = Place(*sizes)
    mover = Mover(send_sems, recv_sems, local_sems)
    tokens, width = hidden.shape
    head = cosine.shape[1]
    query_width, key_width = wq.shape[1], wk.shape[1]
    columns = width // GROUP
    parts = sizes[1]
    repeat = query_width // key_width

    greet(dp_peers(place) + [place.x_peer, place.c_peer])
    key_parts = [(wk, query_width, key_width), (wv, query_width + key_width, key_width)]
    query = GatherDp(place, mover, [(wq, 0, query_width)], full_qkv)
    key = GatherDp(place, mover, key_parts, full_qkv)
    out = GatherDp(place, mover, [(wo, 0, wo.shape[1])], full_wo)
    gate = GatherColumns(place, mover, wg, full_g)
    upper = GatherColumns(place, mover, wu, full_u)
    lower = GatherColumns(place, mover, wd, full_d)
    gate.send_g()
    key.send_h()
    lower.send_g()
    row_len = parts * tokens
    body = tokens - (len_row.shape[2] // place.dp_size) * MAXSHORT
    layout_refs = (len_row, perm_row, len_col, perm_col)
    here = index_of(valid_row.shape, 1) == place.d
    valid = total_of(here, valid_row[...], 1)
    own = Layout(layout_refs, place.s, place.dp_size, body)
    send_map[...] = own.send_map(place.d, tokens)
    recv_map[...] = own.recv_map(place.d, tokens)
    _, _, own_long, own_live = own.labels(place.s, place.d, valid, tokens, row_len, True)
    keep[...] = jnp.where(own_long, 1.0, 0.0)
    live[...] = jnp.where(own_live, 1.0, 0.0)
    gain_row[:, :width] = spread_piece(attn_gain[...], place, width)
    gain_row[:, width : 2 * width] = spread_piece(mlp_gain[...], place, width)
    gain_row[:, 2 * width : 2 * width + head] = spread_piece(query_gain[...], place, head)
    gain_row[:, 2 * width + head :] = spread_piece(key_gain[...], place, head)
    piece_row = index_of((place.dp_size * 16, 1), 0) & 3
    for q in range(GROUP):
        lanes = pl.ds(q * columns, columns)
        piece = jnp.dot(send_map[...], hidden[:, lanes], preferred_element_type=F32)
        piece = jnp.where(piece_row == q, piece, 0.0)
        total = piece if q == 0 else total + piece
    blocks_out[...] = total.astype(BF16).reshape(blocks_out.shape)
    copies = []
    for step in range(1, place.dp_size):
        other = lax.rem(place.d + step, place.dp_size)
        copies.append(mover.send(blocks_out.at[other], blocks_in.at[place.d], (other, place.s)))
        copies.append(mover.send(gain_row, rows_in.at[place.d], (other, place.s)))
    blocks_in[place.d] = blocks_out[place.d]
    rows_in[place.d] = gain_row[...]
    for copy in copies:
        copy.wait_recv()
    all_gains = rows_in[0]
    for index in range(1, place.dp_size):
        all_gains = all_gains + rows_in[index]
    gains[...] = all_gains
    incoming = blocks_in[...].reshape(place.dp_size * 16, columns)
    for q in range(GROUP):
        lanes = pl.ds(q * columns, columns)
        chosen = jnp.where(piece_row == q, incoming, jnp.zeros_like(incoming))
        here = jnp.dot(recv_map[...], chosen, preferred_element_type=F32)
        here = here + jnp.where(keep[...] > 0.0, hidden[:, lanes].astype(F32), 0.0)
        moved[:, lanes] = here.astype(BF16)

    def norm_moved(index, carry):
        rows = pl.ds(pl.multiple_of(index * 32, 32), 32)
        normed_own[rows, :] = norm_rows(moved[rows, :].astype(F32), gains[:, :width]).astype(BF16)
        grad_y[rows, :] = (out_grad[rows, :].astype(F32) * live[rows, :]).astype(BF16)
        return carry

    lax.fori_loop(0, tokens // 32, norm_moved, 0)
    row = GatherSeq(place, mover, normed_own, normed)

    def label_part(part, carry):
        layout = Layout(layout_refs, part, place.dp_size, body)
        spots = pl.ds(pl.multiple_of(part * tokens, tokens), tokens)
        segment, position, _, _ = layout.labels(part, place.d, valid, tokens, row_len, True)
        seg_col[spots, :], pos_col[spots, :] = segment, position
        segment, position, _, _ = layout.labels(part, place.d, valid, tokens, row_len, False)
        part_seg[part], part_pos[part] = segment, position
        half = head // 2
        lane = index_of((1, head), 1)
        power = jnp.where(lane < half, lane, lane - half).astype(F32)
        angles = pos_col[spots, :].astype(F32) * jnp.exp(
            power * (-2.0 * math.log(ROPE_BASE) / head)
        )
        cosine[spots, :] = jnp.cos(angles)
        sine[spots, :] = jnp.where(lane < half, -1.0, 1.0) * jnp.sin(angles)
        return carry

    query.send_y()
    out.send_h()
    key.send_l()
    lower.wait_g()
    key.pass_h_to_l()
    key.pass_h_to_y()
    query.send_h()
    query.send_l()
    key.pass_own_l_to_y()
    gate.wait_g()
    gate.send_h()
    gate.send_x()
    key.send_y()
    query.pass_h_to_l()
    upper.send_g()
    out.send_l()
    key.pass_l_to_y()
    lower.send_x()
    query.pass_h_to_y()
    query.pass_own_l_to_y()
    row.forward()
    lower.send_h()
    out.pass_h_to_l()
    query.pass_l_to_y()
    out.pass_h_to_y()
    upper.wait_g()
    upper.send_x()
    out.send_y()
    upper.send_h()
    lax.fori_loop(0, parts, label_part, 0)
    seg_row[...] = jnp.concatenate([part_seg[part] for part in range(parts)], axis=1)
    pos_row[...] = jnp.concatenate([part_pos[part] for part in range(parts)], axis=1)
    row.finish()
    query.finish()
    key.finish()

    gain_query = gains[:, 2 * width : 2 * width + head]
    gain_key = gains[:, 2 * width + head : 2 * width + 2 * head]
    rotated = query_width + key_width
    tile = 2 * head

    def project(part, carry):
        spots = pl.ds(pl.multiple_of(part * tokens, tokens), tokens)
        source = normed[part]
        cos_part, sin_part = cosine[spots, :], sine[spots, :]
        for start in range(0, rotated + key_width, tile):
            result = jnp.dot(source, full_qkv[:, start : start + tile], preferred_element_type=F32)
            if start < rotated:
                lin[spots, start : start + tile] = result.astype(BF16)
                gain = gain_query if start < query_width else gain_key
                for inner in (0, head):
                    unit = norm_rows(result[:, inner : inner + head], gain)
                    turned = unit * cos_part + lane_swap(unit) * sin_part
                    rot[spots, start + inner : start + inner + head] = turned.astype(BF16)
            else:
                rot[spots, start : start + tile] = result.astype(BF16)
        return carry

    lax.fori_loop(0, parts, project, 0)
    out.pass_own_l_to_y()
    gate.pass_h_to_x()
    scale = head ** (-0.5)
    for part in range(parts):
        keys = (part + 1) * tokens
        spots = pl.ds(part * tokens, tokens)
        allowed = (seg_col[spots, :] == seg_row[:, :keys]) & (pos_row[:, :keys] <= pos_col[spots, :])
        some = jnp.where(allowed, 0.0, MASKED)
        for copy in range(repeat):
            bias[copy * tokens : (copy + 1) * tokens, :keys] = some

        def attend(pair, carry):
            key_lanes = pl.ds(pl.multiple_of(query_width + pair * head, head), head)
            value_lanes = pl.ds(pl.multiple_of(rotated + pair * head, head), head)
            query_lanes = [
                pl.ds(pl.multiple_of((pair * repeat + copy) * head, head), head)
                for copy in range(repeat)
            ]
            queries = jnp.concatenate([rot[spots, lanes] for lanes in query_lanes], axis=0)
            scores = product(queries, rot[:keys, key_lanes], CONTRACT_COLS) * scale
            scores = scores + bias[:, :keys]
            peak = jnp.max(scores, axis=-1, keepdims=True)
            expd = jnp.exp(scores - peak)
            weight = jnp.sum(expd, axis=-1, keepdims=True)
            probs = (expd / weight).astype(BF16)
            log_total[pair, part] = peak + jnp.log(weight)
            context = jnp.dot(probs, rot[:keys, value_lanes], preferred_element_type=F32)
            for copy in range(repeat):
                attended[spots, query_lanes[copy]] = context[
                    copy * tokens : (copy + 1) * tokens
                ].astype(BF16)
            return carry

        lax.fori_loop(0, key_width // head, attend, 0)
        if part == 2:
            out.pass_l_to_y()
    out.finish()

    def project_out(part, target):
        source = attended[pl.ds(pl.multiple_of(part * tokens, tokens), tokens), :]

        def step(index, carry):
            block = pl.ds(pl.multiple_of(index * 256, 256), 256)
            target[:, block] = product(source, full_wo[block, :], CONTRACT_COLS).astype(BF16)
            return carry

        lax.fori_loop(0, width // 256, step, 0)

    cores = place.cores
    places = ((1 - place.x) * cores, place.x * cores)
    project_out(places[0] + 1 - place.c, to_c.at[0])
    over_c = [mover.send(to_c.at[0], from_c.at[0], place.c_peer)]
    project_out(places[0] + place.c, part_own.at[0])
    over_c[0].wait_recv()
    add_rows(part_own.at[0], [part_own.at[0], from_c.at[0]], tokens, 32)
    over_x = mover.send(part_own.at[0], from_x, place.x_peer)
    project_out(places[1] + 1 - place.c, to_c.at[1])
    over_c.append(mover.send(to_c.at[1], from_c.at[1], place.c_peer))
    project_out(places[1] + place.c, part_own.at[1])
    lower.pass_h_to_x()
    over_c[1].wait_recv()
    over_x.wait_recv()

    def norm_resid(index, carry):
        rows = pl.ds(pl.multiple_of(index * 32, 32), 32)
        total = moved[rows, :].astype(F32) + part_own[1, rows, :].astype(F32)
        total = total + from_c[1, rows, :].astype(F32) + from_x[rows, :].astype(F32)
        resid[rows, :] = total
        nm_own[rows, :] = norm_rows(total, gains[:, width : 2 * width]).astype(BF16)
        return carry

    lax.fori_loop(0, tokens // 32, norm_resid, 0)
    group = GatherGroup(place, mover, nm_own, full_nm)
    upper.pass_h_to_x()
    group.forward()
    group.finish_ici()
    for part in (group, gate, upper, lower):
        part.finish()
    mover.finish()


def forward(sizes, collective_id, head_size, args):
    dp_size, seq_size = sizes
    hidden, wq, wk, wo, wg = args[0], args[11], args[12], args[14], args[15]
    tokens, width = hidden.shape
    high = dp_size // GROUP
    rows = wq.shape[0]
    row_len = seq_size * tokens
    rotated = wq.shape[1] + wk.shape[1]
    inner = wg.shape[1] // 2
    group = (GROUP, seq_size // 2, tokens, width)
    heads = wq.shape[1] // head_size
    gain_width = 2 * (width + head_size)
    routes = dp_size * 16
    column, line = (row_len, 1), (1, row_len)
    outs = [
        ((tokens, width), BF16, VMEM),
        ((1, gain_width), F32, VMEM),
        ((seq_size, tokens, width), BF16, VMEM),
        ((width, rotated + wk.shape[1]), BF16, VMEM),
        ((width, wo.shape[1]), BF16, VMEM),
        ((width, inner), BF16, HBM),
        ((width, inner), BF16, HBM),
        ((width, inner), BF16, HBM),
        ((tokens, width), BF16, VMEM),
        ((row_len, rotated), BF16, VMEM),
        ((row_len, rotated + wk.shape[1]), BF16, VMEM),
        ((row_len, wq.shape[1]), BF16, VMEM),
        ((wk.shape[1] // head_size, seq_size, heads * head_size // wk.shape[1] * tokens, 1), F32, VMEM),
        ((tokens, width), F32, VMEM),
        (group, BF16, HBM),
        ((row_len, head_size), F32, VMEM),
        ((row_len, head_size), F32, VMEM),
        (column, jnp.int32, VMEM),
        (column, jnp.int32, VMEM),
        (line, jnp.int32, VMEM),
        (line, jnp.int32, VMEM),
        ((tokens, 1), F32, VMEM),
        ((tokens, 1), F32, VMEM),
        ((routes, tokens), BF16, VMEM),
        ((tokens, routes), BF16, VMEM),
    ]
    scratch = [
        pltpu.VMEM((dp_size, 16, width // GROUP), BF16),
        pltpu.VMEM((dp_size, 16, width // GROUP), BF16),
        pltpu.VMEM((dp_size, 1, gain_width), F32),
        pltpu.VMEM((1, gain_width), F32),
        pltpu.VMEM((seq_size, 1, tokens), jnp.int32),
        pltpu.VMEM((seq_size, 1, tokens), jnp.int32),
        pltpu.VMEM((tokens, width), BF16),
        pltpu.VMEM((wq.shape[1] // wk.shape[1] * tokens, row_len), F32),
        pltpu.VMEM((2, tokens, width), BF16),
        pltpu.VMEM((2, tokens, width), BF16),
        pltpu.VMEM((tokens, width), BF16),
        pltpu.VMEM((2, tokens, width), BF16),
        pltpu.VMEM((tokens, width), BF16),
    ]
    sends = 2 * (dp_size - 1) + 4 * (high + 1) + 9 * high
    sends += 3 * (3 + 2 * high) + 2 * GatherGroup.sends + GatherSeq.sends + 3
    return pl.pallas_call(
        functools.partial(forward_kernel, sizes),
        out_shape=[jax.ShapeDtypeStruct(shape, dtype) for shape, dtype, _ in outs],
        in_specs=[VMEM] * 11 + [HBM] * 7,
        out_specs=[spec for _, _, spec in outs],
        scratch_shapes=scratch + sems(sends, 16),
        compiler_params=comm_params(collective_id),
        name="forward_attention",
    )(*args)


class ScatterColumns:
    stage_rows = 512

    @staticmethod
    def scratch(high, rows, quarter):
        group_rows = GROUP * rows
        return [
            pltpu.VMEM((high * group_rows, quarter), BF16),
            pltpu.VMEM((max(high - 1, 1), group_rows, quarter), BF16),
            pltpu.VMEM((GROUP - 1, rows, quarter), BF16),
        ]

    def __init__(self, place, mover, parts, from_x, from_h, from_g):
        self.place, self.mover, self.parts = place, mover, parts
        self.from_x, self.from_h, self.from_g = from_x, from_h, from_g
        self.group_rows = from_h.shape[1]
        self.quarter = from_x.shape[1]

    def rows_of(self, step):
        high = lax.rem(self.place.h + step, self.place.high)
        return high * self.group_rows

    def start(self, steps):
        quarter = self.quarter
        for step in steps:
            rows = pl.ds(pl.multiple_of(self.rows_of(step), self.group_rows), self.group_rows)
            self.over_x[step] = self.mover.send(
                self.parts.at[rows, pl.ds(quarter, quarter)],
                self.from_x.at[rows],
                self.place.x_peer,
            )

    def start_far(self):
        self.over_x = {}
        self.start(range(1, self.place.high))

    def start_near(self):
        self.start((0,))

    def add_x(self, step, stage):
        mover, total = self.mover, self.from_x
        rows = stage.shape[1]
        base = self.rows_of(step)
        near = pl.ds(0, self.quarter)
        pieces = self.group_rows // rows

        def block(index):
            return pl.ds(pl.multiple_of(base + index * rows, rows), rows)

        def load(index):
            return mover.local(self.parts.at[block(index), near], stage.at[index % 2])

        copies = [load(0)]
        self.over_x[step].wait_recv()
        for index in range(pieces):
            if index + 1 < pieces:
                copies.append(load(index + 1))
            copies[index].wait()
            part = total.at[block(index)]
            add_rows(part, [part, stage.at[index % 2]], rows, 64)

    def forward_far(self, stage):
        place = self.place
        self.over_h = []
        for step in range(1, place.high):
            self.add_x(step, stage)
            block = pl.ds(pl.multiple_of(self.rows_of(step), self.group_rows), self.group_rows)
            self.over_h.append(
                self.mover.send(
                    self.from_x.at[block], self.from_h.at[step - 1], place.h_peer(step)
                )
            )

    def add_near(self, stage):
        self.add_x(0, stage)

    def block(self, index):
        rows = self.group_rows // GROUP
        return pl.ds(
            pl.multiple_of(self.place.h * self.group_rows + index * rows, rows), rows
        )

    def forward_high(self):
        place = self.place
        own_rows = pl.ds(
            pl.multiple_of(place.h * self.group_rows, self.group_rows), self.group_rows
        )
        for copy in self.over_h:
            copy.wait_recv()
        mine = self.from_x.at[own_rows]
        terms = [mine] + [self.from_h.at[step] for step in range(place.high - 1)]
        add_rows(mine, terms, self.group_rows, 64)
        self.over_g = []
        for step in (3, 1, 2):
            block = self.block(lax.rem(place.g + step, GROUP))
            self.over_g.append(
                (
                    step,
                    self.mover.send(
                        self.from_x.at[block], self.from_g.at[step - 1], place.g_peer(step)
                    ),
                )
            )

    def finish(self, stage, out):
        place, quarter = self.place, self.quarter
        columns = pl.ds(pl.multiple_of(place.g * quarter, quarter), quarter)
        stage[:, columns] = self.from_x[self.block(place.g), :].astype(F32)
        for step, copy in self.over_g:
            copy.wait_recv()
            source = lax.rem(place.g + GROUP - step, GROUP)
            columns = pl.ds(pl.multiple_of(source * quarter, quarter), quarter)
            stage[:, columns] = self.from_g[step - 1].astype(F32)
        self.mover.local(stage, out).wait()


class ScatterDp:
    @staticmethod
    def sends(high):
        return 2 * high + high + high - 1

    @staticmethod
    def scratch(high, rows, width):
        return [
            pltpu.VMEM((2, high, rows, width), BF16),
            pltpu.VMEM((high, rows, width), BF16),
            pltpu.VMEM((max(high - 1, 1), rows, width), BF16),
        ]

    def __init__(self, place, mover, parts, out, from_y, from_l, from_h):
        self.place, self.mover, self.parts, self.out = place, mover, parts, out
        self.from_y, self.from_l, self.from_h = from_y, from_l, from_h
        self.rows = out.shape[0]

    def block(self, high, l_index, y_index):
        index = high * GROUP + l_index * 2 + y_index
        return self.parts.at[pl.ds(pl.multiple_of(index * self.rows, self.rows), self.rows)]

    def start(self):
        place = self.place
        self.owners = (1 - place.l, place.l)
        self.over_y = []
        for index, l_owner in enumerate(self.owners):
            for high in range(place.high):
                source = self.block(high, l_owner, 1 - place.y)
                self.over_y.append(
                    self.mover.send(source, self.from_y.at[index, high], place.y_peer)
                )

    def ready(self, index, extra=None):
        place = self.place
        for high in range(place.high):
            self.over_y[index * place.high + high].wait_recv()
            mine = self.block(high, self.owners[index], place.y)
            terms = [mine, self.from_y.at[index, high]]
            if extra is not None:
                extra[high].wait_recv()
                terms.append(self.from_l.at[high])
            add_rows(mine, terms, self.rows, 32)

    def forward_y(self):
        place = self.place
        self.ready(0)
        self.over_l = []
        for high in range(place.high):
            source = self.block(high, 1 - place.l, place.y)
            self.over_l.append(self.mover.send(source, self.from_l.at[high], place.l_peer))

    def forward_l(self):
        place = self.place
        self.ready(1, self.over_l)
        self.over_h = []
        for step in range(1, place.high):
            source = self.block(lax.rem(place.h + step, place.high), place.l, place.y)
            self.over_h.append(
                self.mover.send(source, self.from_h.at[step - 1], place.h_peer(step))
            )

    def finish(self):
        place = self.place
        for copy in self.over_h:
            copy.wait_recv()
        terms = [self.block(place.h, place.l, place.y)]
        terms += [self.from_h.at[step] for step in range(place.high - 1)]
        add_rows(self.out, terms, self.rows, 32)


class ScatterGroup:
    sends = 10

    @staticmethod
    def scratch(rows, width):
        return [
            pltpu.VMEM((GROUP, rows, width), BF16),
            pltpu.VMEM((6, rows // 2, width), BF16),
        ]

    def __init__(self, place, mover, parts, from_c, landed):
        self.place, self.mover, self.parts = place, mover, parts
        self.from_c, self.landed = from_c, landed
        self.owners = (place.gd, place.gy, place.gl, place.g)
        self.over_c = []
        half = from_c.shape[1] // 2
        self.low, self.top = pl.ds(0, half), pl.ds(half, half)

    def start(self, index):
        place = self.place
        source = self.parts.at[self.owners[index], 1 - place.c]
        self.over_c.append(self.mover.send(source, self.from_c.at[index], place.c_peer))

    def forward(self, index):
        place, mover, sums, landed = self.place, self.mover, self.from_c, self.landed
        low, top = self.low, self.top
        self.over_c[index].wait_recv()
        total = sums.at[index]
        own = self.parts.at[self.owners[index], place.c]
        add_rows(total, [total, own], total.shape[0], 32)
        if index == 0:
            self.y_diag = mover.send(sums.at[0, low], landed.at[0], place.y_peer)
            self.l_diag = mover.send(sums.at[0, top], landed.at[1], place.l_peer)
        if index == 1:
            self.y_own = mover.send(sums.at[1, low], landed.at[2], place.y_peer)
        if index == 2:
            self.l_own = mover.send(sums.at[2, top], landed.at[3], place.l_peer)

    def forward_diag(self):
        place, mover, sums, landed = self.place, self.mover, self.from_c, self.landed
        half = sums.shape[1] // 2
        low, top = self.low, self.top
        self.y_diag.wait_recv()
        add_rows(sums.at[2, low], [sums.at[2, low], landed.at[0]], half, 32)
        self.l_last = mover.send(sums.at[2, low], landed.at[4], place.l_peer)
        self.l_diag.wait_recv()
        add_rows(sums.at[1, top], [sums.at[1, top], landed.at[1]], half, 32)
        self.y_last = mover.send(sums.at[1, top], landed.at[5], place.y_peer)

    def finish(self, take):
        half = self.from_c.shape[1] // 2
        chunk = 32
        self.y_own.wait_recv()
        self.l_last.wait_recv()
        self.l_own.wait_recv()
        self.y_last.wait_recv()
        for base, first, second in ((0, 2, 4), (half, 3, 5)):

            def step(index, carry):
                rows = pl.ds(pl.multiple_of(base + index * chunk, chunk), chunk)
                inner = pl.ds(pl.multiple_of(index * chunk, chunk), chunk)
                total = self.from_c[3, rows, :].astype(F32)
                total = total + self.landed[first, inner, :].astype(F32)
                take(rows, total + self.landed[second, inner, :].astype(F32))
                return carry

            lax.fori_loop(0, half // chunk, step, 0)


def norm_back(values, gain, cotangent):
    scale = lax.rsqrt(jnp.mean(values * values, axis=-1, keepdims=True) + NORM_EPS)
    weighted = cotangent * gain
    inner = jnp.mean(weighted * values, axis=-1, keepdims=True)
    unit = values * scale
    return scale * (weighted - unit * (scale * inner)), cotangent * unit


def feed_forward_kernel(sizes, *refs):
    nm_hbm, wg_hbm, wu_hbm, wd_hbm, grad_y, resid, live, gains = refs[:8]
    mixed, grad_resid, full_proj, gain_sum, out_gd, out_gg, out_gu = refs[8:15]
    (nm, gy, wg, wu, wd, hidden, gate_grad, up_grad, part_nmlp, part_down, nmlp_c, nmlp_landed,
     down_c, down_landed, grad_proj, stage) = refs[15:31]
    send_sems, recv_sems, local_sems = refs[31:]
    place = Place(*sizes)
    mover = Mover(send_sems, recv_sems, local_sems)
    tokens, width = resid.shape
    cores = place.cores
    block = cores * tokens
    inner = wg.shape[1]
    tile = 256
    loads = [mover.local(wg_hbm, wg), mover.local(wu_hbm, wu)]
    nm_loads = [mover.local(nm_hbm.at[index], nm.at[index]) for index in range(GROUP)]
    wd_load = mover.local(wd_hbm, wd)
    greet([place.y_peer, place.l_peer, place.c_peer, place.x_peer])
    gather = GatherGroup(place, mover, grad_y, gy)
    gain_sum[...] = jnp.zeros_like(gain_sum)
    for copy in loads:
        copy.wait()

    def gate_up(index, carry):
        source = nm[index].reshape(block, width)
        rows = pl.ds(pl.multiple_of(index * block, block), block)
        for start in range(0, inner, tile):
            lanes = slice(start, start + tile)
            gate = jnp.dot(source, wg[:, lanes], preferred_element_type=F32)
            upper = jnp.dot(source, wu[:, lanes], preferred_element_type=F32)
            gain = 1.0 / (1.0 + jnp.exp(-gate))
            silu = gate * gain
            hidden[rows, lanes] = (silu * upper).astype(BF16)
            up_grad[rows, lanes] = silu.astype(BF16)
            gate_grad[rows, lanes] = (upper * (gain + silu * (1.0 - gain))).astype(BF16)
        return carry

    def weight_grads(source, grads, targets):
        copies = []
        count = len(grads)
        for index in range(width // tile):
            lanes = pl.ds(index * tile, tile)
            left = source[:, :, :, lanes].reshape(GROUP * block, tile)
            for which in range(count):
                slot = (index * count + which) % 2
                if len(copies) >= 2:
                    copies[-2].wait()
                stage[slot] = product(left, grads[which][...], CONTRACT_ROWS).astype(BF16)
                copies.append(mover.local(stage.at[slot], targets[which].at[lanes]))
        copies[-2].wait()
        copies[-1].wait()

    nm_loads[0].wait()
    nm_loads[1].wait()
    lax.fori_loop(0, 2, gate_up, 0)
    gather.forward()
    nm_loads[2].wait()
    nm_loads[3].wait()
    lax.fori_loop(2, GROUP, gate_up, 0)
    gather.finish_ici()
    wd_load.wait()

    def down_block(owner):
        rows = pl.ds(pl.multiple_of(owner * block, block), block)

        def step(index, carry):
            lanes = pl.ds(pl.multiple_of(index * tile, tile), tile)
            result = product(hidden[rows, :], wd[lanes, :], CONTRACT_COLS).astype(BF16)
            part_down[owner, :, :, lanes] = result.reshape(cores, tokens, tile)
            return carry

        lax.fori_loop(0, width // tile, step, 0)

    down = ScatterGroup(place, mover, part_down, down_c, down_landed)
    down_block(down.owners[0])
    down_block(down.owners[1])
    gather.finish()

    def back_block(owner):
        rows = pl.ds(pl.multiple_of(owner * block, block), block)
        source = gy[owner].reshape(block, width)
        for start in range(0, inner, tile):
            lanes = slice(start, start + tile)
            grad_mid = jnp.dot(source, wd[:, lanes], preferred_element_type=F32)
            gate_grad[rows, lanes] = (grad_mid * gate_grad[rows, lanes].astype(F32)).astype(BF16)
            up_grad[rows, lanes] = (grad_mid * up_grad[rows, lanes].astype(F32)).astype(BF16)

        def step(index, carry):
            lanes = pl.ds(pl.multiple_of(index * tile, tile), tile)
            result = product(gate_grad[rows, :], wg[lanes, :], CONTRACT_COLS)
            result = result + product(up_grad[rows, :], wu[lanes, :], CONTRACT_COLS)
            part_nmlp[owner, :, :, lanes] = result.astype(BF16).reshape(cores, tokens, tile)
            return carry

        lax.fori_loop(0, width // tile, step, 0)

    nmlp = ScatterGroup(place, mover, part_nmlp, nmlp_c, nmlp_landed)
    back_block(nmlp.owners[0])
    nmlp.start(0)
    back_block(nmlp.owners[1])
    nmlp.start(1)
    nmlp.forward(0)
    back_block(nmlp.owners[2])
    nmlp.start(2)
    nmlp.forward(1)
    back_block(nmlp.owners[3])
    nmlp.start(3)
    nmlp.forward(2)
    down_block(down.owners[2])
    nmlp.forward(3)
    nmlp.forward_diag()
    down_block(down.owners[3])
    for index in range(GROUP):
        down.start(index)

    def back_mlp(rows, total):
        grad, terms = norm_back(resid[rows, :], gains[:, width : 2 * width], total)
        grad = grad + grad_y[rows, :].astype(F32)
        grad_resid[rows, :] = grad
        grad_proj[rows, :] = grad.astype(BF16)
        gain_sum[...] += jnp.sum(terms, axis=0, keepdims=True)

    def mix(rows, total):
        mixed[rows, :] = ((resid[rows, :] + total) * live[rows, :]).astype(BF16)

    weight_grads(gy, [hidden], [out_gd])
    nmlp.finish(back_mlp)
    row = GatherSeq(place, mover, grad_proj, full_proj)
    for index in range(GROUP):
        down.forward(index)
    weight_grads(nm, [gate_grad, up_grad], [out_gg, out_gu])
    down.forward_diag()
    row.forward()
    down.finish(mix)
    row.finish()
    mover.finish()


def feed_forward(sizes, collective_id, args):
    dp_size, seq_size = sizes
    nm, wg, resid, gains = args[0], args[1], args[5], args[7]
    tokens, width = resid.shape
    inner = wg.shape[1]
    rows = GROUP * (seq_size // 2) * tokens
    outs = [
        ((tokens, width), BF16, VMEM),
        ((tokens, width), F32, VMEM),
        ((seq_size, tokens, width), BF16, HBM),
        ((1, width), F32, VMEM),
        ((width, inner), BF16, HBM),
        ((width, inner), BF16, HBM),
        ((width, inner), BF16, HBM),
    ]
    scratch = [pltpu.VMEM(nm.shape, BF16)] * 2
    scratch += [pltpu.VMEM((width, inner), BF16)] * 3
    scratch += [pltpu.VMEM((rows, inner), BF16)] * 3
    scratch += [pltpu.VMEM(nm.shape, BF16)] * 2
    scratch += ScatterGroup.scratch(tokens, width) * 2
    scratch += [pltpu.VMEM((tokens, width), BF16), pltpu.VMEM((2, 256, inner), BF16)]
    sends = 3 * 10 + GatherSeq.sends
    local = 9 + 3 * (width // 256)
    return pl.pallas_call(
        functools.partial(feed_forward_kernel, sizes),
        out_shape=[jax.ShapeDtypeStruct(shape, dtype) for shape, dtype, _ in outs],
        in_specs=[HBM] * 4 + [VMEM] * 4,
        out_specs=[spec for _, _, spec in outs],
        scratch_shapes=scratch + sems(sends, local),
        compiler_params=comm_params(collective_id, 63 * 1024 * 1024),
        name="feed_forward",
    )(*args)


def backward_kernel(sizes, *refs):
    (part_gd, part_gg, part_gu, wo, grad_resid, full_proj, moved, keep, gain_mlp, gains, cosine,
     sine, seg_col, pos_col, seg_row, pos_row, log_row, normed, full_qkv, lin, rot, attended,
     recv_map, send_map) = refs[:24]
    grad_hidden, gain_sums, out_gd, out_gg, out_gu, out_qkv, out_wo = refs[24:31]
    send_sems, recv_sems, local_sems = refs[-3:]
    scratch = list(refs[31:-3])

    def take(count):
        taken = scratch[:count]
        del scratch[:count]
        return taken

    place = Place(*sizes)
    mover = Mover(send_sems, recv_sems, local_sems)
    tokens, width = moved.shape
    parts = sizes[1]
    head = cosine.shape[1]
    query_width = attended.shape[1]
    key_width = (rot.shape[1] - query_width) // 2
    rotated = query_width + key_width
    columns = width // GROUP
    repeat = query_width // key_width
    column_stage, out_stage = take(2)
    grad_wo, grad_key, grad_query = take(3)
    mlp = [
        ScatterColumns(place, mover, part, *take(3)) for part in (part_gd, part_gg, part_gu)
    ]
    wo_sum = ScatterDp(place, mover, grad_wo, out_wo, *take(3))
    key_sum = ScatterDp(place, mover, grad_key, out_qkv.at[:, pl.ds(query_width, 2 * key_width)], *take(3))
    query_sum = ScatterDp(place, mover, grad_query, out_qkv.at[:, pl.ds(0, query_width)], *take(3))
    grad_moved, to_c, from_c, from_x = take(4)
    grad_att, grad_keys, grad_values, grad_lin, bias = take(5)
    blocks_out, blocks_in, rows_in, row_c, row_x = take(5)

    greet(dp_peers(place) + [place.x_peer, place.c_peer])
    lower, gate, upper = mlp
    gate.start_far()
    lower.start_far()
    upper.start_far()
    gain_sums[...] = jnp.zeros_like(gain_sums)
    gain_sums[:, width : 2 * width] = gain_mlp[...]
    grad_keys[...] = jnp.zeros_like(grad_keys)
    grad_values[...] = jnp.zeros_like(grad_values)

    def attended_grad(part, carry):
        spots = pl.ds(pl.multiple_of(part * tokens, tokens), tokens)
        for start in range(0, query_width, 256):
            result = jnp.dot(full_proj[part], wo[:, start : start + 256], preferred_element_type=F32)
            grad_att[spots, start : start + 256] = result.astype(BF16)
        return carry

    lax.fori_loop(0, parts, attended_grad, 0)

    def out_weight_grad(index, carry):
        lanes = pl.ds(pl.multiple_of(index * 256, 256), 256)
        source = full_proj[:, :, lanes].reshape(parts * tokens, 256)
        grad_wo[lanes, :] = product(source, attended[...], CONTRACT_ROWS).astype(BF16)
        return carry

    scale = head ** (-0.5)
    gain_query = gains[:, 2 * width : 2 * width + head]
    gain_key = gains[:, 2 * width + head : 2 * width + 2 * head]

    def unrotate(spots, lanes, grad, gain, gain_lanes):
        turned = grad * cosine[spots, :] - lane_swap(grad) * sine[spots, :]
        values, terms = norm_back(lin[spots, lanes].astype(F32), gain, turned)
        grad_lin[spots, lanes] = values.astype(BF16)
        gain_sums[:, gain_lanes] += jnp.sum(terms, axis=0, keepdims=True)

    for part in range(parts):
        keys = (part + 1) * tokens
        spots = pl.ds(part * tokens, tokens)
        allowed = (seg_col[:keys, :] == seg_row[:, spots]) & (pos_col[:keys, :] <= pos_row[:, spots])
        some = jnp.where(allowed, 0.0, MASKED)
        for copy in range(repeat):
            bias[:keys, copy * tokens : (copy + 1) * tokens] = some

        def attend(pair, carry):
            key_lanes = pl.ds(pl.multiple_of(query_width + pair * head, head), head)
            value_lanes = pl.ds(pl.multiple_of(rotated + pair * head, head), head)
            own_lanes = pl.ds(pl.multiple_of(pair * head, head), head)
            query_lanes = [
                pl.ds(pl.multiple_of((pair * repeat + copy) * head, head), head)
                for copy in range(repeat)
            ]
            queries = jnp.concatenate([rot[spots, lanes] for lanes in query_lanes], axis=0)
            grads = jnp.concatenate([grad_att[spots, lanes] for lanes in query_lanes], axis=0)
            key_rows, value_rows = rot[:keys, key_lanes], rot[:keys, value_lanes]
            scores = product(key_rows, queries, CONTRACT_COLS) * scale + bias[:keys, :]
            probs = jnp.exp(scores - log_row[pair, part])
            grad_values[:keys, own_lanes] += jnp.dot(
                probs.astype(BF16), grads, preferred_element_type=F32
            )
            grad_probs = product(value_rows, grads, CONTRACT_COLS)
            spread = jnp.sum(probs * grad_probs, axis=0, keepdims=True)
            grad_scores = (probs * (grad_probs - spread)).astype(BF16)
            grad_keys[:keys, own_lanes] += jnp.dot(
                grad_scores, queries, preferred_element_type=F32
            )
            grad_queries = product(grad_scores, key_rows, CONTRACT_ROWS) * scale
            for copy in range(repeat):
                unrotate(
                    spots,
                    query_lanes[copy],
                    grad_queries[copy * tokens : (copy + 1) * tokens],
                    gain_query,
                    pl.ds(2 * width, head),
                )
            return carry

        lax.fori_loop(0, key_width // head, attend, 0)
        if part == 0:
            gate.forward_far(column_stage)
        if part == parts - 2:
            lax.fori_loop(0, width // 256, out_weight_grad, 0)
            lower.forward_far(column_stage)
            wo_sum.start()
            for columns_sum in (gate, upper, lower):
                columns_sum.start_near()
    for pair in range(key_width // head):

        def back_keys(part, carry):
            spots = pl.ds(pl.multiple_of(part * tokens, tokens), tokens)
            lanes = pl.ds(pair * head, head)
            unrotate(
                spots,
                pl.ds(query_width + pair * head, head),
                grad_keys[spots, lanes] * scale,
                gain_key,
                pl.ds(2 * width + head, head),
            )
            grad_lin[spots, pl.ds(rotated + pair * head, head)] = grad_values[spots, lanes].astype(
                BF16
            )
            return carry

        lax.fori_loop(0, parts, back_keys, 0)

    def weight_grad(target, start, size):
        def step(index, carry):
            lanes = pl.ds(pl.multiple_of(index * 256, 256), 256)
            source = normed[:, :, lanes].reshape(parts * tokens, 256)
            target[lanes, :] = product(
                source, grad_lin[:, start : start + size], CONTRACT_ROWS
            ).astype(BF16)
            return carry

        lax.fori_loop(0, width // 256, step, 0)

    wo_sum.forward_y()
    weight_grad(grad_query, 0, query_width)
    weight_grad(grad_key, query_width, 2 * key_width)
    query_sum.start()
    gate.add_near(column_stage)
    upper.forward_far(column_stage)
    gate.forward_high()

    def normed_grad(part, target):
        source = grad_lin[pl.ds(pl.multiple_of(part * tokens, tokens), tokens), :]

        def step(index, carry):
            block = pl.ds(pl.multiple_of(index * 256, 256), 256)
            target[:, block] = product(source, full_qkv[block, :], CONTRACT_COLS).astype(BF16)
            return carry

        lax.fori_loop(0, width // 256, step, 0)

    cores = place.cores
    places = ((1 - place.x) * cores, place.x * cores)
    normed_grad(places[0] + 1 - place.c, to_c.at[0])
    over_c = [mover.send(to_c.at[0], from_c.at[0], place.c_peer)]
    normed_grad(places[0] + place.c, to_c.at[1])
    over_c[0].wait_recv()
    add_rows(to_c.at[1], [to_c.at[1], from_c.at[0]], tokens, 32)
    over_x = mover.send(to_c.at[1], from_x, place.x_peer)
    query_sum.forward_y()
    key_sum.start()
    lower.add_near(column_stage)
    lower.forward_high()
    normed_grad(places[1] + 1 - place.c, to_c.at[2])
    over_c.append(mover.send(to_c.at[2], from_c.at[1], place.c_peer))
    normed_grad(places[1] + place.c, to_c.at[3])
    upper.add_near(column_stage)
    gate.finish(out_stage, out_gg)
    query_sum.forward_l()
    wo_sum.forward_l()
    key_sum.forward_y()
    key_sum.forward_l()
    upper.forward_high()
    over_c[1].wait_recv()
    over_x.wait_recv()

    def back_normed(index, carry):
        rows = pl.ds(pl.multiple_of(index * 32, 32), 32)
        total = to_c[3, rows, :].astype(F32) + from_c[1, rows, :].astype(F32)
        total = total + from_x[rows, :].astype(F32)
        grad, terms = norm_back(moved[rows, :].astype(F32), gains[:, :width], total)
        grad_moved[rows, :] = (grad_resid[rows, :] + grad).astype(BF16)
        gain_sums[:, :width] += jnp.sum(terms, axis=0, keepdims=True)
        return carry

    lax.fori_loop(0, tokens // 32, back_normed, 0)
    piece_row = index_of((place.dp_size * 16, 1), 0) & 3
    for q in range(GROUP):
        lanes = pl.ds(q * columns, columns)
        piece = product(recv_map[...], grad_moved[:, lanes], CONTRACT_ROWS)
        piece = jnp.where(piece_row == q, piece, 0.0)
        total = piece if q == 0 else total + piece
    blocks_out[...] = total.astype(BF16).reshape(blocks_out.shape)
    copies = []
    for step in range(1, place.dp_size):
        other = lax.rem(place.d + step, place.dp_size)
        copies.append(mover.send(blocks_out.at[other], blocks_in.at[place.d], (other, place.s)))
        copies.append(mover.send(gain_sums, rows_in.at[place.d], (other, place.s)))
    blocks_in[place.d] = blocks_out[place.d]
    rows_in[place.d] = gain_sums[...]
    query_sum.finish()
    for copy in copies:
        copy.wait_recv()
    row_total = rows_in[0]
    for index in range(1, place.dp_size):
        row_total = row_total + rows_in[index]
    row_c[0] = row_total
    pass_c = mover.send(row_c.at[0], row_c.at[1], place.c_peer)
    returned = blocks_in[...].reshape(place.dp_size * 16, columns)
    for q in range(GROUP):
        lanes = pl.ds(q * columns, columns)
        chosen = jnp.where(piece_row == q, returned, jnp.zeros_like(returned))
        here = product(send_map[...], chosen, CONTRACT_ROWS)
        here = here + jnp.where(keep[...] > 0.0, grad_moved[:, lanes].astype(F32), 0.0)
        grad_hidden[:, lanes] = here.astype(BF16)
    pass_c.wait_recv()
    row_x[0] = row_c[0] + row_c[1]
    pass_x = mover.send(row_x.at[0], row_x.at[1], place.x_peer)
    lower.finish(out_stage, out_gd)
    upper.finish(out_stage, out_gu)
    wo_sum.finish()
    key_sum.finish()
    pass_x.wait_recv()
    mover.finish()
    gain_sums[...] = row_x[0] + row_x[1]


def backward(sizes, collective_id, args):
    dp_size, seq_size = sizes
    part_gd, wo, moved, gains = args[0], args[3], args[6], args[9]
    rot, attended = args[20], args[21]
    tokens, width = moved.shape
    high = dp_size // GROUP
    rows = width // dp_size
    quarter = part_gd.shape[1] // 2
    row_len = seq_size * tokens
    query_width = attended.shape[1]
    key_width = (rot.shape[1] - query_width) // 2
    repeat = query_width // key_width
    outs = [
        ((tokens, width), BF16, VMEM),
        (gains.shape, F32, VMEM),
        ((rows, GROUP * quarter), F32, HBM),
        ((rows, GROUP * quarter), F32, HBM),
        ((rows, GROUP * quarter), F32, HBM),
        ((rows, rot.shape[1]), F32, VMEM),
        ((rows, query_width), F32, VMEM),
    ]
    piece = min(GROUP * rows, ScatterColumns.stage_rows)
    scratch = [
        pltpu.VMEM((2, piece, quarter), BF16),
        pltpu.VMEM((rows, GROUP * quarter), F32),
    ]
    scratch += [
        pltpu.VMEM(wo.shape, BF16),
        pltpu.VMEM((width, 2 * key_width), BF16),
        pltpu.VMEM((width, query_width), BF16),
    ]
    for _ in range(3):
        scratch += ScatterColumns.scratch(high, rows, quarter)
    scratch += ScatterDp.scratch(high, rows, query_width)
    scratch += ScatterDp.scratch(high, rows, 2 * key_width)
    scratch += ScatterDp.scratch(high, rows, query_width)
    scratch += [
        pltpu.VMEM((tokens, width), BF16),
        pltpu.VMEM((seq_size, tokens, width), BF16),
        pltpu.VMEM((2, tokens, width), BF16),
        pltpu.VMEM((tokens, width), BF16),
        pltpu.VMEM((row_len, query_width), BF16),
        pltpu.VMEM((row_len, key_width), F32),
        pltpu.VMEM((row_len, key_width), F32),
        pltpu.VMEM((row_len, rot.shape[1]), BF16),
        pltpu.VMEM((row_len, repeat * tokens), F32),
        pltpu.VMEM((dp_size, 16, width // GROUP), BF16),
        pltpu.VMEM((dp_size, 16, width // GROUP), BF16),
        pltpu.VMEM((dp_size,) + gains.shape, F32),
        pltpu.VMEM((2,) + gains.shape, F32),
        pltpu.VMEM((2,) + gains.shape, F32),
    ]
    sends = 3 * (2 * high + 2) + 3 * ScatterDp.sends(high)
    sends += 3 + 2 * (dp_size - 1) + 2
    local = 3 * (high * GROUP * rows // piece + 1)
    return pl.pallas_call(
        functools.partial(backward_kernel, sizes),
        out_shape=[jax.ShapeDtypeStruct(shape, dtype) for shape, dtype, _ in outs],
        in_specs=[HBM] * 3 + [VMEM] * 21,
        out_specs=[spec for _, _, spec in outs],
        scratch_shapes=scratch + sems(sends, local),
        compiler_params=comm_params(collective_id, 63 * 1024 * 1024),
        name="backward_attention",
    )(*args)


def per_device(
    sizes,
    hidden_in,
    valid_len,
    doc_lengths,
    doc_perm,
    attn_norm,
    w_query,
    key_weight,
    value_weight,
    w_out,
    query_norm,
    key_norm_gain,
    mlp_norm,
    w_gate,
    w_up,
    w_down,
    out_grad,
):
    model_width = hidden_in.shape[1]
    seq_count, row_count, _ = doc_lengths.shape
    my_row = lax.axis_index("dp")
    my_part = lax.axis_index("seq")
    head_size = query_norm.shape[0] * row_count
    lengths = doc_lengths.reshape(seq_count, -1)
    (
        moved_low,
        gains,
        normed,
        qkv_mat,
        out_mat,
        gate_mat,
        up_mat,
        down_mat,
        grad_y_own,
        rotated_lin,
        rotated_all,
        attended,
        log_total,
        resid_rows,
        normed_mlp,
        cosine,
        sine,
        seg_col,
        pos_col,
        seg_row,
        pos_row,
        keep,
        live,
        send_map,
        recv_map,
    ) = forward(
        sizes,
        1,
        head_size,
        (
            hidden_in,
            valid_len[None, :],
            lengths[:, None, :],
            doc_perm[:, None, :],
            lengths[:, :, None],
            doc_perm[:, :, None],
            attn_norm[None, :],
            mlp_norm[None, :],
            query_norm[None, :],
            key_norm_gain[None, :],
            out_grad,
            w_query,
            key_weight,
            value_weight,
            w_out.T,
            w_gate,
            w_up,
            w_down.T,
        ),
    )
    cuts = (model_width, 2 * model_width, 2 * model_width + head_size)
    query_width = w_query.shape[1]
    key_width = key_weight.shape[1]
    qkv_cuts = (query_width, query_width + key_width)
    mixed, grad_resid, grad_proj, gain_mlp_sum, grad_down, grad_gate, grad_up = feed_forward(
        sizes,
        2,
        (normed_mlp, gate_mat, up_mat, down_mat, grad_y_own, resid_rows, live, gains),
    )
    grad_hidden, gain_sums, out_down, out_gate, out_up, out_qkv, out_wo = backward(
        sizes,
        3,
        (
            grad_down,
            grad_gate,
            grad_up,
            out_mat,
            grad_resid,
            grad_proj,
            moved_low,
            keep,
            gain_mlp_sum,
            gains,
            cosine,
            sine,
            seg_col,
            pos_col,
            seg_row,
            pos_row,
            jnp.swapaxes(log_total, 2, 3),
            normed,
            qkv_mat,
            rotated_lin,
            rotated_all,
            attended,
            recv_map,
            send_map,
        ),
    )
    out_query, out_key, out_value = jnp.split(out_qkv, qkv_cuts, axis=1)
    device = my_row * seq_count + my_part

    def own_piece(vector):
        size = vector.shape[0] // (row_count * seq_count)
        return lax.dynamic_slice_in_dim(vector, device * size, size)

    sum_attn, sum_mlp, sum_query, sum_key = [own_piece(v) for v in jnp.split(gain_sums[0], cuts)]
    return (
        mixed,
        grad_hidden,
        sum_attn,
        out_query,
        out_key,
        out_value,
        out_wo.T,
        sum_query,
        sum_key,
        sum_mlp,
        out_gate,
        out_up,
        out_down.T,
    )


def solution(mesh):
    in_specs = (
        P(("dp", "seq"), None),
        P(),
        P(),
        P(),
        P("dp"),
        P("dp", "seq"),
        P("dp", "seq"),
        P("dp", "seq"),
        P("seq", "dp"),
        P("dp"),
        P("dp"),
        P("dp"),
        P("dp", "seq"),
        P("dp", "seq"),
        P("seq", "dp"),
        P(("dp", "seq"), None),
    )
    out_specs = (
        P(("dp", "seq"), None),
        P(("dp", "seq"), None),
        P(("dp", "seq")),
        P("dp", "seq"),
        P("dp", "seq"),
        P("dp", "seq"),
        P("seq", "dp"),
        P(("dp", "seq")),
        P(("dp", "seq")),
        P(("dp", "seq")),
        P("dp", "seq"),
        P("dp", "seq"),
        P("seq", "dp"),
    )
    return jax.shard_map(
        functools.partial(per_device, (mesh.shape["dp"], mesh.shape["seq"])), mesh=mesh, in_specs=in_specs, out_specs=out_specs, check_vma=False
    )
```

```python
import functools
import math

import jax
import jax.numpy as jnp
from jax import lax
from jax.experimental import pallas as pl
from jax.experimental.pallas import tpu as pltpu
from jax.sharding import PartitionSpec as P

MAXSHORT = 4
GROUP = 4
MESH = pl.DeviceIdType.MESH
HBM = pl.BlockSpec(memory_space=pltpu.HBM)
VMEM = pl.BlockSpec(memory_space=pltpu.VMEM)
BF16 = jnp.bfloat16
F32 = jnp.float32


NORM_EPS = 1e-06
ROPE_BASE = 1000000.0
MASKED = -1e30
CONTRACT_ROWS = (((0,), (0,)), ((), ()))
CONTRACT_COLS = (((1,), (1,)), ((), ()))


def product(left, right, dims):
    return lax.dot_general(left, right, dims, preferred_element_type=jnp.float32)


class Place:
    def __init__(self, dp_size, seq_size):
        self.dp_size = dp_size
        self.seq_size = seq_size
        self.high = dp_size // GROUP
        self.cores = seq_size // 2
        self.d = lax.axis_index("dp")
        self.s = lax.axis_index("seq")
        self.g = lax.rem(self.d, GROUP)
        self.h = lax.div(self.d, GROUP)
        self.x = lax.div(self.s, self.cores)
        self.c = lax.rem(self.s, self.cores)
        self.y = lax.rem(self.g, 2)
        self.l = lax.div(self.g, 2)
        self.gy = self.g + 1 - 2 * self.y
        self.gl = lax.rem(self.g + 2, GROUP)
        self.gd = 3 - self.g
        self.y_peer = (self.h * GROUP + self.gy, self.s)
        self.l_peer = (self.h * GROUP + self.gl, self.s)
        self.d_peer = (self.h * GROUP + self.gd, self.s)
        self.x_peer = (self.d, (1 - self.x) * self.cores + self.c)
        self.c_peer = (self.d, self.x * self.cores + 1 - self.c)

    def h_peer(self, step):
        return (lax.rem(self.h + step, self.high) * GROUP + self.g, self.s)

    def h_from(self, step):
        return lax.rem(self.h + self.high - step, self.high)

    def g_peer(self, step):
        return (self.h * GROUP + lax.rem(self.g + step, GROUP), self.s)


class Mover:
    def __init__(self, send_sems, recv_sems, local_sems):
        self.send_sems = send_sems
        self.recv_sems = recv_sems
        self.local_sems = local_sems
        self.count = 0
        self.local_count = 0
        self.sent = []

    def send(self, source, target, device):
        index = self.count
        self.count += 1
        copy = pltpu.make_async_remote_copy(
            src_ref=source,
            dst_ref=target,
            send_sem=self.send_sems.at[index],
            recv_sem=self.recv_sems.at[index],
            device_id=device,
            device_id_type=MESH,
        )
        copy.start()
        self.sent.append(copy)
        return copy

    def local(self, source, target):
        index = self.local_count
        self.local_count += 1
        copy = pltpu.make_async_copy(source, target, self.local_sems.at[index])
        copy.start()
        return copy

    def drain(self, copy):
        copy.wait_send()
        self.sent = [other for other in self.sent if other is not copy]

    def finish(self):
        for copy in self.sent:
            copy.wait_send()


def greet(peers):
    barrier = pltpu.get_barrier_semaphore()
    for peer in peers:
        pl.semaphore_signal(barrier, inc=1, device_id=peer, device_id_type=MESH)
    pl.semaphore_wait(barrier, len(peers))


def dp_peers(place):
    return [
        (lax.rem(place.d + step, place.dp_size), place.s) for step in range(1, place.dp_size)
    ]


def sems(count, local):
    return [
        pltpu.SemaphoreType.DMA((count,)),
        pltpu.SemaphoreType.DMA((count,)),
        pltpu.SemaphoreType.DMA((max(local, 1),)),
    ]


def comm_params(collective_id, vmem=None):
    return pltpu.CompilerParams(
        collective_id=collective_id,
        has_side_effects=True,
        vmem_limit_bytes=vmem if vmem is not None else 60 * 1024 * 1024,
    )


def add_rows(target, terms, rows, chunk):
    def step(index, carry):
        part = pl.ds(pl.multiple_of(index * chunk, chunk), chunk)
        total = terms[0][part, :].astype(F32)
        for term in terms[1:]:
            total = total + term[part, :].astype(F32)
        target[part, :] = total.astype(target.dtype)
        return carry

    lax.fori_loop(0, rows // chunk, step, 0)


class GatherSeq:
    sends = 3

    def __init__(self, place, mover, own, full):
        self.place, self.mover, self.full = place, mover, full
        self.local = mover.local(own, full.at[place.s])
        self.over_x = mover.send(own, full.at[place.s], place.x_peer)
        self.over_c = mover.send(own, full.at[place.s], place.c_peer)

    def forward(self):
        self.over_x.wait_recv()
        block = self.full.at[self.place.x_peer[1]]
        self.passed = self.mover.send(block, block, self.place.c_peer)

    def finish(self):
        self.local.wait()
        self.over_c.wait_recv()
        self.passed.wait_recv()


class GatherGroup:
    sends = 10

    def __init__(self, place, mover, own, full):
        self.place, self.mover, self.full = place, mover, full
        half = own.shape[0] // 2
        self.low, self.top = pl.ds(0, half), pl.ds(half, half)
        self.local = mover.local(own, full.at[place.g, place.c])
        spot = full.at[place.g, place.c]
        self.y_low = mover.send(own.at[self.low], spot.at[self.low], place.y_peer)
        self.l_top = mover.send(own.at[self.top], spot.at[self.top], place.l_peer)
        self.y_top = mover.send(own.at[self.top], spot.at[self.top], place.y_peer)
        self.l_low = mover.send(own.at[self.low], spot.at[self.low], place.l_peer)
        self.core = [mover.send(own, spot, place.c_peer)]

    def forward(self):
        place, mover, full = self.place, self.mover, self.full
        self.y_low.wait_recv()
        part = full.at[place.gy, place.c, self.low]
        self.d_low = mover.send(part, part, place.l_peer)
        self.l_top.wait_recv()
        part = full.at[place.gl, place.c, self.top]
        self.d_top = mover.send(part, part, place.y_peer)
        self.y_top.wait_recv()
        part = full.at[place.gy, place.c]
        self.core.append(mover.send(part, part, place.c_peer))
        self.l_low.wait_recv()
        part = full.at[place.gl, place.c]
        self.core.append(mover.send(part, part, place.c_peer))

    def finish_ici(self):
        place = self.place
        self.d_low.wait_recv()
        self.d_top.wait_recv()
        part = self.full.at[place.gd, place.c]
        self.core.append(self.mover.send(part, part, place.c_peer))

    def finish(self):
        self.local.wait()
        for copy in self.core:
            copy.wait_recv()


class GatherDp:
    def __init__(self, place, mover, pieces, full):
        self.place, self.mover, self.full, self.pieces = place, mover, full, pieces
        first, last = pieces[0], pieces[-1]
        self.window = pl.ds(first[1], last[1] + last[2] - first[1])
        self.rows = full.shape[0] // place.dp_size
        own_rows = self.block(place.d)
        self.spots = [full.at[own_rows, pl.ds(start, size)] for _, start, size in pieces]
        self.local = [
            mover.local(piece[0], spot) for piece, spot in zip(pieces, self.spots)
        ]
        self.over_y, self.passed_l = [], []

    def block(self, index):
        return pl.ds(pl.multiple_of(index * self.rows, self.rows), self.rows)

    def own_to(self, peer):
        return [
            self.mover.send(piece[0], spot, peer) for piece, spot in zip(self.pieces, self.spots)
        ]

    def send_h(self):
        place = self.place
        self.over_h = [self.own_to(place.h_peer(step)) for step in range(1, place.high)]

    def send_l(self):
        self.own_l = self.own_to(self.place.l_peer)

    def send_y(self):
        self.over_y += self.own_to(self.place.y_peer)

    def part(self, high, index):
        return self.full.at[self.block(high * GROUP + index), self.window]

    def pass_h_to_l(self):
        place = self.place
        for step, copies in enumerate(self.over_h, 1):
            for copy in copies:
                copy.wait_recv()
            part = self.part(place.h_from(step), place.g)
            self.passed_l.append(self.mover.send(part, part, place.l_peer))

    def pass_h_to_y(self):
        place = self.place
        for step in range(1, place.high):
            part = self.part(place.h_from(step), place.g)
            self.over_y.append(self.mover.send(part, part, place.y_peer))

    def pass_own_l_to_y(self):
        place = self.place
        for copy in self.own_l:
            copy.wait_recv()
        part = self.part(place.h, place.gl)
        self.over_y.append(self.mover.send(part, part, place.y_peer))

    def pass_l_to_y(self):
        place = self.place
        for step, copy in enumerate(self.passed_l, 1):
            copy.wait_recv()
            part = self.part(place.h_from(step), place.gl)
            self.over_y.append(self.mover.send(part, part, place.y_peer))

    def finish(self):
        for copy in self.local:
            copy.wait()
        for copy in self.over_y:
            copy.wait_recv()


class GatherColumns:
    def __init__(self, place, mover, own, full):
        self.place, self.mover, self.full, self.own = place, mover, full, own
        self.quarter = own.shape[1] // GROUP
        self.rows = own.shape[0]
        self.near = pl.ds(0, self.quarter)
        self.far = pl.ds(self.quarter, self.quarter)

    def block(self, high):
        rows = GROUP * self.rows
        return pl.ds(pl.multiple_of(high * rows, rows), rows)

    def send_g(self, spot=None):
        place, mover, own = self.place, self.mover, self.own
        if spot is None:
            spot = self.full.at[
                pl.ds(pl.multiple_of(place.d * self.rows, self.rows), self.rows), self.near
            ]
        self.over_g = []
        for step in (3, 1, 2):
            to = lax.rem(place.g + step, GROUP)
            columns = pl.ds(pl.multiple_of(to * self.quarter, self.quarter), self.quarter)
            self.over_g.append(mover.send(own.at[:, columns], spot, place.g_peer(step)))
        columns = pl.ds(pl.multiple_of(place.g * self.quarter, self.quarter), self.quarter)
        self.local = mover.local(own.at[:, columns], spot)

    def wait_g(self):
        self.local.wait()
        for copy in self.over_g:
            copy.wait_recv()

    def send_h(self, source=None):
        place = self.place
        near = self.full.at[self.block(place.h), self.near]
        source = near if source is None else source
        self.over_h = [
            self.mover.send(source, near, place.h_peer(step)) for step in range(1, place.high)
        ]

    def send_x(self, source=None):
        place = self.place
        rows = self.block(place.h)
        source = self.full.at[rows, self.near] if source is None else source
        self.over_x = [self.mover.send(source, self.full.at[rows, self.far], place.x_peer)]

    def pass_h_to_x(self):
        place = self.place
        for step, copy in enumerate(self.over_h, 1):
            copy.wait_recv()
            rows = self.block(place.h_from(step))
            self.over_x.append(
                self.mover.send(
                    self.full.at[rows, self.near], self.full.at[rows, self.far], place.x_peer
                )
            )

    def finish(self):
        for copy in self.over_x:
            copy.wait_recv()


def lane_swap(values):
    half = values.shape[-1] // 2
    return jnp.concatenate([values[:, half:], values[:, :half]], axis=-1)


def norm_rows(values, gain):
    scale = lax.rsqrt(jnp.mean(values * values, axis=-1, keepdims=True) + NORM_EPS)
    return values * scale * gain


def index_of(shape, dim):
    return lax.broadcasted_iota(jnp.int32, shape, dim)


def total_of(condition, values, axis):
    picked = jnp.where(condition, values.astype(F32), 0.0)
    return jnp.sum(picked, axis=axis, keepdims=True)


class Layout:
    def __init__(self, refs, part, row_count, body):
        len_row, perm_row, len_col, perm_col = refs
        docs = len_row.shape[-1]
        self.docs, self.body, self.row_count = docs, body, row_count
        self.bits = (docs // row_count).bit_length() - 1
        down, along = index_of((docs, docs), 0), index_of((docs, docs), 1)
        same_row = (down >> self.bits) == (along >> self.bits)
        before = jnp.where(same_row & (down < along), 1.0, 0.0).astype(BF16)
        self.lens = len_row[part].astype(F32)
        self.lens_col = len_col[part].astype(F32)
        perm, perm_of_col = perm_row[part], perm_col[part]
        matched = perm_of_col == along
        self.dest, self.dest_col = perm >> self.bits, perm_of_col >> self.bits
        self.starts = body + jnp.dot(self.lens.astype(BF16), before, preferred_element_type=F32)
        placed = total_of(matched, jnp.broadcast_to(self.lens_col, matched.shape), 0)
        new_at = body + jnp.dot(placed.astype(BF16), before, preferred_element_type=F32)
        self.new_col = total_of(matched, jnp.broadcast_to(new_at, matched.shape), 1)
        self.new = product(
            new_at.astype(BF16), jnp.where(matched, 1.0, 0.0).astype(BF16), CONTRACT_COLS
        )

    def labels(self, part, row, valid, tokens, row_len, column):
        shape = (tokens, self.docs) if column else (self.docs, tokens)
        axis = 1 if column else 0
        slot, doc = index_of(shape, 1 - axis).astype(F32), index_of(shape, axis)
        start, size, dest = (
            (self.new, self.lens, self.dest)
            if column
            else (self.new_col, self.lens_col, self.dest_col)
        )
        inside = (dest == row) & (slot >= start) & (slot < start + size)
        first = self.row_count + part * self.docs
        segment = total_of(inside, doc + first, axis).astype(jnp.int32)
        position = total_of(inside, slot - start, axis).astype(jnp.int32)
        here = total_of(inside, jnp.ones(shape, F32), axis) > 0.0
        local = index_of((tokens, 1) if column else (1, tokens), 1 - axis)
        long_position = part * self.body + local
        in_long = (local < self.body) & (long_position.astype(F32) < valid)
        empty = -1 - (row * row_len + part * tokens + local)
        segment = jnp.where(in_long, row, jnp.where(here, segment, empty))
        return segment, jnp.where(in_long, long_position, position), in_long, in_long | here

    def send_map(self, row, tokens):
        shape = (self.row_count * 16, self.docs)
        target, doc = index_of(shape, 0) >> 4, index_of(shape, 1)
        mine = ((doc >> self.bits) == row) & (self.dest == target)
        start = total_of(mine, jnp.broadcast_to(self.starts, shape), 1)
        size = total_of(mine, jnp.broadcast_to(self.lens, shape), 1)
        shape = (shape[0], tokens)
        token = ((index_of(shape, 0) >> 2) & 3).astype(F32)
        slot = index_of(shape, 1).astype(F32)
        return jnp.where((token < size) & (slot == start + token), 1.0, 0.0).astype(BF16)

    def recv_map(self, row, tokens):
        shape = (self.docs, self.row_count * 16)
        source, doc = index_of(shape, 1) >> 4, index_of(shape, 0)
        mine = ((doc >> self.bits) == source) & (self.dest_col == row)
        start = total_of(mine, jnp.broadcast_to(self.new_col, shape), 0)
        size = total_of(mine, jnp.broadcast_to(self.lens_col, shape), 0)
        shape = (tokens, shape[1])
        token = ((index_of(shape, 1) >> 2) & 3).astype(F32)
        slot = index_of(shape, 0).astype(F32)
        return jnp.where((token < size) & (slot == start + token), 1.0, 0.0).astype(BF16)


def spread_piece(piece, place, total):
    size = piece.shape[1]
    shape = (size, total)
    spot = index_of(shape, 1) == index_of(shape, 0) + place.d * size
    return jnp.dot(piece, jnp.where(spot, 1.0, 0.0).astype(BF16), preferred_element_type=F32)


def forward_kernel(sizes, *refs):
    (hidden, valid_row, len_row, perm_row, len_col, perm_col, attn_gain, mlp_gain, query_gain,
     key_gain, out_grad, wq, wk, wv, wo, wg, wu, wd) = refs[:18]
    (moved, gains, normed_out, qkv_out, wo_out, full_g, full_u, full_d, grad_y, lin_out, rot_out,
     attended_out, log_total, resid, full_nm, cosine, sine, seg_col, pos_col, seg_row, pos_row, keep, live,
     send_map, recv_map) = refs[18:43]
    (blocks_out, blocks_in, rows_in, gain_row, part_seg, part_pos, normed_own, bias, part_own,
     from_c, from_x, to_c, nm_own, normed, full_qkv, full_wo, lin, rot, attended, send_sems,
     recv_sems, local_sems) = refs[43:]
    place = Place(*sizes)
    mover = Mover(send_sems, recv_sems, local_sems)
    tokens, width = hidden.shape
    head = cosine.shape[1]
    query_width, key_width = wq.shape[1], wk.shape[1]
    columns = width // GROUP
    parts = sizes[1]
    repeat = query_width // key_width

    greet(dp_peers(place) + [place.x_peer, place.c_peer])
    key_parts = [(wk, query_width, key_width), (wv, query_width + key_width, key_width)]
    query = GatherDp(place, mover, [(wq, 0, query_width)], full_qkv)
    key = GatherDp(place, mover, key_parts, full_qkv)
    out = GatherDp(place, mover, [(wo, 0, wo.shape[1])], full_wo)
    gate = GatherColumns(place, mover, wg, full_g)
    upper = GatherColumns(place, mover, wu, full_u)
    lower = GatherColumns(place, mover, wd, full_d)
    gate.send_g()
    key.send_h()
    lower.send_g()
    row_len = parts * tokens
    body = tokens - (len_row.shape[2] // place.dp_size) * MAXSHORT
    layout_refs = (len_row, perm_row, len_col, perm_col)
    here = index_of(valid_row.shape, 1) == place.d
    valid = total_of(here, valid_row[...], 1)
    own = Layout(layout_refs, place.s, place.dp_size, body)
    send_map[...] = own.send_map(place.d, tokens)
    recv_map[...] = own.recv_map(place.d, tokens)
    _, _, own_long, own_live = own.labels(place.s, place.d, valid, tokens, row_len, True)
    keep[...] = jnp.where(own_long, 1.0, 0.0)
    live[...] = jnp.where(own_live, 1.0, 0.0)
    gain_row[:, :width] = spread_piece(attn_gain[...], place, width)
    gain_row[:, width : 2 * width] = spread_piece(mlp_gain[...], place, width)
    gain_row[:, 2 * width : 2 * width + head] = spread_piece(query_gain[...], place, head)
    gain_row[:, 2 * width + head :] = spread_piece(key_gain[...], place, head)
    piece_row = index_of((place.dp_size * 16, 1), 0) & 3
    for q in range(GROUP):
        lanes = pl.ds(q * columns, columns)
        piece = jnp.dot(send_map[...], hidden[:, lanes], preferred_element_type=F32)
        piece = jnp.where(piece_row == q, piece, 0.0)
        total = piece if q == 0 else total + piece
    blocks_out[...] = total.astype(BF16).reshape(blocks_out.shape)
    copies = []
    for step in range(1, place.dp_size):
        other = lax.rem(place.d + step, place.dp_size)
        copies.append(mover.send(blocks_out.at[other], blocks_in.at[place.d], (other, place.s)))
        copies.append(mover.send(gain_row, rows_in.at[place.d], (other, place.s)))
    blocks_in[place.d] = blocks_out[place.d]
    rows_in[place.d] = gain_row[...]
    for copy in copies:
        copy.wait_recv()
    all_gains = rows_in[0]
    for index in range(1, place.dp_size):
        all_gains = all_gains + rows_in[index]
    gains[...] = all_gains
    incoming = blocks_in[...].reshape(place.dp_size * 16, columns)
    for q in range(GROUP):
        lanes = pl.ds(q * columns, columns)
        chosen = jnp.where(piece_row == q, incoming, jnp.zeros_like(incoming))
        here = jnp.dot(recv_map[...], chosen, preferred_element_type=F32)
        here = here + jnp.where(keep[...] > 0.0, hidden[:, lanes].astype(F32), 0.0)
        moved[:, lanes] = here.astype(BF16)

    def norm_moved(index, carry):
        rows = pl.ds(pl.multiple_of(index * 32, 32), 32)
        normed_own[rows, :] = norm_rows(moved[rows, :].astype(F32), gains[:, :width]).astype(BF16)
        grad_y[rows, :] = (out_grad[rows, :].astype(F32) * live[rows, :]).astype(BF16)
        return carry

    lax.fori_loop(0, tokens // 32, norm_moved, 0)
    row = GatherSeq(place, mover, normed_own, normed)

    def label_part(part, carry):
        layout = Layout(layout_refs, part, place.dp_size, body)
        spots = pl.ds(pl.multiple_of(part * tokens, tokens), tokens)
        segment, position, _, _ = layout.labels(part, place.d, valid, tokens, row_len, True)
        seg_col[spots, :], pos_col[spots, :] = segment, position
        segment, position, _, _ = layout.labels(part, place.d, valid, tokens, row_len, False)
        part_seg[part], part_pos[part] = segment, position
        half = head // 2
        lane = index_of((1, head), 1)
        power = jnp.where(lane < half, lane, lane - half).astype(F32)
        angles = pos_col[spots, :].astype(F32) * jnp.exp(
            power * (-2.0 * math.log(ROPE_BASE) / head)
        )
        cosine[spots, :] = jnp.cos(angles)
        sine[spots, :] = jnp.where(lane < half, -1.0, 1.0) * jnp.sin(angles)
        return carry

    query.send_y()
    out.send_h()
    key.send_l()
    lower.wait_g()
    key.pass_h_to_l()
    key.pass_h_to_y()
    query.send_h()
    query.send_l()
    key.pass_own_l_to_y()
    gate.wait_g()
    gate.send_h()
    gate.send_x()
    key.send_y()
    query.pass_h_to_l()
    upper.send_g()
    out.send_l()
    key.pass_l_to_y()
    lower.send_x()
    query.pass_h_to_y()
    query.pass_own_l_to_y()
    row.forward()
    lower.send_h()
    out.pass_h_to_l()
    query.pass_l_to_y()
    out.pass_h_to_y()
    upper.wait_g()
    upper.send_x()
    out.send_y()
    upper.send_h()
    lax.fori_loop(0, parts, label_part, 0)
    seg_row[...] = jnp.concatenate([part_seg[part] for part in range(parts)], axis=1)
    pos_row[...] = jnp.concatenate([part_pos[part] for part in range(parts)], axis=1)
    row.finish()
    query.finish()
    key.finish()
    stores = [mover.local(normed, normed_out), mover.local(full_qkv, qkv_out)]

    gain_query = gains[:, 2 * width : 2 * width + head]
    gain_key = gains[:, 2 * width + head : 2 * width + 2 * head]
    rotated = query_width + key_width
    tile = 2 * head

    def project(part, carry):
        spots = pl.ds(pl.multiple_of(part * tokens, tokens), tokens)
        source = normed[part]
        cos_part, sin_part = cosine[spots, :], sine[spots, :]
        for start in range(0, rotated + key_width, tile):
            result = jnp.dot(source, full_qkv[:, start : start + tile], preferred_element_type=F32)
            if start < rotated:
                lin[spots, start : start + tile] = result.astype(BF16)
                gain = gain_query if start < query_width else gain_key
                for inner in (0, head):
                    unit = norm_rows(result[:, inner : inner + head], gain)
                    turned = unit * cos_part + lane_swap(unit) * sin_part
                    rot[spots, start + inner : start + inner + head] = turned.astype(BF16)
            else:
                rot[spots, start : start + tile] = result.astype(BF16)
        return carry

    lax.fori_loop(0, parts, project, 0)
    stores += [mover.local(lin, lin_out), mover.local(rot, rot_out)]
    out.pass_own_l_to_y()
    gate.pass_h_to_x()
    scale = head ** (-0.5)
    for part in range(parts):
        keys = (part + 1) * tokens
        spots = pl.ds(part * tokens, tokens)
        allowed = (seg_col[spots, :] == seg_row[:, :keys]) & (pos_row[:, :keys] <= pos_col[spots, :])
        some = jnp.where(allowed, 0.0, MASKED)
        for copy in range(repeat):
            bias[copy * tokens : (copy + 1) * tokens, :keys] = some

        def attend(pair, carry):
            key_lanes = pl.ds(pl.multiple_of(query_width + pair * head, head), head)
            value_lanes = pl.ds(pl.multiple_of(rotated + pair * head, head), head)
            query_lanes = [
                pl.ds(pl.multiple_of((pair * repeat + copy) * head, head), head)
                for copy in range(repeat)
            ]
            queries = jnp.concatenate([rot[spots, lanes] for lanes in query_lanes], axis=0)
            scores = product(queries, rot[:keys, key_lanes], CONTRACT_COLS) * scale
            scores = scores + bias[:, :keys]
            peak = jnp.max(scores, axis=-1, keepdims=True)
            expd = jnp.exp(scores - peak)
            weight = jnp.sum(expd, axis=-1, keepdims=True)
            probs = (expd / weight).astype(BF16)
            log_total[pair, part] = peak + jnp.log(weight)
            context = jnp.dot(probs, rot[:keys, value_lanes], preferred_element_type=F32)
            for copy in range(repeat):
                attended[spots, query_lanes[copy]] = context[
                    copy * tokens : (copy + 1) * tokens
                ].astype(BF16)
            return carry

        lax.fori_loop(0, key_width // head, attend, 0)
        if part == 2:
            out.pass_l_to_y()
    out.finish()
    stores += [mover.local(full_wo, wo_out), mover.local(attended, attended_out)]

    def project_out(part, target):
        source = attended[pl.ds(pl.multiple_of(part * tokens, tokens), tokens), :]

        def step(index, carry):
            block = pl.ds(pl.multiple_of(index * 256, 256), 256)
            target[:, block] = product(source, full_wo[block, :], CONTRACT_COLS).astype(BF16)
            return carry

        lax.fori_loop(0, width // 256, step, 0)

    cores = place.cores
    places = ((1 - place.x) * cores, place.x * cores)
    project_out(places[0] + 1 - place.c, to_c.at[0])
    over_c = [mover.send(to_c.at[0], from_c.at[0], place.c_peer)]
    project_out(places[0] + place.c, part_own.at[0])
    over_c[0].wait_recv()
    add_rows(part_own.at[0], [part_own.at[0], from_c.at[0]], tokens, 32)
    over_x = mover.send(part_own.at[0], from_x, place.x_peer)
    project_out(places[1] + 1 - place.c, to_c.at[1])
    over_c.append(mover.send(to_c.at[1], from_c.at[1], place.c_peer))
    project_out(places[1] + place.c, part_own.at[1])
    lower.pass_h_to_x()
    over_c[1].wait_recv()
    over_x.wait_recv()

    def norm_resid(index, carry):
        rows = pl.ds(pl.multiple_of(index * 32, 32), 32)
        total = moved[rows, :].astype(F32) + part_own[1, rows, :].astype(F32)
        total = total + from_c[1, rows, :].astype(F32) + from_x[rows, :].astype(F32)
        resid[rows, :] = total
        nm_own[rows, :] = norm_rows(total, gains[:, width : 2 * width]).astype(BF16)
        return carry

    lax.fori_loop(0, tokens // 32, norm_resid, 0)
    group = GatherGroup(place, mover, nm_own, full_nm)
    upper.pass_h_to_x()
    group.forward()
    group.finish_ici()
    for part in (group, gate, upper, lower):
        part.finish()
    for copy in stores:
        copy.wait()
    mover.finish()


def forward(sizes, collective_id, head_size, args):
    dp_size, seq_size = sizes
    hidden, wq, wk, wo, wg = args[0], args[11], args[12], args[14], args[15]
    tokens, width = hidden.shape
    high = dp_size // GROUP
    rows = wq.shape[0]
    row_len = seq_size * tokens
    rotated = wq.shape[1] + wk.shape[1]
    inner = wg.shape[1] // 2
    group = (GROUP, seq_size // 2, tokens, width)
    heads = wq.shape[1] // head_size
    gain_width = 2 * (width + head_size)
    routes = dp_size * 16
    column, line = (row_len, 1), (1, row_len)
    outs = [
        ((tokens, width), BF16, VMEM),
        ((1, gain_width), F32, VMEM),
        ((seq_size, tokens, width), BF16, HBM),
        ((width, rotated + wk.shape[1]), BF16, HBM),
        ((width, wo.shape[1]), BF16, HBM),
        ((width, inner), BF16, HBM),
        ((width, inner), BF16, HBM),
        ((width, inner), BF16, HBM),
        ((tokens, width), BF16, VMEM),
        ((row_len, rotated), BF16, HBM),
        ((row_len, rotated + wk.shape[1]), BF16, HBM),
        ((row_len, wq.shape[1]), BF16, HBM),
        ((wk.shape[1] // head_size, seq_size, heads * head_size // wk.shape[1] * tokens, 1), F32, VMEM),
        ((tokens, width), F32, VMEM),
        (group, BF16, HBM),
        ((row_len, head_size), F32, VMEM),
        ((row_len, head_size), F32, VMEM),
        (column, jnp.int32, VMEM),
        (column, jnp.int32, VMEM),
        (line, jnp.int32, VMEM),
        (line, jnp.int32, VMEM),
        ((tokens, 1), F32, VMEM),
        ((tokens, 1), F32, VMEM),
        ((routes, tokens), BF16, VMEM),
        ((tokens, routes), BF16, VMEM),
    ]
    scratch = [
        pltpu.VMEM((dp_size, 16, width // GROUP), BF16),
        pltpu.VMEM((dp_size, 16, width // GROUP), BF16),
        pltpu.VMEM((dp_size, 1, gain_width), F32),
        pltpu.VMEM((1, gain_width), F32),
        pltpu.VMEM((seq_size, 1, tokens), jnp.int32),
        pltpu.VMEM((seq_size, 1, tokens), jnp.int32),
        pltpu.VMEM((tokens, width), BF16),
        pltpu.VMEM((wq.shape[1] // wk.shape[1] * tokens, row_len), F32),
        pltpu.VMEM((2, tokens, width), BF16),
        pltpu.VMEM((2, tokens, width), BF16),
        pltpu.VMEM((tokens, width), BF16),
        pltpu.VMEM((2, tokens, width), BF16),
        pltpu.VMEM((tokens, width), BF16),
    ]
    scratch += [
        pltpu.VMEM((seq_size, tokens, width), BF16),
        pltpu.VMEM((width, rotated + wk.shape[1]), BF16),
        pltpu.VMEM((width, wo.shape[1]), BF16),
        pltpu.VMEM((row_len, rotated), BF16),
        pltpu.VMEM((row_len, rotated + wk.shape[1]), BF16),
        pltpu.VMEM((row_len, wq.shape[1]), BF16),
    ]
    sends = 2 * (dp_size - 1) + 4 * (high + 1) + 9 * high
    sends += 3 * (3 + 2 * high) + 2 * GatherGroup.sends + GatherSeq.sends + 3
    return pl.pallas_call(
        functools.partial(forward_kernel, sizes),
        out_shape=[jax.ShapeDtypeStruct(shape, dtype) for shape, dtype, _ in outs],
        in_specs=[VMEM] * 11 + [HBM] * 7,
        out_specs=[spec for _, _, spec in outs],
        scratch_shapes=scratch + sems(sends, 24),
        compiler_params=comm_params(collective_id),
        name="forward_attention",
    )(*args)


class ScatterColumns:
    stage_rows = 512

    @staticmethod
    def scratch(high, rows, quarter):
        group_rows = GROUP * rows
        return [
            pltpu.VMEM((high * group_rows, quarter), BF16),
            pltpu.VMEM((max(high - 1, 1), group_rows, quarter), BF16),
            pltpu.VMEM((GROUP - 1, rows, quarter), BF16),
        ]

    def __init__(self, place, mover, parts, from_x, from_h, from_g, mine=None):
        self.place, self.mover, self.parts, self.mine = place, mover, parts, mine
        self.from_x, self.from_h, self.from_g = from_x, from_h, from_g
        self.group_rows, self.quarter = (from_h.shape[1:] if mine is None else mine.shape)

    def rows_of(self, step):
        high = lax.rem(self.place.h + step, self.place.high)
        return high * self.group_rows

    def start(self, steps):
        quarter = self.quarter
        for step in steps:
            rows = pl.ds(pl.multiple_of(self.rows_of(step), self.group_rows), self.group_rows)
            self.over_x[step] = self.mover.send(
                self.parts.at[rows, pl.ds(quarter, quarter)],
                self.from_x.at[rows],
                self.place.x_peer,
            )

    def start_far(self):
        self.over_x = {}
        self.start(range(1, self.place.high))

    def start_near(self):
        self.start((0,))

    def add_x(self, step, stage):
        mover, total = self.mover, self.from_x
        rows = stage.shape[1]
        base = self.rows_of(step)
        near = pl.ds(0, self.quarter)
        pieces = self.group_rows // rows

        def block(index):
            return pl.ds(pl.multiple_of(base + index * rows, rows), rows)

        def load(index):
            return mover.local(self.parts.at[block(index), near], stage.at[index % 2])

        copies = [load(0)]
        self.over_x[step].wait_recv()
        for index in range(pieces):
            if index + 1 < pieces:
                copies.append(load(index + 1))
            copies[index].wait()
            part = total.at[block(index)]
            add_rows(part, [part, stage.at[index % 2]], rows, 64)

    def forward_far(self, stage):
        place = self.place
        self.over_h = []
        for step in range(1, place.high):
            self.add_x(step, stage)
            block = pl.ds(pl.multiple_of(self.rows_of(step), self.group_rows), self.group_rows)
            self.over_h.append(
                self.mover.send(
                    self.from_x.at[block], self.from_h.at[step - 1], place.h_peer(step)
                )
            )

    def send_far(self, added):
        self.over_x, self.over_h = {}, []
        for step in range(1, self.place.high):
            rows = pl.ds(pl.multiple_of(self.rows_of(step), self.group_rows), self.group_rows)
            peer = self.place.h_peer(step)
            self.over_h.append(
                self.mover.send(added.at[rows], self.from_h.at[step - 1], peer)
            )

    def add_near(self, stage):
        self.add_x(0, stage)

    def merge(self):
        rows = pl.ds(pl.multiple_of(self.rows_of(0), self.group_rows), self.group_rows)
        self.mine = self.from_x.at[rows]
        for copy in self.over_h:
            copy.wait_recv()
        terms = [self.mine] + [self.from_h.at[step] for step in range(self.place.high - 1)]
        add_rows(self.mine, terms, self.group_rows, 64)

    def block(self, index):
        rows = self.group_rows // GROUP
        return self.mine.at[pl.ds(pl.multiple_of(index * rows, rows), rows)]

    def send_g(self):
        place = self.place
        self.over_g = []
        for step in (3, 1, 2):
            block = self.block(lax.rem(place.g + step, GROUP))
            copy = self.mover.send(block, self.from_g.at[step - 1], place.g_peer(step))
            self.over_g.append((step, copy))

    def finish(self, stage, out):
        place, quarter = self.place, self.quarter
        columns = pl.ds(pl.multiple_of(place.g * quarter, quarter), quarter)
        stage[:, columns] = self.block(place.g)[...].astype(F32)
        for step, copy in self.over_g:
            copy.wait_recv()
            source = lax.rem(place.g + GROUP - step, GROUP)
            columns = pl.ds(pl.multiple_of(source * quarter, quarter), quarter)
            stage[:, columns] = self.from_g[step - 1].astype(F32)
        if out is not None:
            self.mover.local(stage, out).wait()


class ScatterDp:
    @staticmethod
    def sends(high):
        return 2 * high + high + high - 1

    @staticmethod
    def scratch(high, rows, width):
        return [
            pltpu.VMEM((2, high, rows, width), BF16),
            pltpu.VMEM((high, rows, width), BF16),
            pltpu.VMEM((max(high - 1, 1), rows, width), BF16),
        ]

    def __init__(self, place, mover, parts, out, from_y, from_l, from_h):
        self.place, self.mover, self.parts, self.out = place, mover, parts, out
        self.from_y, self.from_l, self.from_h = from_y, from_l, from_h
        self.rows = out.shape[0]

    def block(self, high, l_index, y_index):
        index = high * GROUP + l_index * 2 + y_index
        return self.parts.at[pl.ds(pl.multiple_of(index * self.rows, self.rows), self.rows)]

    def start(self):
        place = self.place
        self.owners = (1 - place.l, place.l)
        self.over_y = []
        for index, l_owner in enumerate(self.owners):
            for high in range(place.high):
                source = self.block(high, l_owner, 1 - place.y)
                self.over_y.append(
                    self.mover.send(source, self.from_y.at[index, high], place.y_peer)
                )

    def ready(self, index, extra=None):
        place = self.place
        for high in range(place.high):
            self.over_y[index * place.high + high].wait_recv()
            mine = self.block(high, self.owners[index], place.y)
            terms = [mine, self.from_y.at[index, high]]
            if extra is not None:
                extra[high].wait_recv()
                terms.append(self.from_l.at[high])
            add_rows(mine, terms, self.rows, 32)

    def forward_y(self):
        place = self.place
        self.ready(0)
        self.over_l = []
        for high in range(place.high):
            source = self.block(high, 1 - place.l, place.y)
            self.over_l.append(self.mover.send(source, self.from_l.at[high], place.l_peer))

    def forward_l(self):
        place = self.place
        self.ready(1, self.over_l)
        self.over_h = []
        for step in range(1, place.high):
            source = self.block(lax.rem(place.h + step, place.high), place.l, place.y)
            self.over_h.append(
                self.mover.send(source, self.from_h.at[step - 1], place.h_peer(step))
            )

    def finish(self):
        place = self.place
        for copy in self.over_h:
            copy.wait_recv()
        terms = [self.block(place.h, place.l, place.y)]
        terms += [self.from_h.at[step] for step in range(place.high - 1)]
        add_rows(self.out, terms, self.rows, 32)


class ScatterGroup:
    sends = 10

    @staticmethod
    def scratch(rows, width):
        return [
            pltpu.VMEM((GROUP, rows, width), BF16),
            pltpu.VMEM((6, rows // 2, width), BF16),
        ]

    def __init__(self, place, mover, parts, from_c, landed):
        self.place, self.mover, self.parts = place, mover, parts
        self.from_c, self.landed = from_c, landed
        self.owners = (place.gd, place.gy, place.gl, place.g)
        self.over_c = []
        half = from_c.shape[1] // 2
        self.low, self.top = pl.ds(0, half), pl.ds(half, half)

    def start(self, index):
        place = self.place
        source = self.parts.at[self.owners[index], 1 - place.c]
        self.over_c.append(self.mover.send(source, self.from_c.at[index], place.c_peer))

    def forward(self, index):
        place, mover, sums, landed = self.place, self.mover, self.from_c, self.landed
        low, top = self.low, self.top
        self.over_c[index].wait_recv()
        total = sums.at[index]
        own = self.parts.at[self.owners[index], place.c]
        add_rows(total, [total, own], total.shape[0], 32)
        if index == 0:
            self.y_diag = mover.send(sums.at[0, low], landed.at[0], place.y_peer)
            self.l_diag = mover.send(sums.at[0, top], landed.at[1], place.l_peer)
        if index == 1:
            self.y_own = mover.send(sums.at[1, low], landed.at[2], place.y_peer)
        if index == 2:
            self.l_own = mover.send(sums.at[2, top], landed.at[3], place.l_peer)

    def forward_diag(self):
        place, mover, sums, landed = self.place, self.mover, self.from_c, self.landed
        half = sums.shape[1] // 2
        low, top = self.low, self.top
        self.y_diag.wait_recv()
        add_rows(sums.at[2, low], [sums.at[2, low], landed.at[0]], half, 32)
        self.l_last = mover.send(sums.at[2, low], landed.at[4], place.l_peer)
        self.l_diag.wait_recv()
        add_rows(sums.at[1, top], [sums.at[1, top], landed.at[1]], half, 32)
        self.y_last = mover.send(sums.at[1, top], landed.at[5], place.y_peer)

    def finish(self, take):
        half = self.from_c.shape[1] // 2
        chunk = 32
        self.y_own.wait_recv()
        self.l_last.wait_recv()
        self.l_own.wait_recv()
        self.y_last.wait_recv()
        for base, first, second in ((0, 2, 4), (half, 3, 5)):

            def step(index, carry):
                rows = pl.ds(pl.multiple_of(base + index * chunk, chunk), chunk)
                inner = pl.ds(pl.multiple_of(index * chunk, chunk), chunk)
                total = self.from_c[3, rows, :].astype(F32)
                total = total + self.landed[first, inner, :].astype(F32)
                take(rows, total + self.landed[second, inner, :].astype(F32))
                return carry

            lax.fori_loop(0, half // chunk, step, 0)


def norm_back(values, gain, cotangent):
    scale = lax.rsqrt(jnp.mean(values * values, axis=-1, keepdims=True) + NORM_EPS)
    weighted = cotangent * gain
    inner = jnp.mean(weighted * values, axis=-1, keepdims=True)
    unit = values * scale
    return scale * (weighted - unit * (scale * inner)), cotangent * unit


def feed_forward_kernel(sizes, *refs):
    nm_hbm, wg_hbm, wu_hbm, wd_hbm, grad_y, resid, live, gains = refs[:8]
    mixed, grad_resid, full_proj, gain_sum, part_gd, out_gd, out_gg, out_gu = refs[8:16]
    (nm, gy, wg, wu, wd, hidden, gate_grad, up_grad, part_nmlp, part_down, nmlp_c, nmlp_landed,
     down_c, down_landed, grad_proj, stage, column_stage, gd_from_x, gd_from_h) = refs[16:35]
    send_sems, recv_sems, local_sems = refs[35:]
    place = Place(*sizes)
    mover = Mover(send_sems, recv_sems, local_sems)
    tokens, width = resid.shape
    cores = place.cores
    block = cores * tokens
    inner = wg.shape[1]
    tile = 256
    loads = [mover.local(wg_hbm, wg), mover.local(wu_hbm, wu)]
    nm_loads = [mover.local(nm_hbm.at[index], nm.at[index]) for index in range(GROUP)]
    wd_load = mover.local(wd_hbm, wd)
    greet(
        [place.y_peer, place.l_peer, place.c_peer, place.x_peer]
        + [place.h_peer(step) for step in range(1, place.high)]
    )
    gather = GatherGroup(place, mover, grad_y, gy)
    gain_sum[...] = jnp.zeros_like(gain_sum)
    for copy in loads:
        copy.wait()

    def gate_up(index, carry):
        source = nm[index].reshape(block, width)
        rows = pl.ds(pl.multiple_of(index * block, block), block)
        for start in range(0, inner, tile):
            lanes = slice(start, start + tile)
            gate = jnp.dot(source, wg[:, lanes], preferred_element_type=F32)
            upper = jnp.dot(source, wu[:, lanes], preferred_element_type=F32)
            gain = 1.0 / (1.0 + jnp.exp(-gate))
            silu = gate * gain
            hidden[rows, lanes] = (silu * upper).astype(BF16)
            up_grad[rows, lanes] = silu.astype(BF16)
            gate_grad[rows, lanes] = (upper * (gain + silu * (1.0 - gain))).astype(BF16)
        return carry

    def weight_grads(source, grads, targets):
        copies = []
        count = len(grads)
        for index in range(width // tile):
            lanes = pl.ds(index * tile, tile)
            left = source[:, :, :, lanes].reshape(GROUP * block, tile)
            for which in range(count):
                slot = (index * count + which) % 2
                if len(copies) >= 2:
                    copies[-2].wait()
                stage[slot] = product(left, grads[which][...], CONTRACT_ROWS).astype(BF16)
                copies.append(mover.local(stage.at[slot], targets[which].at[lanes]))
        copies[-2].wait()
        copies[-1].wait()

    nm_loads[0].wait()
    nm_loads[1].wait()
    lax.fori_loop(0, 2, gate_up, 0)
    gather.forward()
    nm_loads[2].wait()
    nm_loads[3].wait()
    lax.fori_loop(2, GROUP, gate_up, 0)
    wd_load.wait()

    def down_block(owner):
        rows = pl.ds(pl.multiple_of(owner * block, block), block)

        def step(index, carry):
            lanes = pl.ds(pl.multiple_of(index * tile, tile), tile)
            result = product(hidden[rows, :], wd[lanes, :], CONTRACT_COLS).astype(BF16)
            part_down[owner, :, :, lanes] = result.reshape(cores, tokens, tile)
            return carry

        lax.fori_loop(0, width // tile, step, 0)

    down = ScatterGroup(place, mover, part_down, down_c, down_landed)
    for index in range(GROUP):
        down_block(down.owners[index])
        down.start(index)
    gather.finish_ici()
    gather.finish()
    lower = ScatterColumns(place, mover, part_gd, gd_from_x, gd_from_h, None)

    def back_block(owner):
        rows = pl.ds(pl.multiple_of(owner * block, block), block)
        source = gy[owner].reshape(block, width)
        for start in range(0, inner, tile):
            lanes = slice(start, start + tile)
            grad_mid = jnp.dot(source, wd[:, lanes], preferred_element_type=F32)
            gate_grad[rows, lanes] = (grad_mid * gate_grad[rows, lanes].astype(F32)).astype(BF16)
            up_grad[rows, lanes] = (grad_mid * up_grad[rows, lanes].astype(F32)).astype(BF16)

        def step(index, carry):
            lanes = pl.ds(pl.multiple_of(index * tile, tile), tile)
            result = product(gate_grad[rows, :], wg[lanes, :], CONTRACT_COLS)
            result = result + product(up_grad[rows, :], wu[lanes, :], CONTRACT_COLS)
            part_nmlp[owner, :, :, lanes] = result.astype(BF16).reshape(cores, tokens, tile)
            return carry

        lax.fori_loop(0, width // tile, step, 0)

    nmlp = ScatterGroup(place, mover, part_nmlp, nmlp_c, nmlp_landed)
    back_block(nmlp.owners[0])
    nmlp.start(0)
    back_block(nmlp.owners[1])
    nmlp.start(1)
    nmlp.forward(0)
    back_block(nmlp.owners[2])
    nmlp.start(2)
    nmlp.forward(1)
    nmlp.forward(2)
    weight_grads(gy, [hidden], [part_gd])
    lower.start_far()
    nmlp.forward_diag()
    back_block(nmlp.owners[3])
    nmlp.start(3)
    nmlp.forward(3)

    def back_mlp(rows, total):
        grad, terms = norm_back(resid[rows, :], gains[:, width : 2 * width], total)
        grad = grad + grad_y[rows, :].astype(F32)
        grad_resid[rows, :] = grad
        grad_proj[rows, :] = grad.astype(BF16)
        gain_sum[...] += jnp.sum(terms, axis=0, keepdims=True)

    def mix(rows, total):
        mixed[rows, :] = ((resid[rows, :] + total) * live[rows, :]).astype(BF16)

    nmlp.finish(back_mlp)
    row = GatherSeq(place, mover, grad_proj, full_proj)
    for index in range(GROUP):
        down.forward(index)
    weight_grads(nm, [gate_grad, up_grad], [out_gg, out_gu])
    row.forward()
    down.forward_diag()
    added = []
    for step in range(1, place.high):
        lower.add_x(step, column_stage)
        rows = pl.ds(pl.multiple_of(lower.rows_of(step), lower.group_rows), lower.group_rows)
        added.append(mover.local(gd_from_x.at[rows], out_gd.at[rows]))
    down.finish(mix)
    row.finish()
    for copy in added:
        copy.wait()
    mover.finish()


def feed_forward(sizes, collective_id, args):
    dp_size, seq_size = sizes
    nm, wg, resid, gains = args[0], args[1], args[5], args[7]
    tokens, width = resid.shape
    inner = wg.shape[1]
    high = dp_size // GROUP
    piece = min(width // high, ScatterColumns.stage_rows)
    rows = GROUP * (seq_size // 2) * tokens
    outs = [
        ((tokens, width), BF16, VMEM),
        ((tokens, width), F32, VMEM),
        ((seq_size, tokens, width), BF16, HBM),
        ((1, width), F32, VMEM),
        ((width, inner), BF16, HBM),
        ((width, inner // 2), BF16, HBM),
        ((width, inner), BF16, HBM),
        ((width, inner), BF16, HBM),
    ]
    scratch = [pltpu.VMEM(nm.shape, BF16)] * 2
    scratch += [pltpu.VMEM((width, inner), BF16)] * 3
    scratch += [pltpu.VMEM((rows, inner), BF16)] * 3
    scratch += [pltpu.VMEM(nm.shape, BF16)] * 2
    scratch += ScatterGroup.scratch(tokens, width) * 2
    scratch += [pltpu.VMEM((tokens, width), BF16), pltpu.VMEM((2, 256, inner), BF16)]
    scratch += [pltpu.VMEM((2, piece, inner // 2), BF16)]
    scratch += ScatterColumns.scratch(high, width // dp_size, inner // 2)[:2]
    sends = 3 * 10 + GatherSeq.sends + 2 * high
    local = 10 + 3 * (width // 256) + high * (width // high // piece)
    return pl.pallas_call(
        functools.partial(feed_forward_kernel, sizes),
        out_shape=[jax.ShapeDtypeStruct(shape, dtype) for shape, dtype, _ in outs],
        in_specs=[HBM] * 4 + [VMEM] * 4,
        out_specs=[spec for _, _, spec in outs],
        scratch_shapes=scratch + sems(sends, local),
        compiler_params=comm_params(collective_id, 63 * 1024 * 1024),
        name="feed_forward",
    )(*args)


def backward_kernel(sizes, *refs):
    part_gg, part_gu, part_gd, gd_far = refs[:4]
    moved, keep, gain_mlp, gains, cosine, sine = refs[12:18]
    seg_col, pos_col, seg_row, pos_row, log_row, recv_map, send_map = refs[18:25]
    grad_hidden, gain_sums, out_gd, out_gg, out_gu, out_q, out_k, out_v, out_wo = refs[25:34]
    send_sems, recv_sems, local_sems = refs[-3:]
    scratch = list(refs[34:-3])

    def take(count):
        taken = scratch[:count]
        del scratch[:count]
        return taken

    place = Place(*sizes)
    mover = Mover(send_sems, recv_sems, local_sems)
    tokens, width = moved.shape
    parts = sizes[1]
    head = cosine.shape[1]
    query_width = refs[6].shape[1]
    key_width = (refs[7].shape[1] - query_width) // 2
    rotated = query_width + key_width
    columns = width // GROUP
    repeat = query_width // key_width
    column_stage, out_stage = take(2)
    grad_wo, grad_key, grad_query = take(3)
    loaded = take(8)
    wo, full_proj, attended, rot, lin, normed, full_qkv, grad_resid = loaded
    lower = ScatterColumns(place, mover, part_gd, *take(3))
    gate = ScatterColumns(place, mover, part_gg, *take(3))
    upper = ScatterColumns(place, mover, part_gu, *take(3))
    wo_total, key_total = take(2)
    wo_sum = ScatterDp(place, mover, grad_wo, wo_total, *take(3))
    key_sum = ScatterDp(place, mover, grad_key, key_total, *take(3))
    query_sum = ScatterDp(place, mover, grad_query, out_q, *take(3))
    grad_moved, to_c, from_c, from_x = take(4)
    grad_att, grad_keys, grad_values, grad_lin, bias = take(5)
    blocks_out, blocks_in, rows_in, row_c, row_x = take(5)

    loads = [mover.local(source, target) for source, target in zip(refs[4:12], loaded)]
    greet(dp_peers(place) + [place.x_peer, place.c_peer])
    gain_sums[...] = jnp.zeros_like(gain_sums)
    gain_sums[:, width : 2 * width] = gain_mlp[...]
    grad_keys[...] = jnp.zeros_like(grad_keys)
    grad_values[...] = jnp.zeros_like(grad_values)

    def attended_grad(part, carry):
        spots = pl.ds(pl.multiple_of(part * tokens, tokens), tokens)
        for start in range(0, query_width, 256):
            result = jnp.dot(full_proj[part], wo[:, start : start + 256], preferred_element_type=F32)
            grad_att[spots, start : start + 256] = result.astype(BF16)
        return carry


    def out_weight_grad(index, carry):
        lanes = pl.ds(pl.multiple_of(index * 256, 256), 256)
        source = full_proj[:, :, lanes].reshape(parts * tokens, 256)
        grad_wo[lanes, :] = product(source, attended[...], CONTRACT_ROWS).astype(BF16)
        return carry

    scale = head ** (-0.5)
    gain_query = gains[:, 2 * width : 2 * width + head]
    gain_key = gains[:, 2 * width + head : 2 * width + 2 * head]

    def unrotate(spots, lanes, grad, gain, gain_lanes):
        turned = grad * cosine[spots, :] - lane_swap(grad) * sine[spots, :]
        values, terms = norm_back(lin[spots, lanes].astype(F32), gain, turned)
        grad_lin[spots, lanes] = values.astype(BF16)
        gain_sums[:, gain_lanes] += jnp.sum(terms, axis=0, keepdims=True)

    def attention_part(part):
        keys = (part + 1) * tokens
        spots = pl.ds(part * tokens, tokens)
        allowed = (seg_col[:keys, :] == seg_row[:, spots]) & (pos_col[:keys, :] <= pos_row[:, spots])
        some = jnp.where(allowed, 0.0, MASKED)
        for copy in range(repeat):
            bias[:keys, copy * tokens : (copy + 1) * tokens] = some

        def attend(pair, carry):
            key_lanes = pl.ds(pl.multiple_of(query_width + pair * head, head), head)
            value_lanes = pl.ds(pl.multiple_of(rotated + pair * head, head), head)
            own_lanes = pl.ds(pl.multiple_of(pair * head, head), head)
            query_lanes = [
                pl.ds(pl.multiple_of((pair * repeat + copy) * head, head), head)
                for copy in range(repeat)
            ]
            queries = jnp.concatenate([rot[spots, lanes] for lanes in query_lanes], axis=0)
            grads = jnp.concatenate([grad_att[spots, lanes] for lanes in query_lanes], axis=0)
            key_rows, value_rows = rot[:keys, key_lanes], rot[:keys, value_lanes]
            scores = product(key_rows, queries, CONTRACT_COLS) * scale + bias[:keys, :]
            probs = jnp.exp(scores - log_row[pair, part])
            grad_values[:keys, own_lanes] += jnp.dot(
                probs.astype(BF16), grads, preferred_element_type=F32
            )
            grad_probs = product(value_rows, grads, CONTRACT_COLS)
            spread = jnp.sum(probs * grad_probs, axis=0, keepdims=True)
            grad_scores = (probs * (grad_probs - spread)).astype(BF16)
            grad_keys[:keys, own_lanes] += jnp.dot(
                grad_scores, queries, preferred_element_type=F32
            )
            grad_queries = product(grad_scores, key_rows, CONTRACT_ROWS) * scale
            for copy in range(repeat):
                unrotate(
                    spots,
                    query_lanes[copy],
                    grad_queries[copy * tokens : (copy + 1) * tokens],
                    gain_query,
                    pl.ds(2 * width, head),
                )
            return carry

        lax.fori_loop(0, key_width // head, attend, 0)

    def back_all_keys():
        for pair in range(key_width // head):

            def back_keys(part, carry):
                spots = pl.ds(pl.multiple_of(part * tokens, tokens), tokens)
                lanes = pl.ds(pair * head, head)
                unrotate(
                    spots,
                    pl.ds(query_width + pair * head, head),
                    grad_keys[spots, lanes] * scale,
                    gain_key,
                    pl.ds(2 * width + head, head),
                )
                grad_lin[spots, pl.ds(rotated + pair * head, head)] = grad_values[spots, lanes].astype(
                    BF16
                )
                return carry

            lax.fori_loop(0, parts, back_keys, 0)

    def weight_grad(target, start, size):
        def step(index, carry):
            lanes = pl.ds(pl.multiple_of(index * 256, 256), 256)
            source = normed[:, :, lanes].reshape(parts * tokens, 256)
            target[lanes, :] = product(
                source, grad_lin[:, start : start + size], CONTRACT_ROWS
            ).astype(BF16)
            return carry

        lax.fori_loop(0, width // 256, step, 0)

    def normed_grad(part, target):
        source = grad_lin[pl.ds(pl.multiple_of(part * tokens, tokens), tokens), :]

        def step(index, carry):
            block = pl.ds(pl.multiple_of(index * 256, 256), 256)
            target[:, block] = product(source, full_qkv[block, :], CONTRACT_COLS).astype(BF16)
            return carry

        lax.fori_loop(0, width // 256, step, 0)

    cores = place.cores
    places = ((1 - place.x) * cores, place.x * cores)
    over = {}

    def send_other_row():
        normed_grad(places[0] + 1 - place.c, to_c.at[0])
        first = mover.send(to_c.at[0], from_c.at[0], place.c_peer)
        normed_grad(places[0] + place.c, to_c.at[1])
        first.wait_recv()
        add_rows(to_c.at[1], [to_c.at[1], from_c.at[0]], tokens, 32)
        over["x"] = mover.send(to_c.at[1], from_x, place.x_peer)

    def send_own_row():
        normed_grad(places[1] + 1 - place.c, to_c.at[2])
        over["c"] = mover.send(to_c.at[2], from_c.at[1], place.c_peer)
        normed_grad(places[1] + place.c, to_c.at[3])

    def back_normed(index, carry):
        rows = pl.ds(pl.multiple_of(index * 32, 32), 32)
        total = to_c[3, rows, :].astype(F32) + from_c[1, rows, :].astype(F32)
        total = total + from_x[rows, :].astype(F32)
        grad, terms = norm_back(moved[rows, :].astype(F32), gains[:, :width], total)
        grad_moved[rows, :] = (grad_resid[rows, :] + grad).astype(BF16)
        gain_sums[:, :width] += jnp.sum(terms, axis=0, keepdims=True)
        return carry

    piece_row = index_of((place.dp_size * 16, 1), 0) & 3
    copies = []

    def finish_row():
        over["c"].wait_recv()
        over["x"].wait_recv()
        lax.fori_loop(0, tokens // 32, back_normed, 0)
        for q in range(GROUP):
            lanes = pl.ds(q * columns, columns)
            piece = product(recv_map[...], grad_moved[:, lanes], CONTRACT_ROWS)
            piece = jnp.where(piece_row == q, piece, 0.0)
            total = piece if q == 0 else total + piece
        blocks_out[...] = total.astype(BF16).reshape(blocks_out.shape)
        for step in range(1, place.dp_size):
            other = lax.rem(place.d + step, place.dp_size)
            copies.append(mover.send(blocks_out.at[other], blocks_in.at[place.d], (other, place.s)))
            copies.append(mover.send(gain_sums, rows_in.at[place.d], (other, place.s)))
        blocks_in[place.d] = blocks_out[place.d]
        rows_in[place.d] = gain_sums[...]

    def finish_hidden():
        for copy in copies:
            copy.wait_recv()
        row_total = rows_in[0]
        for index in range(1, place.dp_size):
            row_total = row_total + rows_in[index]
        row_c[0] = row_total
        over["gc"] = mover.send(row_c.at[0], row_c.at[1], place.c_peer)
        returned = blocks_in[...].reshape(place.dp_size * 16, columns)
        for q in range(GROUP):
            lanes = pl.ds(q * columns, columns)
            chosen = jnp.where(piece_row == q, returned, jnp.zeros_like(returned))
            here = product(send_map[...], chosen, CONTRACT_ROWS)
            here = here + jnp.where(keep[...] > 0.0, grad_moved[:, lanes].astype(F32), 0.0)
            grad_hidden[:, lanes] = here.astype(BF16)

    def pass_gains():
        over["gc"].wait_recv()
        row_x[0] = row_c[0] + row_c[1]
        over["gx"] = mover.send(row_x.at[0], row_x.at[1], place.x_peer)

    lower.send_far(gd_far)
    for copy in loads[:2]:
        copy.wait()
    lax.fori_loop(0, parts, attended_grad, 0)
    for copy in loads[2:5]:
        copy.wait()
    gate.start_far()
    upper.start_far()
    lax.fori_loop(0, width // 256, out_weight_grad, 0)
    wo_sum.start()
    attention_part(0)
    attention_part(1)
    attention_part(2)
    lower.start_near()
    for part in range(3, parts):
        attention_part(part)
    gate.start_near()
    gate.forward_far(column_stage)
    back_all_keys()
    wo_sum.forward_y()
    for copy in loads[5:]:
        copy.wait()
    weight_grad(grad_query, 0, query_width)
    query_sum.start()
    query_sum.forward_y()
    send_other_row()
    wo_sum.forward_l()
    lower.add_near(column_stage)
    upper.forward_far(column_stage)
    weight_grad(grad_key, query_width, 2 * key_width)
    upper.start_near()
    key_sum.start()
    lower.merge()
    lower.send_g()
    key_sum.forward_y()
    key_sum.forward_l()
    gate.add_near(column_stage)
    gate.merge()
    gate.send_g()
    lower.finish(out_stage, None)
    out_gd[...] = out_stage[...].T
    upper.add_near(column_stage)
    wo_sum.finish()
    out_wo[...] = wo_total[...].T
    send_own_row()
    finish_row()
    upper.merge()
    upper.send_g()
    query_sum.forward_l()
    key_sum.finish()
    out_k[...] = key_total[:, :key_width]
    out_v[...] = key_total[:, key_width:]
    finish_hidden()
    pass_gains()
    gate.finish(out_stage, out_gg)
    upper.finish(out_stage, out_gu)
    query_sum.finish()
    over["gx"].wait_recv()
    mover.finish()
    gain_sums[...] = row_x[0] + row_x[1]


def backward(sizes, collective_id, args):
    dp_size, seq_size = sizes
    part_gg, attended, rot, moved, gains = args[0], args[6], args[7], args[12], args[15]
    tokens, width = moved.shape
    high = dp_size // GROUP
    rows = width // dp_size
    quarter = part_gg.shape[1] // 2
    row_len = seq_size * tokens
    query_width = attended.shape[1]
    key_width = (rot.shape[1] - query_width) // 2
    repeat = query_width // key_width
    outs = [
        ((tokens, width), BF16, VMEM),
        (gains.shape, F32, VMEM),
        ((GROUP * quarter, rows), F32, VMEM),
        ((rows, GROUP * quarter), F32, HBM),
        ((rows, GROUP * quarter), F32, HBM),
        ((rows, query_width), F32, VMEM),
        ((rows, key_width), F32, VMEM),
        ((rows, key_width), F32, VMEM),
        ((query_width, rows), F32, VMEM),
    ]
    piece = min(GROUP * rows, ScatterColumns.stage_rows)
    scratch = [
        pltpu.VMEM((2, piece, quarter), BF16),
        pltpu.VMEM((rows, GROUP * quarter), F32),
    ]
    scratch += [
        pltpu.VMEM((width, query_width), BF16),
        pltpu.VMEM((width, 2 * key_width), BF16),
        pltpu.VMEM((width, query_width), BF16),
    ]
    scratch += [pltpu.VMEM(array.shape, array.dtype) for array in args[4:12]]
    for _ in range(3):
        scratch += ScatterColumns.scratch(high, rows, quarter)
    scratch += [
        pltpu.VMEM((rows, query_width), F32),
        pltpu.VMEM((rows, 2 * key_width), F32),
    ]
    scratch += ScatterDp.scratch(high, rows, query_width)
    scratch += ScatterDp.scratch(high, rows, 2 * key_width)
    scratch += ScatterDp.scratch(high, rows, query_width)
    scratch += [
        pltpu.VMEM((tokens, width), BF16),
        pltpu.VMEM((seq_size, tokens, width), BF16),
        pltpu.VMEM((2, tokens, width), BF16),
        pltpu.VMEM((tokens, width), BF16),
        pltpu.VMEM((row_len, query_width), BF16),
        pltpu.VMEM((row_len, key_width), F32),
        pltpu.VMEM((row_len, key_width), F32),
        pltpu.VMEM((row_len, rot.shape[1]), BF16),
        pltpu.VMEM((row_len, repeat * tokens), F32),
        pltpu.VMEM((dp_size, 16, width // GROUP), BF16),
        pltpu.VMEM((dp_size, 16, width // GROUP), BF16),
        pltpu.VMEM((dp_size,) + gains.shape, F32),
        pltpu.VMEM((2,) + gains.shape, F32),
        pltpu.VMEM((2,) + gains.shape, F32),
    ]
    sends = 3 * (2 * high + 2) + 3 * ScatterDp.sends(high)
    sends += 3 + 2 * (dp_size - 1) + 2
    local = 3 * (high * GROUP * rows // piece + 1) + 9
    return pl.pallas_call(
        functools.partial(backward_kernel, sizes),
        out_shape=[jax.ShapeDtypeStruct(shape, dtype) for shape, dtype, _ in outs],
        in_specs=[HBM] * 12 + [VMEM] * 13,
        out_specs=[spec for _, _, spec in outs],
        scratch_shapes=scratch + sems(sends, local),
        compiler_params=comm_params(collective_id, 63 * 1024 * 1024),
        name="backward_attention",
    )(*args)


def hand_over_kernel(count, *refs):
    held = refs[2 * count : 3 * count]
    sems_in, sems_out = refs[3 * count :]
    loads = [
        pltpu.make_async_copy(refs[index], held[index], sems_in.at[index])
        for index in range(count)
    ]
    stores = [
        pltpu.make_async_copy(held[index], refs[count + index], sems_out.at[index])
        for index in range(count)
    ]
    for copy in loads:
        copy.start()
    for load, store in zip(loads, stores):
        load.wait()
        store.start()
    for copy in stores:
        copy.wait()


def hand_over(arrays):
    count = len(arrays)
    return pl.pallas_call(
        functools.partial(hand_over_kernel, count),
        out_shape=[jax.ShapeDtypeStruct(array.shape, array.dtype) for array in arrays],
        in_specs=[HBM] * count,
        out_specs=[HBM] * count,
        scratch_shapes=[pltpu.VMEM(array.shape, array.dtype) for array in arrays]
        + [pltpu.SemaphoreType.DMA((count,)), pltpu.SemaphoreType.DMA((count,))],
        compiler_params=pltpu.CompilerParams(vmem_limit_bytes=62 * 1024 * 1024),
        name="hand_over",
    )(*arrays)


def per_device(
    sizes,
    hidden_in,
    valid_len,
    doc_lengths,
    doc_perm,
    attn_norm,
    w_query,
    key_weight,
    value_weight,
    w_out,
    query_norm,
    key_norm_gain,
    mlp_norm,
    w_gate,
    w_up,
    w_down,
    out_grad,
):
    model_width = hidden_in.shape[1]
    seq_count, row_count, _ = doc_lengths.shape
    my_row = lax.axis_index("dp")
    my_part = lax.axis_index("seq")
    head_size = query_norm.shape[0] * row_count
    lengths = doc_lengths.reshape(seq_count, -1)
    (
        moved_low,
        gains,
        normed,
        qkv_mat,
        out_mat,
        gate_mat,
        up_mat,
        down_mat,
        grad_y_own,
        rotated_lin,
        rotated_all,
        attended,
        log_total,
        resid_rows,
        normed_mlp,
        cosine,
        sine,
        seg_col,
        pos_col,
        seg_row,
        pos_row,
        keep,
        live,
        send_map,
        recv_map,
    ) = forward(
        sizes,
        1,
        head_size,
        (
            hidden_in,
            valid_len[None, :],
            lengths[:, None, :],
            doc_perm[:, None, :],
            lengths[:, :, None],
            doc_perm[:, :, None],
            attn_norm[None, :],
            mlp_norm[None, :],
            query_norm[None, :],
            key_norm_gain[None, :],
            out_grad,
            w_query,
            key_weight,
            value_weight,
            w_out.T,
            w_gate,
            w_up,
            w_down.T,
        ),
    )
    cuts = (model_width, 2 * model_width, 2 * model_width + head_size)
    mixed, grad_resid, grad_proj, gain_mlp_sum, part_down, grad_down, grad_gate, grad_up = feed_forward(
        sizes,
        2,
        (normed_mlp, gate_mat, up_mat, down_mat, grad_y_own, resid_rows, live, gains),
    )
    (
        grad_hidden,
        gain_sums,
        out_down,
        out_gate,
        out_up,
        out_query,
        out_key,
        out_value,
        out_wo,
    ) = backward(
        sizes,
        3,
        (
            grad_gate,
            grad_up,
            part_down,
            grad_down,
            out_mat,
            grad_proj,
            attended,
            rotated_all,
            rotated_lin,
            normed,
            qkv_mat,
            grad_resid,
            moved_low,
            keep,
            gain_mlp_sum,
            gains,
            cosine,
            sine,
            seg_col,
            pos_col,
            seg_row,
            pos_row,
            jnp.swapaxes(log_total, 2, 3),
            recv_map,
            send_map,
        ),
    )
    device = my_row * seq_count + my_part

    def own_piece(vector):
        size = vector.shape[0] // (row_count * seq_count)
        return lax.dynamic_slice_in_dim(vector, device * size, size)

    sum_attn, sum_mlp, sum_query, sum_key = [own_piece(v) for v in jnp.split(gain_sums[0], cuts)]
    (
        mixed,
        grad_hidden,
        out_query,
        out_key,
        out_value,
        out_wo,
        out_gate,
        out_up,
        out_down,
    ) = hand_over(
        (
            mixed,
            grad_hidden,
            out_query,
            out_key,
            out_value,
            out_wo,
            out_gate,
            out_up,
            out_down,
        )
    )
    return (
        mixed,
        grad_hidden,
        sum_attn,
        out_query,
        out_key,
        out_value,
        out_wo,
        sum_query,
        sum_key,
        sum_mlp,
        out_gate,
        out_up,
        out_down,
    )


def solution(mesh):
    in_specs = (
        P(("dp", "seq"), None),
        P(),
        P(),
        P(),
        P("dp"),
        P("dp", "seq"),
        P("dp", "seq"),
        P("dp", "seq"),
        P("seq", "dp"),
        P("dp"),
        P("dp"),
        P("dp"),
        P("dp", "seq"),
        P("dp", "seq"),
        P("seq", "dp"),
        P(("dp", "seq"), None),
    )
    out_specs = (
        P(("dp", "seq"), None),
        P(("dp", "seq"), None),
        P(("dp", "seq")),
        P("dp", "seq"),
        P("dp", "seq"),
        P("dp", "seq"),
        P("seq", "dp"),
        P(("dp", "seq")),
        P(("dp", "seq")),
        P(("dp", "seq")),
        P("dp", "seq"),
        P("dp", "seq"),
        P("seq", "dp"),
    )
    return jax.shard_map(
        functools.partial(per_device, (mesh.shape["dp"], mesh.shape["seq"])), mesh=mesh, in_specs=in_specs, out_specs=out_specs, check_vma=False
    )
```

```python
import functools
import math

import jax
import jax.numpy as jnp
from jax import lax
from jax.experimental import pallas as pl
from jax.experimental.pallas import tpu as pltpu
from jax.sharding import PartitionSpec as P

MAXSHORT = 4
GROUP = 4
MESH = pl.DeviceIdType.MESH
HBM = pl.BlockSpec(memory_space=pltpu.HBM)
VMEM = pl.BlockSpec(memory_space=pltpu.VMEM)
BF16 = jnp.bfloat16
F32 = jnp.float32


NORM_EPS = 1e-06
ROPE_BASE = 1000000.0
MASKED = -1e30
CONTRACT_ROWS = (((0,), (0,)), ((), ()))
CONTRACT_COLS = (((1,), (1,)), ((), ()))


def product(left, right, dims):
    return lax.dot_general(left, right, dims, preferred_element_type=jnp.float32)


class Place:
    def __init__(self, dp_size, seq_size):
        self.dp_size = dp_size
        self.seq_size = seq_size
        self.high = dp_size // GROUP
        self.cores = seq_size // 2
        self.d = lax.axis_index("dp")
        self.s = lax.axis_index("seq")
        self.g = lax.rem(self.d, GROUP)
        self.h = lax.div(self.d, GROUP)
        self.x = lax.div(self.s, self.cores)
        self.c = lax.rem(self.s, self.cores)
        self.y = lax.rem(self.g, 2)
        self.l = lax.div(self.g, 2)
        self.gy = self.g + 1 - 2 * self.y
        self.gl = lax.rem(self.g + 2, GROUP)
        self.gd = 3 - self.g
        self.y_peer = (self.h * GROUP + self.gy, self.s)
        self.l_peer = (self.h * GROUP + self.gl, self.s)
        self.d_peer = (self.h * GROUP + self.gd, self.s)
        self.x_peer = (self.d, (1 - self.x) * self.cores + self.c)
        self.c_peer = (self.d, self.x * self.cores + 1 - self.c)

    def h_peer(self, step):
        return (lax.rem(self.h + step, self.high) * GROUP + self.g, self.s)

    def h_from(self, step):
        return lax.rem(self.h + self.high - step, self.high)

    def g_peer(self, step):
        return (self.h * GROUP + lax.rem(self.g + step, GROUP), self.s)


class Mover:
    def __init__(self, send_sems, recv_sems, local_sems):
        self.send_sems = send_sems
        self.recv_sems = recv_sems
        self.local_sems = local_sems
        self.count = 0
        self.local_count = 0
        self.sent = []

    def send(self, source, target, device):
        index = self.count
        self.count += 1
        copy = pltpu.make_async_remote_copy(
            src_ref=source,
            dst_ref=target,
            send_sem=self.send_sems.at[index],
            recv_sem=self.recv_sems.at[index],
            device_id=device,
            device_id_type=MESH,
        )
        copy.start()
        self.sent.append(copy)
        return copy

    def local(self, source, target):
        index = self.local_count
        self.local_count += 1
        copy = pltpu.make_async_copy(source, target, self.local_sems.at[index])
        copy.start()
        return copy

    def drain(self, copy):
        copy.wait_send()
        self.sent = [other for other in self.sent if other is not copy]

    def finish(self):
        for copy in self.sent:
            copy.wait_send()


def greet(peers):
    barrier = pltpu.get_barrier_semaphore()
    for peer in peers:
        pl.semaphore_signal(barrier, inc=1, device_id=peer, device_id_type=MESH)
    pl.semaphore_wait(barrier, len(peers))


def dp_peers(place):
    return [
        (lax.rem(place.d + step, place.dp_size), place.s) for step in range(1, place.dp_size)
    ]


def sems(count, local):
    return [
        pltpu.SemaphoreType.DMA((count,)),
        pltpu.SemaphoreType.DMA((count,)),
        pltpu.SemaphoreType.DMA((max(local, 1),)),
    ]


def comm_params(collective_id, vmem=None):
    return pltpu.CompilerParams(
        collective_id=collective_id,
        has_side_effects=True,
        vmem_limit_bytes=vmem if vmem is not None else 60 * 1024 * 1024,
    )


def add_rows(target, terms, rows, chunk):
    def step(index, carry):
        part = pl.ds(pl.multiple_of(index * chunk, chunk), chunk)
        total = terms[0][part, :].astype(F32)
        for term in terms[1:]:
            total = total + term[part, :].astype(F32)
        target[part, :] = total.astype(target.dtype)
        return carry

    lax.fori_loop(0, rows // chunk, step, 0)


class GatherSeq:
    sends = 3

    def __init__(self, place, mover, own, full):
        self.place, self.mover, self.full = place, mover, full
        self.local = mover.local(own, full.at[place.s])
        self.over_x = mover.send(own, full.at[place.s], place.x_peer)
        self.over_c = mover.send(own, full.at[place.s], place.c_peer)

    def forward(self):
        self.over_x.wait_recv()
        block = self.full.at[self.place.x_peer[1]]
        self.passed = self.mover.send(block, block, self.place.c_peer)

    def finish(self):
        self.local.wait()
        self.over_c.wait_recv()
        self.passed.wait_recv()


class GatherGroup:
    sends = 10

    def __init__(self, place, mover, own, full):
        self.place, self.mover, self.full = place, mover, full
        half = own.shape[0] // 2
        self.low, self.top = pl.ds(0, half), pl.ds(half, half)
        self.local = mover.local(own, full.at[place.g, place.c])
        spot = full.at[place.g, place.c]
        self.y_low = mover.send(own.at[self.low], spot.at[self.low], place.y_peer)
        self.l_top = mover.send(own.at[self.top], spot.at[self.top], place.l_peer)
        self.y_top = mover.send(own.at[self.top], spot.at[self.top], place.y_peer)
        self.l_low = mover.send(own.at[self.low], spot.at[self.low], place.l_peer)
        self.core = [mover.send(own, spot, place.c_peer)]

    def forward(self):
        place, mover, full = self.place, self.mover, self.full
        self.y_low.wait_recv()
        part = full.at[place.gy, place.c, self.low]
        self.d_low = mover.send(part, part, place.l_peer)
        self.l_top.wait_recv()
        part = full.at[place.gl, place.c, self.top]
        self.d_top = mover.send(part, part, place.y_peer)
        self.y_top.wait_recv()
        part = full.at[place.gy, place.c]
        self.core.append(mover.send(part, part, place.c_peer))
        self.l_low.wait_recv()
        part = full.at[place.gl, place.c]
        self.core.append(mover.send(part, part, place.c_peer))

    def finish_ici(self):
        place = self.place
        self.d_low.wait_recv()
        self.d_top.wait_recv()
        part = self.full.at[place.gd, place.c]
        self.core.append(self.mover.send(part, part, place.c_peer))

    def finish(self):
        self.local.wait()
        for copy in self.core:
            copy.wait_recv()


class GatherDp:
    def __init__(self, place, mover, pieces, full):
        self.place, self.mover, self.full, self.pieces = place, mover, full, pieces
        first, last = pieces[0], pieces[-1]
        self.window = pl.ds(first[1], last[1] + last[2] - first[1])
        self.rows = full.shape[0] // place.dp_size
        own_rows = self.block(place.d)
        self.spots = [full.at[own_rows, pl.ds(start, size)] for _, start, size in pieces]
        self.local = [
            mover.local(piece[0], spot) for piece, spot in zip(pieces, self.spots)
        ]
        self.over_y, self.passed_l = [], []

    def block(self, index):
        return pl.ds(pl.multiple_of(index * self.rows, self.rows), self.rows)

    def own_to(self, peer):
        return [
            self.mover.send(piece[0], spot, peer) for piece, spot in zip(self.pieces, self.spots)
        ]

    def send_h(self):
        place = self.place
        self.over_h = [self.own_to(place.h_peer(step)) for step in range(1, place.high)]

    def send_l(self):
        self.own_l = self.own_to(self.place.l_peer)

    def send_y(self):
        self.over_y += self.own_to(self.place.y_peer)

    def part(self, high, index):
        return self.full.at[self.block(high * GROUP + index), self.window]

    def pass_h_to_l(self):
        place = self.place
        for step, copies in enumerate(self.over_h, 1):
            for copy in copies:
                copy.wait_recv()
            part = self.part(place.h_from(step), place.g)
            self.passed_l.append(self.mover.send(part, part, place.l_peer))

    def pass_h_to_y(self):
        place = self.place
        for step in range(1, place.high):
            part = self.part(place.h_from(step), place.g)
            self.over_y.append(self.mover.send(part, part, place.y_peer))

    def pass_own_l_to_y(self):
        place = self.place
        for copy in self.own_l:
            copy.wait_recv()
        part = self.part(place.h, place.gl)
        self.over_y.append(self.mover.send(part, part, place.y_peer))

    def pass_l_to_y(self):
        place = self.place
        for step, copy in enumerate(self.passed_l, 1):
            copy.wait_recv()
            part = self.part(place.h_from(step), place.gl)
            self.over_y.append(self.mover.send(part, part, place.y_peer))

    def finish(self):
        for copy in self.local:
            copy.wait()
        for copy in self.over_y:
            copy.wait_recv()


class GatherColumns:
    def __init__(self, place, mover, own, full):
        self.place, self.mover, self.full, self.own = place, mover, full, own
        self.quarter = own.shape[1] // GROUP
        self.rows = own.shape[0]
        self.near = pl.ds(0, self.quarter)
        self.far = pl.ds(self.quarter, self.quarter)

    def block(self, high):
        rows = GROUP * self.rows
        return pl.ds(pl.multiple_of(high * rows, rows), rows)

    def send_g(self, spot=None):
        place, mover, own = self.place, self.mover, self.own
        if spot is None:
            spot = self.full.at[
                pl.ds(pl.multiple_of(place.d * self.rows, self.rows), self.rows), self.near
            ]
        self.over_g = []
        for step in (3, 1, 2):
            to = lax.rem(place.g + step, GROUP)
            columns = pl.ds(pl.multiple_of(to * self.quarter, self.quarter), self.quarter)
            self.over_g.append(mover.send(own.at[:, columns], spot, place.g_peer(step)))
        columns = pl.ds(pl.multiple_of(place.g * self.quarter, self.quarter), self.quarter)
        self.local = mover.local(own.at[:, columns], spot)

    def wait_g(self):
        self.local.wait()
        for copy in self.over_g:
            copy.wait_recv()

    def send_h(self, source=None):
        place = self.place
        near = self.full.at[self.block(place.h), self.near]
        source = near if source is None else source
        self.over_h = [
            self.mover.send(source, near, place.h_peer(step)) for step in range(1, place.high)
        ]

    def send_x(self, source=None):
        place = self.place
        rows = self.block(place.h)
        source = self.full.at[rows, self.near] if source is None else source
        self.over_x = [self.mover.send(source, self.full.at[rows, self.far], place.x_peer)]

    def pass_h_to_x(self):
        place = self.place
        for step, copy in enumerate(self.over_h, 1):
            copy.wait_recv()
            rows = self.block(place.h_from(step))
            self.over_x.append(
                self.mover.send(
                    self.full.at[rows, self.near], self.full.at[rows, self.far], place.x_peer
                )
            )

    def finish(self):
        for copy in self.over_x:
            copy.wait_recv()


def lane_swap(values):
    half = values.shape[-1] // 2
    return jnp.concatenate([values[:, half:], values[:, :half]], axis=-1)


def norm_rows(values, gain):
    scale = lax.rsqrt(jnp.mean(values * values, axis=-1, keepdims=True) + NORM_EPS)
    return values * scale * gain


def index_of(shape, dim):
    return lax.broadcasted_iota(jnp.int32, shape, dim)


def total_of(condition, values, axis):
    picked = jnp.where(condition, values.astype(F32), 0.0)
    return jnp.sum(picked, axis=axis, keepdims=True)


class Layout:
    def __init__(self, refs, part, row_count, body):
        len_row, perm_row, len_col, perm_col = refs
        docs = len_row.shape[-1]
        self.docs, self.body, self.row_count = docs, body, row_count
        self.bits = (docs // row_count).bit_length() - 1
        down, along = index_of((docs, docs), 0), index_of((docs, docs), 1)
        same_row = (down >> self.bits) == (along >> self.bits)
        before = jnp.where(same_row & (down < along), 1.0, 0.0).astype(BF16)
        self.lens = len_row[part].astype(F32)
        self.lens_col = len_col[part].astype(F32)
        perm, perm_of_col = perm_row[part], perm_col[part]
        matched = perm_of_col == along
        self.dest, self.dest_col = perm >> self.bits, perm_of_col >> self.bits
        self.starts = body + jnp.dot(self.lens.astype(BF16), before, preferred_element_type=F32)
        placed = total_of(matched, jnp.broadcast_to(self.lens_col, matched.shape), 0)
        new_at = body + jnp.dot(placed.astype(BF16), before, preferred_element_type=F32)
        self.new_col = total_of(matched, jnp.broadcast_to(new_at, matched.shape), 1)
        self.new = product(
            new_at.astype(BF16), jnp.where(matched, 1.0, 0.0).astype(BF16), CONTRACT_COLS
        )

    def labels(self, part, row, valid, tokens, row_len, column):
        shape = (tokens, self.docs) if column else (self.docs, tokens)
        axis = 1 if column else 0
        slot, doc = index_of(shape, 1 - axis).astype(F32), index_of(shape, axis)
        start, size, dest = (
            (self.new, self.lens, self.dest)
            if column
            else (self.new_col, self.lens_col, self.dest_col)
        )
        inside = (dest == row) & (slot >= start) & (slot < start + size)
        first = self.row_count + part * self.docs
        segment = total_of(inside, doc + first, axis).astype(jnp.int32)
        position = total_of(inside, slot - start, axis).astype(jnp.int32)
        here = total_of(inside, jnp.ones(shape, F32), axis) > 0.0
        local = index_of((tokens, 1) if column else (1, tokens), 1 - axis)
        long_position = part * self.body + local
        in_long = (local < self.body) & (long_position.astype(F32) < valid)
        empty = -1 - (row * row_len + part * tokens + local)
        segment = jnp.where(in_long, row, jnp.where(here, segment, empty))
        return segment, jnp.where(in_long, long_position, position), in_long, in_long | here

    def send_map(self, row, tokens):
        shape = (self.row_count * 16, self.docs)
        target, doc = index_of(shape, 0) >> 4, index_of(shape, 1)
        mine = ((doc >> self.bits) == row) & (self.dest == target)
        start = total_of(mine, jnp.broadcast_to(self.starts, shape), 1)
        size = total_of(mine, jnp.broadcast_to(self.lens, shape), 1)
        shape = (shape[0], tokens)
        token = ((index_of(shape, 0) >> 2) & 3).astype(F32)
        slot = index_of(shape, 1).astype(F32)
        return jnp.where((token < size) & (slot == start + token), 1.0, 0.0).astype(BF16)

    def recv_map(self, row, tokens):
        shape = (self.docs, self.row_count * 16)
        source, doc = index_of(shape, 1) >> 4, index_of(shape, 0)
        mine = ((doc >> self.bits) == source) & (self.dest_col == row)
        start = total_of(mine, jnp.broadcast_to(self.new_col, shape), 0)
        size = total_of(mine, jnp.broadcast_to(self.lens_col, shape), 0)
        shape = (tokens, shape[1])
        token = ((index_of(shape, 1) >> 2) & 3).astype(F32)
        slot = index_of(shape, 0).astype(F32)
        return jnp.where((token < size) & (slot == start + token), 1.0, 0.0).astype(BF16)


def spread_piece(piece, place, total):
    size = piece.shape[1]
    shape = (size, total)
    spot = index_of(shape, 1) == index_of(shape, 0) + place.d * size
    return jnp.dot(piece, jnp.where(spot, 1.0, 0.0).astype(BF16), preferred_element_type=F32)


def forward_kernel(sizes, *refs):
    (hidden, valid_row, len_row, perm_row, len_col, perm_col, attn_gain, mlp_gain, query_gain,
     key_gain, out_grad, wq, wk, wv, wo, wg, wu, wd) = refs[:18]
    (moved, gains, normed_out, qkv_out, wo_out, full_g, full_u, full_d, grad_y, lin_out, rot_out,
     attended_out, log_total, resid, full_nm, cosine, sine, seg_col, pos_col, seg_row, pos_row, keep, live,
     send_map, recv_map) = refs[18:43]
    (blocks_out, blocks_in, rows_in, gain_row, part_seg, part_pos, normed_own, bias, part_own,
     from_c, from_x, to_c, nm_own, normed, full_qkv, full_wo, lin, rot, attended, send_sems,
     recv_sems, local_sems) = refs[43:]
    place = Place(*sizes)
    mover = Mover(send_sems, recv_sems, local_sems)
    tokens, width = hidden.shape
    head = cosine.shape[1]
    query_width, key_width = wq.shape[1], wk.shape[1]
    columns = width // GROUP
    parts = sizes[1]
    repeat = query_width // key_width

    greet(dp_peers(place) + [place.x_peer, place.c_peer])
    key_parts = [(wk, query_width, key_width), (wv, query_width + key_width, key_width)]
    query = GatherDp(place, mover, [(wq, 0, query_width)], full_qkv)
    key = GatherDp(place, mover, key_parts, full_qkv)
    out = GatherDp(place, mover, [(wo, 0, wo.shape[1])], full_wo)
    gate = GatherColumns(place, mover, wg, full_g)
    upper = GatherColumns(place, mover, wu, full_u)
    lower = GatherColumns(place, mover, wd, full_d)
    gate.send_g()
    key.send_h()
    lower.send_g()
    row_len = parts * tokens
    body = tokens - (len_row.shape[2] // place.dp_size) * MAXSHORT
    layout_refs = (len_row, perm_row, len_col, perm_col)
    here = index_of(valid_row.shape, 1) == place.d
    valid = total_of(here, valid_row[...], 1)
    own = Layout(layout_refs, place.s, place.dp_size, body)
    send_map[...] = own.send_map(place.d, tokens)
    recv_map[...] = own.recv_map(place.d, tokens)
    _, _, own_long, own_live = own.labels(place.s, place.d, valid, tokens, row_len, True)
    keep[...] = jnp.where(own_long, 1.0, 0.0)
    live[...] = jnp.where(own_live, 1.0, 0.0)
    gain_row[:, :width] = spread_piece(attn_gain[...], place, width)
    gain_row[:, width : 2 * width] = spread_piece(mlp_gain[...], place, width)
    gain_row[:, 2 * width : 2 * width + head] = spread_piece(query_gain[...], place, head)
    gain_row[:, 2 * width + head :] = spread_piece(key_gain[...], place, head)
    piece_row = index_of((place.dp_size * 16, 1), 0) & 3
    for q in range(GROUP):
        lanes = pl.ds(q * columns, columns)
        piece = jnp.dot(send_map[...], hidden[:, lanes], preferred_element_type=F32)
        piece = jnp.where(piece_row == q, piece, 0.0)
        total = piece if q == 0 else total + piece
    blocks_out[...] = total.astype(BF16).reshape(blocks_out.shape)
    copies = []
    for step in range(1, place.dp_size):
        other = lax.rem(place.d + step, place.dp_size)
        copies.append(mover.send(blocks_out.at[other], blocks_in.at[place.d], (other, place.s)))
        copies.append(mover.send(gain_row, rows_in.at[place.d], (other, place.s)))
    blocks_in[place.d] = blocks_out[place.d]
    rows_in[place.d] = gain_row[...]
    for copy in copies:
        copy.wait_recv()
    all_gains = rows_in[0]
    for index in range(1, place.dp_size):
        all_gains = all_gains + rows_in[index]
    gains[...] = all_gains
    incoming = blocks_in[...].reshape(place.dp_size * 16, columns)
    for q in range(GROUP):
        lanes = pl.ds(q * columns, columns)
        chosen = jnp.where(piece_row == q, incoming, jnp.zeros_like(incoming))
        here = jnp.dot(recv_map[...], chosen, preferred_element_type=F32)
        here = here + jnp.where(keep[...] > 0.0, hidden[:, lanes].astype(F32), 0.0)
        moved[:, lanes] = here.astype(BF16)

    def norm_moved(index, carry):
        rows = pl.ds(pl.multiple_of(index * 32, 32), 32)
        normed_own[rows, :] = norm_rows(moved[rows, :].astype(F32), gains[:, :width]).astype(BF16)
        grad_y[rows, :] = (out_grad[rows, :].astype(F32) * live[rows, :]).astype(BF16)
        return carry

    lax.fori_loop(0, tokens // 32, norm_moved, 0)
    row = GatherSeq(place, mover, normed_own, normed)

    def label_part(part, carry):
        layout = Layout(layout_refs, part, place.dp_size, body)
        spots = pl.ds(pl.multiple_of(part * tokens, tokens), tokens)
        segment, position, _, _ = layout.labels(part, place.d, valid, tokens, row_len, True)
        seg_col[spots, :], pos_col[spots, :] = segment, position
        segment, position, _, _ = layout.labels(part, place.d, valid, tokens, row_len, False)
        part_seg[part], part_pos[part] = segment, position
        half = head // 2
        lane = index_of((1, head), 1)
        power = jnp.where(lane < half, lane, lane - half).astype(F32)
        angles = pos_col[spots, :].astype(F32) * jnp.exp(
            power * (-2.0 * math.log(ROPE_BASE) / head)
        )
        cosine[spots, :] = jnp.cos(angles)
        sine[spots, :] = jnp.where(lane < half, -1.0, 1.0) * jnp.sin(angles)
        return carry

    query.send_y()
    out.send_h()
    key.send_l()
    lower.wait_g()
    key.pass_h_to_l()
    key.pass_h_to_y()
    query.send_h()
    query.send_l()
    key.pass_own_l_to_y()
    gate.wait_g()
    gate.send_h()
    gate.send_x()
    key.send_y()
    query.pass_h_to_l()
    upper.send_g()
    out.send_l()
    key.pass_l_to_y()
    lower.send_x()
    query.pass_h_to_y()
    query.pass_own_l_to_y()
    row.forward()
    lower.send_h()
    out.pass_h_to_l()
    query.pass_l_to_y()
    out.pass_h_to_y()
    upper.wait_g()
    upper.send_x()
    out.send_y()
    upper.send_h()
    lax.fori_loop(0, parts, label_part, 0)
    seg_row[...] = jnp.concatenate([part_seg[part] for part in range(parts)], axis=1)
    pos_row[...] = jnp.concatenate([part_pos[part] for part in range(parts)], axis=1)
    row.finish()
    query.finish()
    key.finish()
    stores = [mover.local(normed, normed_out), mover.local(full_qkv, qkv_out)]

    gain_query = gains[:, 2 * width : 2 * width + head]
    gain_key = gains[:, 2 * width + head : 2 * width + 2 * head]
    rotated = query_width + key_width
    tile = 2 * head

    def project(part, carry):
        spots = pl.ds(pl.multiple_of(part * tokens, tokens), tokens)
        source = normed[part]
        cos_part, sin_part = cosine[spots, :], sine[spots, :]
        for start in range(0, rotated + key_width, tile):
            result = jnp.dot(source, full_qkv[:, start : start + tile], preferred_element_type=F32)
            if start < rotated:
                lin[spots, start : start + tile] = result.astype(BF16)
                gain = gain_query if start < query_width else gain_key
                for inner in (0, head):
                    unit = norm_rows(result[:, inner : inner + head], gain)
                    turned = unit * cos_part + lane_swap(unit) * sin_part
                    rot[spots, start + inner : start + inner + head] = turned.astype(BF16)
            else:
                rot[spots, start : start + tile] = result.astype(BF16)
        return carry

    lax.fori_loop(0, parts, project, 0)
    stores += [mover.local(lin, lin_out), mover.local(rot, rot_out)]
    out.pass_own_l_to_y()
    gate.pass_h_to_x()
    scale = head ** (-0.5)
    for part in range(parts):
        keys = (part + 1) * tokens
        spots = pl.ds(part * tokens, tokens)
        allowed = (seg_col[spots, :] == seg_row[:, :keys]) & (pos_row[:, :keys] <= pos_col[spots, :])
        some = jnp.where(allowed, 0.0, MASKED)
        for copy in range(repeat):
            bias[copy * tokens : (copy + 1) * tokens, :keys] = some

        def attend(pair, carry):
            key_lanes = pl.ds(pl.multiple_of(query_width + pair * head, head), head)
            value_lanes = pl.ds(pl.multiple_of(rotated + pair * head, head), head)
            query_lanes = [
                pl.ds(pl.multiple_of((pair * repeat + copy) * head, head), head)
                for copy in range(repeat)
            ]
            queries = jnp.concatenate([rot[spots, lanes] for lanes in query_lanes], axis=0)
            scores = product(queries, rot[:keys, key_lanes], CONTRACT_COLS) * scale
            scores = scores + bias[:, :keys]
            peak = jnp.max(scores, axis=-1, keepdims=True)
            expd = jnp.exp(scores - peak)
            weight = jnp.sum(expd, axis=-1, keepdims=True)
            probs = (expd / weight).astype(BF16)
            log_total[pair, part] = jnp.broadcast_to(
                peak + jnp.log(weight), (weight.shape[0], head)
            ).T[0:1, :]
            context = jnp.dot(probs, rot[:keys, value_lanes], preferred_element_type=F32)
            for copy in range(repeat):
                attended[spots, query_lanes[copy]] = context[
                    copy * tokens : (copy + 1) * tokens
                ].astype(BF16)
            return carry

        lax.fori_loop(0, key_width // head, attend, 0)
        if part == 2:
            out.pass_l_to_y()
    out.finish()
    stores += [mover.local(full_wo, wo_out), mover.local(attended, attended_out)]

    def project_out(part, target):
        source = attended[pl.ds(pl.multiple_of(part * tokens, tokens), tokens), :]

        def step(index, carry):
            block = pl.ds(pl.multiple_of(index * 256, 256), 256)
            target[:, block] = product(source, full_wo[block, :], CONTRACT_COLS).astype(BF16)
            return carry

        lax.fori_loop(0, width // 256, step, 0)

    cores = place.cores
    places = ((1 - place.x) * cores, place.x * cores)
    project_out(places[0] + 1 - place.c, to_c.at[0])
    over_c = [mover.send(to_c.at[0], from_c.at[0], place.c_peer)]
    project_out(places[0] + place.c, part_own.at[0])
    over_c[0].wait_recv()
    add_rows(part_own.at[0], [part_own.at[0], from_c.at[0]], tokens, 32)
    over_x = mover.send(part_own.at[0], from_x, place.x_peer)
    project_out(places[1] + 1 - place.c, to_c.at[1])
    over_c.append(mover.send(to_c.at[1], from_c.at[1], place.c_peer))
    project_out(places[1] + place.c, part_own.at[1])
    lower.pass_h_to_x()
    over_c[1].wait_recv()
    over_x.wait_recv()

    def norm_resid(index, carry):
        rows = pl.ds(pl.multiple_of(index * 32, 32), 32)
        total = moved[rows, :].astype(F32) + part_own[1, rows, :].astype(F32)
        total = total + from_c[1, rows, :].astype(F32) + from_x[rows, :].astype(F32)
        resid[rows, :] = total
        nm_own[rows, :] = norm_rows(total, gains[:, width : 2 * width]).astype(BF16)
        return carry

    lax.fori_loop(0, tokens // 32, norm_resid, 0)
    group = GatherGroup(place, mover, nm_own, full_nm)
    upper.pass_h_to_x()
    group.forward()
    group.finish_ici()
    for part in (group, gate, upper, lower):
        part.finish()
    for copy in stores:
        copy.wait()
    mover.finish()


def forward(sizes, collective_id, head_size, args):
    dp_size, seq_size = sizes
    hidden, wq, wk, wo, wg = args[0], args[11], args[12], args[14], args[15]
    tokens, width = hidden.shape
    high = dp_size // GROUP
    rows = wq.shape[0]
    row_len = seq_size * tokens
    rotated = wq.shape[1] + wk.shape[1]
    inner = wg.shape[1] // 2
    group = (GROUP, seq_size // 2, tokens, width)
    heads = wq.shape[1] // head_size
    gain_width = 2 * (width + head_size)
    routes = dp_size * 16
    column, line = (row_len, 1), (1, row_len)
    outs = [
        ((tokens, width), BF16, VMEM),
        ((1, gain_width), F32, VMEM),
        ((seq_size, tokens, width), BF16, HBM),
        ((width, rotated + wk.shape[1]), BF16, HBM),
        ((width, wo.shape[1]), BF16, HBM),
        ((width, inner), BF16, HBM),
        ((width, inner), BF16, HBM),
        ((width, inner), BF16, HBM),
        ((tokens, width), BF16, VMEM),
        ((row_len, rotated), BF16, HBM),
        ((row_len, rotated + wk.shape[1]), BF16, HBM),
        ((row_len, wq.shape[1]), BF16, HBM),
        ((wk.shape[1] // head_size, seq_size, 1, heads * head_size // wk.shape[1] * tokens), F32, VMEM),
        ((tokens, width), F32, VMEM),
        (group, BF16, HBM),
        ((row_len, head_size), F32, VMEM),
        ((row_len, head_size), F32, VMEM),
        (column, jnp.int32, VMEM),
        (column, jnp.int32, VMEM),
        (line, jnp.int32, VMEM),
        (line, jnp.int32, VMEM),
        ((tokens, 1), F32, VMEM),
        ((tokens, 1), F32, VMEM),
        ((routes, tokens), BF16, VMEM),
        ((tokens, routes), BF16, VMEM),
    ]
    scratch = [
        pltpu.VMEM((dp_size, 16, width // GROUP), BF16),
        pltpu.VMEM((dp_size, 16, width // GROUP), BF16),
        pltpu.VMEM((dp_size, 1, gain_width), F32),
        pltpu.VMEM((1, gain_width), F32),
        pltpu.VMEM((seq_size, 1, tokens), jnp.int32),
        pltpu.VMEM((seq_size, 1, tokens), jnp.int32),
        pltpu.VMEM((tokens, width), BF16),
        pltpu.VMEM((wq.shape[1] // wk.shape[1] * tokens, row_len), F32),
        pltpu.VMEM((2, tokens, width), BF16),
        pltpu.VMEM((2, tokens, width), BF16),
        pltpu.VMEM((tokens, width), BF16),
        pltpu.VMEM((2, tokens, width), BF16),
        pltpu.VMEM((tokens, width), BF16),
    ]
    scratch += [
        pltpu.VMEM((seq_size, tokens, width), BF16),
        pltpu.VMEM((width, rotated + wk.shape[1]), BF16),
        pltpu.VMEM((width, wo.shape[1]), BF16),
        pltpu.VMEM((row_len, rotated), BF16),
        pltpu.VMEM((row_len, rotated + wk.shape[1]), BF16),
        pltpu.VMEM((row_len, wq.shape[1]), BF16),
    ]
    sends = 2 * (dp_size - 1) + 4 * (high + 1) + 9 * high
    sends += 3 * (3 + 2 * high) + 2 * GatherGroup.sends + GatherSeq.sends + 3
    return pl.pallas_call(
        functools.partial(forward_kernel, sizes),
        out_shape=[jax.ShapeDtypeStruct(shape, dtype) for shape, dtype, _ in outs],
        in_specs=[VMEM] * 11 + [HBM] * 4 + [VMEM] * 3,
        out_specs=[spec for _, _, spec in outs],
        scratch_shapes=scratch + sems(sends, 24),
        compiler_params=comm_params(collective_id),
        name="forward_attention",
    )(*args)


class ScatterColumns:
    stage_rows = 512

    @staticmethod
    def scratch(high, rows, quarter):
        group_rows = GROUP * rows
        return [
            pltpu.VMEM((high * group_rows, quarter), BF16),
            pltpu.VMEM((max(high - 1, 1), group_rows, quarter), BF16),
            pltpu.VMEM((GROUP - 1, rows, quarter), BF16),
        ]

    def __init__(self, place, mover, parts, from_x, from_h, from_g, mine=None):
        self.place, self.mover, self.parts, self.mine = place, mover, parts, mine
        self.from_x, self.from_h, self.from_g = from_x, from_h, from_g
        self.group_rows, self.quarter = (from_h.shape[1:] if mine is None else mine.shape)

    def rows_of(self, step):
        high = lax.rem(self.place.h + step, self.place.high)
        return high * self.group_rows

    def start(self, steps):
        quarter = self.quarter
        for step in steps:
            rows = pl.ds(pl.multiple_of(self.rows_of(step), self.group_rows), self.group_rows)
            self.over_x[step] = self.mover.send(
                self.parts.at[rows, pl.ds(quarter, quarter)],
                self.from_x.at[rows],
                self.place.x_peer,
            )

    def start_far(self):
        self.over_x = {}
        self.start(range(1, self.place.high))

    def start_near(self):
        self.start((0,))

    def add_x(self, step, stage):
        mover, total = self.mover, self.from_x
        rows = stage.shape[1]
        base = self.rows_of(step)
        near = pl.ds(0, self.quarter)
        pieces = self.group_rows // rows

        def block(index):
            return pl.ds(pl.multiple_of(base + index * rows, rows), rows)

        def load(index):
            return mover.local(self.parts.at[block(index), near], stage.at[index % 2])

        copies = [load(0)]
        self.over_x[step].wait_recv()
        for index in range(pieces):
            if index + 1 < pieces:
                copies.append(load(index + 1))
            copies[index].wait()
            part = total.at[block(index)]
            add_rows(part, [part, stage.at[index % 2]], rows, 64)

    def forward_far(self, stage):
        place = self.place
        self.over_h = []
        for step in range(1, place.high):
            self.add_x(step, stage)
            block = pl.ds(pl.multiple_of(self.rows_of(step), self.group_rows), self.group_rows)
            self.over_h.append(
                self.mover.send(
                    self.from_x.at[block], self.from_h.at[step - 1], place.h_peer(step)
                )
            )

    def send_far(self, added):
        self.over_x, self.over_h = {}, []
        for step in range(1, self.place.high):
            rows = pl.ds(pl.multiple_of(self.rows_of(step), self.group_rows), self.group_rows)
            peer = self.place.h_peer(step)
            self.over_h.append(
                self.mover.send(added.at[rows], self.from_h.at[step - 1], peer)
            )

    def add_near(self, stage):
        self.add_x(0, stage)

    def merge(self):
        rows = pl.ds(pl.multiple_of(self.rows_of(0), self.group_rows), self.group_rows)
        self.mine = self.from_x.at[rows]
        for copy in self.over_h:
            copy.wait_recv()
        terms = [self.mine] + [self.from_h.at[step] for step in range(self.place.high - 1)]
        add_rows(self.mine, terms, self.group_rows, 64)

    def block(self, index):
        rows = self.group_rows // GROUP
        return self.mine.at[pl.ds(pl.multiple_of(index * rows, rows), rows)]

    def send_g(self):
        place = self.place
        self.over_g = []
        for step in (3, 1, 2):
            block = self.block(lax.rem(place.g + step, GROUP))
            copy = self.mover.send(block, self.from_g.at[step - 1], place.g_peer(step))
            self.over_g.append((step, copy))

    def finish(self, stage, out):
        place, quarter = self.place, self.quarter
        columns = pl.ds(pl.multiple_of(place.g * quarter, quarter), quarter)
        stage[:, columns] = self.block(place.g)[...].astype(F32)
        for step, copy in self.over_g:
            copy.wait_recv()
            source = lax.rem(place.g + GROUP - step, GROUP)
            columns = pl.ds(pl.multiple_of(source * quarter, quarter), quarter)
            stage[:, columns] = self.from_g[step - 1].astype(F32)
        if out is not None:
            self.mover.local(stage, out).wait()


class ScatterDp:
    @staticmethod
    def sends(high):
        return 2 * high + high + high - 1

    @staticmethod
    def scratch(high, rows, width):
        return [
            pltpu.VMEM((2, high, rows, width), BF16),
            pltpu.VMEM((high, rows, width), BF16),
            pltpu.VMEM((max(high - 1, 1), rows, width), BF16),
        ]

    def __init__(self, place, mover, parts, out, from_y, from_l, from_h):
        self.place, self.mover, self.parts, self.out = place, mover, parts, out
        self.from_y, self.from_l, self.from_h = from_y, from_l, from_h
        self.rows = out.shape[0]

    def block(self, high, l_index, y_index):
        index = high * GROUP + l_index * 2 + y_index
        return self.parts.at[pl.ds(pl.multiple_of(index * self.rows, self.rows), self.rows)]

    def start(self):
        place = self.place
        self.owners = (1 - place.l, place.l)
        self.over_y = []
        for index, l_owner in enumerate(self.owners):
            for high in range(place.high):
                source = self.block(high, l_owner, 1 - place.y)
                self.over_y.append(
                    self.mover.send(source, self.from_y.at[index, high], place.y_peer)
                )

    def ready(self, index, extra=None):
        place = self.place
        for high in range(place.high):
            self.over_y[index * place.high + high].wait_recv()
            mine = self.block(high, self.owners[index], place.y)
            terms = [mine, self.from_y.at[index, high]]
            if extra is not None:
                extra[high].wait_recv()
                terms.append(self.from_l.at[high])
            add_rows(mine, terms, self.rows, 32)

    def forward_y(self):
        place = self.place
        self.ready(0)
        self.over_l = []
        for high in range(place.high):
            source = self.block(high, 1 - place.l, place.y)
            self.over_l.append(self.mover.send(source, self.from_l.at[high], place.l_peer))

    def forward_l(self):
        place = self.place
        self.ready(1, self.over_l)
        self.over_h = []
        for step in range(1, place.high):
            source = self.block(lax.rem(place.h + step, place.high), place.l, place.y)
            self.over_h.append(
                self.mover.send(source, self.from_h.at[step - 1], place.h_peer(step))
            )

    def finish(self):
        place = self.place
        for copy in self.over_h:
            copy.wait_recv()
        terms = [self.block(place.h, place.l, place.y)]
        terms += [self.from_h.at[step] for step in range(place.high - 1)]
        add_rows(self.out, terms, self.rows, 32)


class ScatterGroup:
    sends = 10

    @staticmethod
    def scratch(rows, width):
        return [
            pltpu.VMEM((GROUP, rows, width), BF16),
            pltpu.VMEM((6, rows // 2, width), BF16),
        ]

    def __init__(self, place, mover, parts, from_c, landed):
        self.place, self.mover, self.parts = place, mover, parts
        self.from_c, self.landed = from_c, landed
        self.owners = (place.gd, place.gy, place.gl, place.g)
        self.over_c = []
        half = from_c.shape[1] // 2
        self.low, self.top = pl.ds(0, half), pl.ds(half, half)

    def start(self, index):
        place = self.place
        source = self.parts.at[self.owners[index], 1 - place.c]
        self.over_c.append(self.mover.send(source, self.from_c.at[index], place.c_peer))

    def forward(self, index):
        place, mover, sums, landed = self.place, self.mover, self.from_c, self.landed
        low, top = self.low, self.top
        self.over_c[index].wait_recv()
        total = sums.at[index]
        own = self.parts.at[self.owners[index], place.c]
        add_rows(total, [total, own], total.shape[0], 32)
        if index == 0:
            self.y_diag = mover.send(sums.at[0, low], landed.at[0], place.y_peer)
            self.l_diag = mover.send(sums.at[0, top], landed.at[1], place.l_peer)
        if index == 1:
            self.y_own = mover.send(sums.at[1, low], landed.at[2], place.y_peer)
        if index == 2:
            self.l_own = mover.send(sums.at[2, top], landed.at[3], place.l_peer)

    def forward_diag(self):
        place, mover, sums, landed = self.place, self.mover, self.from_c, self.landed
        half = sums.shape[1] // 2
        low, top = self.low, self.top
        self.y_diag.wait_recv()
        add_rows(sums.at[2, low], [sums.at[2, low], landed.at[0]], half, 32)
        self.l_last = mover.send(sums.at[2, low], landed.at[4], place.l_peer)
        self.l_diag.wait_recv()
        add_rows(sums.at[1, top], [sums.at[1, top], landed.at[1]], half, 32)
        self.y_last = mover.send(sums.at[1, top], landed.at[5], place.y_peer)

    def finish(self, take):
        half = self.from_c.shape[1] // 2
        chunk = 32
        self.y_own.wait_recv()
        self.l_last.wait_recv()
        self.l_own.wait_recv()
        self.y_last.wait_recv()
        for base, first, second in ((0, 2, 4), (half, 3, 5)):

            def step(index, carry):
                rows = pl.ds(pl.multiple_of(base + index * chunk, chunk), chunk)
                inner = pl.ds(pl.multiple_of(index * chunk, chunk), chunk)
                total = self.from_c[3, rows, :].astype(F32)
                total = total + self.landed[first, inner, :].astype(F32)
                take(rows, total + self.landed[second, inner, :].astype(F32))
                return carry

            lax.fori_loop(0, half // chunk, step, 0)


def norm_back(values, gain, cotangent):
    scale = lax.rsqrt(jnp.mean(values * values, axis=-1, keepdims=True) + NORM_EPS)
    weighted = cotangent * gain
    inner = jnp.mean(weighted * values, axis=-1, keepdims=True)
    unit = values * scale
    return scale * (weighted - unit * (scale * inner)), cotangent * unit


def feed_forward_kernel(sizes, *refs):
    nm_hbm, wg_hbm, wu_hbm, wd_hbm, grad_y, resid, live, gains = refs[:8]
    mixed, grad_resid, full_proj, gain_sum, part_gd, out_gd, out_gg, out_gu = refs[8:16]
    (nm, gy, wg, wu, wd, hidden, gate_grad, up_grad, part_nmlp, part_down, nmlp_c, nmlp_landed,
     down_c, down_landed, grad_proj, stage, column_stage, gd_from_x, gd_from_h) = refs[16:35]
    send_sems, recv_sems, local_sems = refs[35:]
    place = Place(*sizes)
    mover = Mover(send_sems, recv_sems, local_sems)
    tokens, width = resid.shape
    cores = place.cores
    block = cores * tokens
    inner = wg.shape[1]
    tile = 256
    loads = [mover.local(wg_hbm, wg), mover.local(wu_hbm, wu)]
    nm_loads = [mover.local(nm_hbm.at[index], nm.at[index]) for index in range(GROUP)]
    wd_load = mover.local(wd_hbm, wd)
    greet(
        [place.y_peer, place.l_peer, place.c_peer, place.x_peer]
        + [place.h_peer(step) for step in range(1, place.high)]
    )
    gather = GatherGroup(place, mover, grad_y, gy)
    gain_sum[...] = jnp.zeros_like(gain_sum)
    for copy in loads:
        copy.wait()

    def gate_up(index, carry):
        source = nm[index].reshape(block, width)
        rows = pl.ds(pl.multiple_of(index * block, block), block)
        for start in range(0, inner, tile):
            lanes = slice(start, start + tile)
            gate = jnp.dot(source, wg[:, lanes], preferred_element_type=F32)
            upper = jnp.dot(source, wu[:, lanes], preferred_element_type=F32)
            gain = 1.0 / (1.0 + jnp.exp(-gate))
            silu = gate * gain
            hidden[rows, lanes] = (silu * upper).astype(BF16)
            up_grad[rows, lanes] = silu.astype(BF16)
            gate_grad[rows, lanes] = (upper * (gain + silu * (1.0 - gain))).astype(BF16)
        return carry

    def weight_grads(source, grads, targets):
        copies = []
        count = len(grads)
        for index in range(width // tile):
            lanes = pl.ds(index * tile, tile)
            left = source[:, :, :, lanes].reshape(GROUP * block, tile)
            for which in range(count):
                slot = (index * count + which) % 2
                if len(copies) >= 2:
                    copies[-2].wait()
                stage[slot] = product(left, grads[which][...], CONTRACT_ROWS).astype(BF16)
                copies.append(mover.local(stage.at[slot], targets[which].at[lanes]))
        copies[-2].wait()
        copies[-1].wait()

    nm_loads[0].wait()
    nm_loads[1].wait()
    lax.fori_loop(0, 2, gate_up, 0)
    gather.forward()
    nm_loads[2].wait()
    nm_loads[3].wait()
    lax.fori_loop(2, GROUP, gate_up, 0)
    wd_load.wait()

    def down_block(owner):
        rows = pl.ds(pl.multiple_of(owner * block, block), block)

        def step(index, carry):
            lanes = pl.ds(pl.multiple_of(index * tile, tile), tile)
            result = product(hidden[rows, :], wd[lanes, :], CONTRACT_COLS).astype(BF16)
            part_down[owner, :, :, lanes] = result.reshape(cores, tokens, tile)
            return carry

        lax.fori_loop(0, width // tile, step, 0)

    down = ScatterGroup(place, mover, part_down, down_c, down_landed)
    for index in range(GROUP):
        down_block(down.owners[index])
        down.start(index)
    gather.finish_ici()
    gather.finish()
    lower = ScatterColumns(place, mover, part_gd, gd_from_x, gd_from_h, None)

    def back_block(owner):
        rows = pl.ds(pl.multiple_of(owner * block, block), block)
        source = gy[owner].reshape(block, width)
        for start in range(0, inner, tile):
            lanes = slice(start, start + tile)
            grad_mid = jnp.dot(source, wd[:, lanes], preferred_element_type=F32)
            gate_grad[rows, lanes] = (grad_mid * gate_grad[rows, lanes].astype(F32)).astype(BF16)
            up_grad[rows, lanes] = (grad_mid * up_grad[rows, lanes].astype(F32)).astype(BF16)

        def step(index, carry):
            lanes = pl.ds(pl.multiple_of(index * tile, tile), tile)
            result = product(gate_grad[rows, :], wg[lanes, :], CONTRACT_COLS)
            result = result + product(up_grad[rows, :], wu[lanes, :], CONTRACT_COLS)
            part_nmlp[owner, :, :, lanes] = result.astype(BF16).reshape(cores, tokens, tile)
            return carry

        lax.fori_loop(0, width // tile, step, 0)

    down.forward(0)
    nmlp = ScatterGroup(place, mover, part_nmlp, nmlp_c, nmlp_landed)
    back_block(nmlp.owners[0])
    nmlp.start(0)
    back_block(nmlp.owners[1])
    nmlp.start(1)
    nmlp.forward(0)
    back_block(nmlp.owners[2])
    nmlp.start(2)
    nmlp.forward(1)
    nmlp.forward(2)
    weight_grads(gy, [hidden], [part_gd])
    lower.start_far()
    nmlp.forward_diag()
    back_block(nmlp.owners[3])
    nmlp.start(3)
    nmlp.forward(3)

    def back_mlp(rows, total):
        grad, terms = norm_back(resid[rows, :], gains[:, width : 2 * width], total)
        grad = grad + grad_y[rows, :].astype(F32)
        grad_resid[rows, :] = grad
        grad_proj[rows, :] = grad.astype(BF16)
        gain_sum[...] += jnp.sum(terms, axis=0, keepdims=True)

    def mix(rows, total):
        mixed[rows, :] = ((resid[rows, :] + total) * live[rows, :]).astype(BF16)

    nmlp.finish(back_mlp)
    row = GatherSeq(place, mover, grad_proj, full_proj)
    for index in range(1, GROUP):
        down.forward(index)
    down.forward_diag()
    weight_grads(nm, [gate_grad, up_grad], [out_gg, out_gu])
    row.forward()
    added = []
    for step in range(1, place.high):
        lower.add_x(step, column_stage)
        rows = pl.ds(pl.multiple_of(lower.rows_of(step), lower.group_rows), lower.group_rows)
        added.append(mover.local(gd_from_x.at[rows], out_gd.at[rows]))
    down.finish(mix)
    row.finish()
    for copy in added:
        copy.wait()
    mover.finish()


def feed_forward(sizes, collective_id, args):
    dp_size, seq_size = sizes
    nm, wg, resid, gains = args[0], args[1], args[5], args[7]
    tokens, width = resid.shape
    inner = wg.shape[1]
    high = dp_size // GROUP
    piece = min(width // high, ScatterColumns.stage_rows)
    rows = GROUP * (seq_size // 2) * tokens
    outs = [
        ((tokens, width), BF16, VMEM),
        ((tokens, width), F32, VMEM),
        ((seq_size, tokens, width), BF16, HBM),
        ((1, width), F32, VMEM),
        ((width, inner), BF16, HBM),
        ((width, inner // 2), BF16, HBM),
        ((width, inner), BF16, HBM),
        ((width, inner), BF16, HBM),
    ]
    scratch = [pltpu.VMEM(nm.shape, BF16)] * 2
    scratch += [pltpu.VMEM((width, inner), BF16)] * 3
    scratch += [pltpu.VMEM((rows, inner), BF16)] * 3
    scratch += [pltpu.VMEM(nm.shape, BF16)] * 2
    scratch += ScatterGroup.scratch(tokens, width) * 2
    scratch += [pltpu.VMEM((tokens, width), BF16), pltpu.VMEM((2, 256, inner), BF16)]
    scratch += [pltpu.VMEM((2, piece, inner // 2), BF16)]
    scratch += ScatterColumns.scratch(high, width // dp_size, inner // 2)[:2]
    sends = 3 * 10 + GatherSeq.sends + 2 * high
    local = 10 + 3 * (width // 256) + high * (width // high // piece)
    return pl.pallas_call(
        functools.partial(feed_forward_kernel, sizes),
        out_shape=[jax.ShapeDtypeStruct(shape, dtype) for shape, dtype, _ in outs],
        in_specs=[HBM] * 4 + [VMEM] * 4,
        out_specs=[spec for _, _, spec in outs],
        scratch_shapes=scratch + sems(sends, local),
        compiler_params=comm_params(collective_id, 63 * 1024 * 1024),
        name="feed_forward",
    )(*args)


def backward_kernel(sizes, *refs):
    part_gg, part_gu, part_gd, gd_far = refs[:4]
    moved, keep, gain_mlp, gains, cosine, sine = refs[12:18]
    seg_col, pos_col, seg_row, pos_row, log_row, recv_map, send_map = refs[18:25]
    grad_hidden, gain_sums, out_gd, out_gg, out_gu, out_q, out_k, out_v, out_wo = refs[25:34]
    send_sems, recv_sems, local_sems = refs[-3:]
    scratch = list(refs[34:-3])

    def take(count):
        taken = scratch[:count]
        del scratch[:count]
        return taken

    place = Place(*sizes)
    mover = Mover(send_sems, recv_sems, local_sems)
    tokens, width = moved.shape
    parts = sizes[1]
    head = cosine.shape[1]
    query_width = refs[6].shape[1]
    key_width = (refs[7].shape[1] - query_width) // 2
    rotated = query_width + key_width
    columns = width // GROUP
    repeat = query_width // key_width
    column_stage, out_stage = take(2)
    grad_wo, grad_key, grad_query = take(3)
    loaded = take(8)
    wo, full_proj, attended, rot, lin, normed, full_qkv, grad_resid = loaded
    lower = ScatterColumns(place, mover, part_gd, *take(3))
    gate = ScatterColumns(place, mover, part_gg, *take(3))
    upper = ScatterColumns(place, mover, part_gu, *take(3))
    wo_total, key_total = take(2)
    wo_sum = ScatterDp(place, mover, grad_wo, wo_total, *take(3))
    key_sum = ScatterDp(place, mover, grad_key, key_total, *take(3))
    query_sum = ScatterDp(place, mover, grad_query, out_q, *take(3))
    grad_moved, to_c, from_c, from_x = take(4)
    grad_att, grad_keys, grad_values, grad_lin, bias = take(5)
    blocks_out, blocks_in, rows_in, row_c, row_x = take(5)

    loads = [mover.local(source, target) for source, target in zip(refs[4:12], loaded)]
    greet(dp_peers(place) + [place.x_peer, place.c_peer])
    gain_sums[...] = jnp.zeros_like(gain_sums)
    gain_sums[:, width : 2 * width] = gain_mlp[...]
    grad_keys[...] = jnp.zeros_like(grad_keys)
    grad_values[...] = jnp.zeros_like(grad_values)

    def attended_grad(part, carry):
        spots = pl.ds(pl.multiple_of(part * tokens, tokens), tokens)
        for start in range(0, query_width, 256):
            result = jnp.dot(full_proj[part], wo[:, start : start + 256], preferred_element_type=F32)
            grad_att[spots, start : start + 256] = result.astype(BF16)
        return carry


    def out_weight_grad(index, carry):
        lanes = pl.ds(pl.multiple_of(index * 256, 256), 256)
        source = full_proj[:, :, lanes].reshape(parts * tokens, 256)
        grad_wo[lanes, :] = product(source, attended[...], CONTRACT_ROWS).astype(BF16)
        return carry

    scale = head ** (-0.5)
    gain_query = gains[:, 2 * width : 2 * width + head]
    gain_key = gains[:, 2 * width + head : 2 * width + 2 * head]

    def unrotate(spots, lanes, grad, gain, gain_lanes):
        turned = grad * cosine[spots, :] - lane_swap(grad) * sine[spots, :]
        values, terms = norm_back(lin[spots, lanes].astype(F32), gain, turned)
        grad_lin[spots, lanes] = values.astype(BF16)
        gain_sums[:, gain_lanes] += jnp.sum(terms, axis=0, keepdims=True)

    def attention_part(part):
        keys = (part + 1) * tokens
        spots = pl.ds(part * tokens, tokens)
        allowed = (seg_col[:keys, :] == seg_row[:, spots]) & (pos_col[:keys, :] <= pos_row[:, spots])
        some = jnp.where(allowed, 0.0, MASKED)
        for copy in range(repeat):
            bias[:keys, copy * tokens : (copy + 1) * tokens] = some

        def attend(pair, carry):
            key_lanes = pl.ds(pl.multiple_of(query_width + pair * head, head), head)
            value_lanes = pl.ds(pl.multiple_of(rotated + pair * head, head), head)
            own_lanes = pl.ds(pl.multiple_of(pair * head, head), head)
            query_lanes = [
                pl.ds(pl.multiple_of((pair * repeat + copy) * head, head), head)
                for copy in range(repeat)
            ]
            queries = jnp.concatenate([rot[spots, lanes] for lanes in query_lanes], axis=0)
            grads = jnp.concatenate([grad_att[spots, lanes] for lanes in query_lanes], axis=0)
            key_rows, value_rows = rot[:keys, key_lanes], rot[:keys, value_lanes]
            scores = product(key_rows, queries, CONTRACT_COLS) * scale + bias[:keys, :]
            probs = jnp.exp(scores - log_row[pair, part])
            grad_values[:keys, own_lanes] += jnp.dot(
                probs.astype(BF16), grads, preferred_element_type=F32
            )
            grad_probs = product(value_rows, grads, CONTRACT_COLS)
            spread = jnp.sum(probs * grad_probs, axis=0, keepdims=True)
            grad_scores = (probs * (grad_probs - spread)).astype(BF16)
            grad_keys[:keys, own_lanes] += jnp.dot(
                grad_scores, queries, preferred_element_type=F32
            )
            grad_queries = product(grad_scores, key_rows, CONTRACT_ROWS) * scale
            for copy in range(repeat):
                unrotate(
                    spots,
                    query_lanes[copy],
                    grad_queries[copy * tokens : (copy + 1) * tokens],
                    gain_query,
                    pl.ds(2 * width, head),
                )
            return carry

        lax.fori_loop(0, key_width // head, attend, 0)

    def back_all_keys():
        for pair in range(key_width // head):

            def back_keys(part, carry):
                spots = pl.ds(pl.multiple_of(part * tokens, tokens), tokens)
                lanes = pl.ds(pair * head, head)
                unrotate(
                    spots,
                    pl.ds(query_width + pair * head, head),
                    grad_keys[spots, lanes] * scale,
                    gain_key,
                    pl.ds(2 * width + head, head),
                )
                grad_lin[spots, pl.ds(rotated + pair * head, head)] = grad_values[spots, lanes].astype(
                    BF16
                )
                return carry

            lax.fori_loop(0, parts, back_keys, 0)

    def weight_grad(target, start, size):
        def step(index, carry):
            lanes = pl.ds(pl.multiple_of(index * 256, 256), 256)
            source = normed[:, :, lanes].reshape(parts * tokens, 256)
            target[lanes, :] = product(
                source, grad_lin[:, start : start + size], CONTRACT_ROWS
            ).astype(BF16)
            return carry

        lax.fori_loop(0, width // 256, step, 0)

    def normed_grad(part, target):
        source = grad_lin[pl.ds(pl.multiple_of(part * tokens, tokens), tokens), :]

        def step(index, carry):
            block = pl.ds(pl.multiple_of(index * 256, 256), 256)
            target[:, block] = product(source, full_qkv[block, :], CONTRACT_COLS).astype(BF16)
            return carry

        lax.fori_loop(0, width // 256, step, 0)

    cores = place.cores
    places = ((1 - place.x) * cores, place.x * cores)
    over = {}

    def send_other_row():
        normed_grad(places[0] + 1 - place.c, to_c.at[0])
        first = mover.send(to_c.at[0], from_c.at[0], place.c_peer)
        normed_grad(places[0] + place.c, to_c.at[1])
        first.wait_recv()
        add_rows(to_c.at[1], [to_c.at[1], from_c.at[0]], tokens, 32)
        over["x"] = mover.send(to_c.at[1], from_x, place.x_peer)

    def send_own_row():
        normed_grad(places[1] + 1 - place.c, to_c.at[2])
        over["c"] = mover.send(to_c.at[2], from_c.at[1], place.c_peer)
        normed_grad(places[1] + place.c, to_c.at[3])

    def back_normed(index, carry):
        rows = pl.ds(pl.multiple_of(index * 32, 32), 32)
        total = to_c[3, rows, :].astype(F32) + from_c[1, rows, :].astype(F32)
        total = total + from_x[rows, :].astype(F32)
        grad, terms = norm_back(moved[rows, :].astype(F32), gains[:, :width], total)
        grad_moved[rows, :] = (grad_resid[rows, :] + grad).astype(BF16)
        gain_sums[:, :width] += jnp.sum(terms, axis=0, keepdims=True)
        return carry

    piece_row = index_of((place.dp_size * 16, 1), 0) & 3
    copies = []

    def finish_row():
        over["c"].wait_recv()
        over["x"].wait_recv()
        lax.fori_loop(0, tokens // 32, back_normed, 0)
        for q in range(GROUP):
            lanes = pl.ds(q * columns, columns)
            piece = product(recv_map[...], grad_moved[:, lanes], CONTRACT_ROWS)
            piece = jnp.where(piece_row == q, piece, 0.0)
            total = piece if q == 0 else total + piece
        blocks_out[...] = total.astype(BF16).reshape(blocks_out.shape)
        for step in range(1, place.dp_size):
            other = lax.rem(place.d + step, place.dp_size)
            copies.append(mover.send(blocks_out.at[other], blocks_in.at[place.d], (other, place.s)))
            copies.append(mover.send(gain_sums, rows_in.at[place.d], (other, place.s)))
        blocks_in[place.d] = blocks_out[place.d]
        rows_in[place.d] = gain_sums[...]

    def finish_hidden():
        for copy in copies:
            copy.wait_recv()
        row_total = rows_in[0]
        for index in range(1, place.dp_size):
            row_total = row_total + rows_in[index]
        row_c[0] = row_total
        over["gc"] = mover.send(row_c.at[0], row_c.at[1], place.c_peer)
        returned = blocks_in[...].reshape(place.dp_size * 16, columns)
        for q in range(GROUP):
            lanes = pl.ds(q * columns, columns)
            chosen = jnp.where(piece_row == q, returned, jnp.zeros_like(returned))
            here = product(send_map[...], chosen, CONTRACT_ROWS)
            here = here + jnp.where(keep[...] > 0.0, grad_moved[:, lanes].astype(F32), 0.0)
            grad_hidden[:, lanes] = here.astype(BF16)

    def pass_gains():
        over["gc"].wait_recv()
        row_x[0] = row_c[0] + row_c[1]
        over["gx"] = mover.send(row_x.at[0], row_x.at[1], place.x_peer)

    gate.start_far()
    lower.send_far(gd_far)
    lower.start_near()
    for copy in loads[:2]:
        copy.wait()
    lax.fori_loop(0, parts, attended_grad, 0)
    for copy in loads[2:5]:
        copy.wait()
    lax.fori_loop(0, width // 256, out_weight_grad, 0)
    attention_part(0)
    upper.start_far()
    wo_sum.start()
    attention_part(1)
    attention_part(2)
    gate.forward_far(column_stage)
    wo_sum.forward_y()
    for part in range(3, parts):
        attention_part(part)
    upper.start_near()
    back_all_keys()
    for copy in loads[5:]:
        copy.wait()
    weight_grad(grad_key, query_width, 2 * key_width)
    key_sum.start()
    weight_grad(grad_query, 0, query_width)
    upper.forward_far(column_stage)
    lower.add_near(column_stage)
    query_sum.start()
    key_sum.forward_y()
    send_other_row()
    query_sum.forward_y()
    gate.start_near()
    wo_sum.forward_l()
    lower.merge()
    lower.send_g()
    key_sum.forward_l()
    gate.add_near(column_stage)
    wo_sum.finish()
    out_wo[...] = wo_total[...].T
    gate.merge()
    gate.send_g()
    send_own_row()
    finish_row()
    query_sum.forward_l()
    upper.add_near(column_stage)
    upper.merge()
    upper.send_g()
    lower.finish(out_stage, None)
    out_gd[...] = out_stage[...].T
    finish_hidden()
    gate.finish(out_stage, out_gg)
    key_sum.finish()
    out_k[...] = key_total[:, :key_width]
    out_v[...] = key_total[:, key_width:]
    pass_gains()
    upper.finish(out_stage, out_gu)
    query_sum.finish()
    over["gx"].wait_recv()
    mover.finish()
    gain_sums[...] = row_x[0] + row_x[1]


def backward(sizes, collective_id, args):
    dp_size, seq_size = sizes
    part_gg, attended, rot, moved, gains = args[0], args[6], args[7], args[12], args[15]
    tokens, width = moved.shape
    high = dp_size // GROUP
    rows = width // dp_size
    quarter = part_gg.shape[1] // 2
    row_len = seq_size * tokens
    query_width = attended.shape[1]
    key_width = (rot.shape[1] - query_width) // 2
    repeat = query_width // key_width
    outs = [
        ((tokens, width), BF16, VMEM),
        (gains.shape, F32, VMEM),
        ((GROUP * quarter, rows), F32, VMEM),
        ((rows, GROUP * quarter), F32, HBM),
        ((rows, GROUP * quarter), F32, HBM),
        ((rows, query_width), F32, VMEM),
        ((rows, key_width), F32, VMEM),
        ((rows, key_width), F32, VMEM),
        ((query_width, rows), F32, VMEM),
    ]
    piece = min(GROUP * rows, ScatterColumns.stage_rows)
    scratch = [
        pltpu.VMEM((2, piece, quarter), BF16),
        pltpu.VMEM((rows, GROUP * quarter), F32),
    ]
    scratch += [
        pltpu.VMEM((width, query_width), BF16),
        pltpu.VMEM((width, 2 * key_width), BF16),
        pltpu.VMEM((width, query_width), BF16),
    ]
    scratch += [pltpu.VMEM(array.shape, array.dtype) for array in args[4:12]]
    for _ in range(3):
        scratch += ScatterColumns.scratch(high, rows, quarter)
    scratch += [
        pltpu.VMEM((rows, query_width), F32),
        pltpu.VMEM((rows, 2 * key_width), F32),
    ]
    scratch += ScatterDp.scratch(high, rows, query_width)
    scratch += ScatterDp.scratch(high, rows, 2 * key_width)
    scratch += ScatterDp.scratch(high, rows, query_width)
    scratch += [
        pltpu.VMEM((tokens, width), BF16),
        pltpu.VMEM((seq_size, tokens, width), BF16),
        pltpu.VMEM((2, tokens, width), BF16),
        pltpu.VMEM((tokens, width), BF16),
        pltpu.VMEM((row_len, query_width), BF16),
        pltpu.VMEM((row_len, key_width), F32),
        pltpu.VMEM((row_len, key_width), F32),
        pltpu.VMEM((row_len, rot.shape[1]), BF16),
        pltpu.VMEM((row_len, repeat * tokens), F32),
        pltpu.VMEM((dp_size, 16, width // GROUP), BF16),
        pltpu.VMEM((dp_size, 16, width // GROUP), BF16),
        pltpu.VMEM((dp_size,) + gains.shape, F32),
        pltpu.VMEM((2,) + gains.shape, F32),
        pltpu.VMEM((2,) + gains.shape, F32),
    ]
    sends = 3 * (2 * high + 2) + 3 * ScatterDp.sends(high)
    sends += 3 + 2 * (dp_size - 1) + 2
    local = 3 * (high * GROUP * rows // piece + 1) + 9
    return pl.pallas_call(
        functools.partial(backward_kernel, sizes),
        out_shape=[jax.ShapeDtypeStruct(shape, dtype) for shape, dtype, _ in outs],
        in_specs=[HBM] * 12 + [VMEM] * 13,
        out_specs=[spec for _, _, spec in outs],
        scratch_shapes=scratch + sems(sends, local),
        compiler_params=comm_params(collective_id, 63 * 1024 * 1024),
        name="backward_attention",
    )(*args)


def hand_over_kernel(count, *refs):
    held = refs[2 * count : 3 * count]
    sems_in, sems_out = refs[3 * count :]
    loads = [
        pltpu.make_async_copy(refs[index], held[index], sems_in.at[index])
        for index in range(count)
    ]
    stores = [
        pltpu.make_async_copy(held[index], refs[count + index], sems_out.at[index])
        for index in range(count)
    ]
    for copy in loads:
        copy.start()
    for load, store in zip(loads, stores):
        load.wait()
        store.start()
    for copy in stores:
        copy.wait()


def hand_over(arrays):
    count = len(arrays)
    return pl.pallas_call(
        functools.partial(hand_over_kernel, count),
        out_shape=[jax.ShapeDtypeStruct(array.shape, array.dtype) for array in arrays],
        in_specs=[HBM] * count,
        out_specs=[HBM] * count,
        scratch_shapes=[pltpu.VMEM(array.shape, array.dtype) for array in arrays]
        + [pltpu.SemaphoreType.DMA((count,)), pltpu.SemaphoreType.DMA((count,))],
        compiler_params=pltpu.CompilerParams(vmem_limit_bytes=62 * 1024 * 1024),
        name="hand_over",
    )(*arrays)


def per_device(
    sizes,
    hidden_in,
    valid_len,
    doc_lengths,
    doc_perm,
    attn_norm,
    w_query,
    key_weight,
    value_weight,
    w_out,
    query_norm,
    key_norm_gain,
    mlp_norm,
    w_gate,
    w_up,
    w_down,
    out_grad,
):
    model_width = hidden_in.shape[1]
    seq_count, row_count, _ = doc_lengths.shape
    my_row = lax.axis_index("dp")
    my_part = lax.axis_index("seq")
    head_size = query_norm.shape[0] * row_count
    lengths = doc_lengths.reshape(seq_count, -1)
    (
        moved_low,
        gains,
        normed,
        qkv_mat,
        out_mat,
        gate_mat,
        up_mat,
        down_mat,
        grad_y_own,
        rotated_lin,
        rotated_all,
        attended,
        log_total,
        resid_rows,
        normed_mlp,
        cosine,
        sine,
        seg_col,
        pos_col,
        seg_row,
        pos_row,
        keep,
        live,
        send_map,
        recv_map,
    ) = forward(
        sizes,
        1,
        head_size,
        (
            hidden_in,
            valid_len[None, :],
            lengths[:, None, :],
            doc_perm[:, None, :],
            lengths[:, :, None],
            doc_perm[:, :, None],
            attn_norm[None, :],
            mlp_norm[None, :],
            query_norm[None, :],
            key_norm_gain[None, :],
            out_grad,
            w_query,
            key_weight,
            value_weight,
            w_out.T,
            w_gate,
            w_up,
            w_down.T,
        ),
    )
    cuts = (model_width, 2 * model_width, 2 * model_width + head_size)
    mixed, grad_resid, grad_proj, gain_mlp_sum, part_down, grad_down, grad_gate, grad_up = feed_forward(
        sizes,
        2,
        (normed_mlp, gate_mat, up_mat, down_mat, grad_y_own, resid_rows, live, gains),
    )
    (
        grad_hidden,
        gain_sums,
        out_down,
        out_gate,
        out_up,
        out_query,
        out_key,
        out_value,
        out_wo,
    ) = backward(
        sizes,
        3,
        (
            grad_gate,
            grad_up,
            part_down,
            grad_down,
            out_mat,
            grad_proj,
            attended,
            rotated_all,
            rotated_lin,
            normed,
            qkv_mat,
            grad_resid,
            moved_low,
            keep,
            gain_mlp_sum,
            gains,
            cosine,
            sine,
            seg_col,
            pos_col,
            seg_row,
            pos_row,
            log_total,
            recv_map,
            send_map,
        ),
    )
    device = my_row * seq_count + my_part

    def own_piece(vector):
        size = vector.shape[0] // (row_count * seq_count)
        return lax.dynamic_slice_in_dim(vector, device * size, size)

    sum_attn, sum_mlp, sum_query, sum_key = [own_piece(v) for v in jnp.split(gain_sums[0], cuts)]
    (
        mixed,
        grad_hidden,
        out_query,
        out_key,
        out_value,
        out_wo,
        out_gate,
        out_up,
        out_down,
    ) = hand_over(
        (
            mixed,
            grad_hidden,
            out_query,
            out_key,
            out_value,
            out_wo,
            out_gate,
            out_up,
            out_down,
        )
    )
    return (
        mixed,
        grad_hidden,
        sum_attn,
        out_query,
        out_key,
        out_value,
        out_wo,
        sum_query,
        sum_key,
        sum_mlp,
        out_gate,
        out_up,
        out_down,
    )


def solution(mesh):
    in_specs = (
        P(("dp", "seq"), None),
        P(),
        P(),
        P(),
        P("dp"),
        P("dp", "seq"),
        P("dp", "seq"),
        P("dp", "seq"),
        P("seq", "dp"),
        P("dp"),
        P("dp"),
        P("dp"),
        P("dp", "seq"),
        P("dp", "seq"),
        P("seq", "dp"),
        P(("dp", "seq"), None),
    )
    out_specs = (
        P(("dp", "seq"), None),
        P(("dp", "seq"), None),
        P(("dp", "seq")),
        P("dp", "seq"),
        P("dp", "seq"),
        P("dp", "seq"),
        P("seq", "dp"),
        P(("dp", "seq")),
        P(("dp", "seq")),
        P(("dp", "seq")),
        P("dp", "seq"),
        P("dp", "seq"),
        P("seq", "dp"),
    )
    return jax.shard_map(
        functools.partial(per_device, (mesh.shape["dp"], mesh.shape["seq"])), mesh=mesh, in_specs=in_specs, out_specs=out_specs, check_vma=False
    )
```

```python
import functools
import math

import jax
import jax.numpy as jnp
from jax import lax
from jax.experimental import pallas as pl
from jax.experimental.pallas import tpu as pltpu
from jax.sharding import PartitionSpec as P

MAXSHORT = 4
GROUP = 4
MESH = pl.DeviceIdType.MESH
HBM = pl.BlockSpec(memory_space=pltpu.HBM)
VMEM = pl.BlockSpec(memory_space=pltpu.VMEM)
BF16 = jnp.bfloat16
F32 = jnp.float32


NORM_EPS = 1e-06
ROPE_BASE = 1000000.0
MASKED = -1e30
CONTRACT_ROWS = (((0,), (0,)), ((), ()))
CONTRACT_COLS = (((1,), (1,)), ((), ()))


def product(left, right, dims):
    return lax.dot_general(left, right, dims, preferred_element_type=jnp.float32)


class Place:
    def __init__(self, dp_size, seq_size):
        self.dp_size = dp_size
        self.seq_size = seq_size
        self.high = dp_size // GROUP
        self.cores = seq_size // 2
        self.d = lax.axis_index("dp")
        self.s = lax.axis_index("seq")
        self.g = lax.rem(self.d, GROUP)
        self.h = lax.div(self.d, GROUP)
        self.x = lax.div(self.s, self.cores)
        self.c = lax.rem(self.s, self.cores)
        self.y = lax.rem(self.g, 2)
        self.l = lax.div(self.g, 2)
        self.gy = self.g + 1 - 2 * self.y
        self.gl = lax.rem(self.g + 2, GROUP)
        self.gd = 3 - self.g
        self.y_peer = (self.h * GROUP + self.gy, self.s)
        self.l_peer = (self.h * GROUP + self.gl, self.s)
        self.d_peer = (self.h * GROUP + self.gd, self.s)
        self.x_peer = (self.d, (1 - self.x) * self.cores + self.c)
        self.c_peer = (self.d, self.x * self.cores + 1 - self.c)

    def h_peer(self, step):
        return (lax.rem(self.h + step, self.high) * GROUP + self.g, self.s)

    def h_from(self, step):
        return lax.rem(self.h + self.high - step, self.high)

    def g_peer(self, step):
        return (self.h * GROUP + lax.rem(self.g + step, GROUP), self.s)


class Mover:
    def __init__(self, send_sems, recv_sems, local_sems):
        self.send_sems = send_sems
        self.recv_sems = recv_sems
        self.local_sems = local_sems
        self.count = 0
        self.local_count = 0
        self.sent = []

    def send(self, source, target, device):
        index = self.count
        self.count += 1
        copy = pltpu.make_async_remote_copy(
            src_ref=source,
            dst_ref=target,
            send_sem=self.send_sems.at[index],
            recv_sem=self.recv_sems.at[index],
            device_id=device,
            device_id_type=MESH,
        )
        copy.start()
        self.sent.append(copy)
        return copy

    def local(self, source, target):
        index = self.local_count
        self.local_count += 1
        copy = pltpu.make_async_copy(source, target, self.local_sems.at[index])
        copy.start()
        return copy

    def drain(self, copy):
        copy.wait_send()
        self.sent = [other for other in self.sent if other is not copy]

    def finish(self):
        for copy in self.sent:
            copy.wait_send()


def greet(peers):
    barrier = pltpu.get_barrier_semaphore()
    for peer in peers:
        pl.semaphore_signal(barrier, inc=1, device_id=peer, device_id_type=MESH)
    pl.semaphore_wait(barrier, len(peers))


def dp_peers(place):
    return [
        (lax.rem(place.d + step, place.dp_size), place.s) for step in range(1, place.dp_size)
    ]


def sems(count, local):
    return [
        pltpu.SemaphoreType.DMA((count,)),
        pltpu.SemaphoreType.DMA((count,)),
        pltpu.SemaphoreType.DMA((max(local, 1),)),
    ]


def comm_params(collective_id, vmem=None):
    return pltpu.CompilerParams(
        collective_id=collective_id,
        has_side_effects=True,
        vmem_limit_bytes=vmem if vmem is not None else 60 * 1024 * 1024,
    )


def add_rows(target, terms, rows, chunk):
    def step(index, carry):
        part = pl.ds(pl.multiple_of(index * chunk, chunk), chunk)
        total = terms[0][part, :].astype(F32)
        for term in terms[1:]:
            total = total + term[part, :].astype(F32)
        target[part, :] = total.astype(target.dtype)
        return carry

    lax.fori_loop(0, rows // chunk, step, 0)


class GatherSeq:
    sends = 3

    def __init__(self, place, mover, own, full):
        self.place, self.mover, self.full = place, mover, full
        self.local = mover.local(own, full.at[place.s])
        self.over_x = mover.send(own, full.at[place.s], place.x_peer)
        self.over_c = mover.send(own, full.at[place.s], place.c_peer)

    def forward(self):
        self.over_x.wait_recv()
        block = self.full.at[self.place.x_peer[1]]
        self.passed = self.mover.send(block, block, self.place.c_peer)

    def finish(self):
        self.local.wait()
        self.over_c.wait_recv()
        self.passed.wait_recv()


class GatherGroup:
    sends = 10

    def __init__(self, place, mover, own, full):
        self.place, self.mover, self.full = place, mover, full
        half = own.shape[0] // 2
        self.low, self.top = pl.ds(0, half), pl.ds(half, half)
        self.local = mover.local(own, full.at[place.g, place.c])
        spot = full.at[place.g, place.c]
        self.y_low = mover.send(own.at[self.low], spot.at[self.low], place.y_peer)
        self.l_top = mover.send(own.at[self.top], spot.at[self.top], place.l_peer)
        self.y_top = mover.send(own.at[self.top], spot.at[self.top], place.y_peer)
        self.l_low = mover.send(own.at[self.low], spot.at[self.low], place.l_peer)
        self.core = [mover.send(own, spot, place.c_peer)]

    def forward(self):
        place, mover, full = self.place, self.mover, self.full
        self.y_low.wait_recv()
        part = full.at[place.gy, place.c, self.low]
        self.d_low = mover.send(part, part, place.l_peer)
        self.l_top.wait_recv()
        part = full.at[place.gl, place.c, self.top]
        self.d_top = mover.send(part, part, place.y_peer)
        self.y_top.wait_recv()
        part = full.at[place.gy, place.c]
        self.core.append(mover.send(part, part, place.c_peer))
        self.l_low.wait_recv()
        part = full.at[place.gl, place.c]
        self.core.append(mover.send(part, part, place.c_peer))

    def finish_ici(self):
        place = self.place
        self.d_low.wait_recv()
        self.d_top.wait_recv()
        part = self.full.at[place.gd, place.c]
        self.core.append(self.mover.send(part, part, place.c_peer))

    def finish(self):
        self.local.wait()
        for copy in self.core:
            copy.wait_recv()


class GatherDp:
    def __init__(self, place, mover, pieces, full):
        self.place, self.mover, self.full, self.pieces = place, mover, full, pieces
        first, last = pieces[0], pieces[-1]
        self.window = pl.ds(first[1], last[1] + last[2] - first[1])
        self.rows = full.shape[0] // place.dp_size
        own_rows = self.block(place.d)
        self.spots = [full.at[own_rows, pl.ds(start, size)] for _, start, size in pieces]
        self.local = [
            mover.local(piece[0], spot) for piece, spot in zip(pieces, self.spots)
        ]
        self.over_y, self.passed_l = [], []

    def block(self, index):
        return pl.ds(pl.multiple_of(index * self.rows, self.rows), self.rows)

    def own_to(self, peer):
        return [
            self.mover.send(piece[0], spot, peer) for piece, spot in zip(self.pieces, self.spots)
        ]

    def send_h(self):
        place = self.place
        self.over_h = [self.own_to(place.h_peer(step)) for step in range(1, place.high)]

    def send_l(self):
        self.own_l = self.own_to(self.place.l_peer)

    def send_y(self):
        self.over_y += self.own_to(self.place.y_peer)

    def part(self, high, index):
        return self.full.at[self.block(high * GROUP + index), self.window]

    def pass_h_to_l(self):
        place = self.place
        for step, copies in enumerate(self.over_h, 1):
            for copy in copies:
                copy.wait_recv()
            part = self.part(place.h_from(step), place.g)
            self.passed_l.append(self.mover.send(part, part, place.l_peer))

    def pass_h_to_y(self):
        place = self.place
        for step in range(1, place.high):
            part = self.part(place.h_from(step), place.g)
            self.over_y.append(self.mover.send(part, part, place.y_peer))

    def pass_own_l_to_y(self):
        place = self.place
        for copy in self.own_l:
            copy.wait_recv()
        part = self.part(place.h, place.gl)
        self.over_y.append(self.mover.send(part, part, place.y_peer))

    def pass_l_to_y(self):
        place = self.place
        for step, copy in enumerate(self.passed_l, 1):
            copy.wait_recv()
            part = self.part(place.h_from(step), place.gl)
            self.over_y.append(self.mover.send(part, part, place.y_peer))

    def finish(self):
        for copy in self.local:
            copy.wait()
        for copy in self.over_y:
            copy.wait_recv()


class GatherColumns:
    def __init__(self, place, mover, own, full):
        self.place, self.mover, self.full, self.own = place, mover, full, own
        self.quarter = own.shape[1] // GROUP
        self.rows = own.shape[0]
        self.near = pl.ds(0, self.quarter)
        self.far = pl.ds(self.quarter, self.quarter)

    def block(self, high):
        rows = GROUP * self.rows
        return pl.ds(pl.multiple_of(high * rows, rows), rows)

    def send_g(self, spot=None):
        place, mover, own = self.place, self.mover, self.own
        if spot is None:
            spot = self.full.at[
                pl.ds(pl.multiple_of(place.d * self.rows, self.rows), self.rows), self.near
            ]
        self.over_g = []
        for step in (3, 1, 2):
            to = lax.rem(place.g + step, GROUP)
            columns = pl.ds(pl.multiple_of(to * self.quarter, self.quarter), self.quarter)
            self.over_g.append(mover.send(own.at[:, columns], spot, place.g_peer(step)))
        columns = pl.ds(pl.multiple_of(place.g * self.quarter, self.quarter), self.quarter)
        self.local = mover.local(own.at[:, columns], spot)

    def wait_g(self):
        self.local.wait()
        for copy in self.over_g:
            copy.wait_recv()

    def send_h(self, source=None):
        place = self.place
        near = self.full.at[self.block(place.h), self.near]
        source = near if source is None else source
        self.over_h = [
            self.mover.send(source, near, place.h_peer(step)) for step in range(1, place.high)
        ]

    def send_x(self, source=None):
        place = self.place
        rows = self.block(place.h)
        source = self.full.at[rows, self.near] if source is None else source
        self.over_x = [self.mover.send(source, self.full.at[rows, self.far], place.x_peer)]

    def pass_h_to_x(self):
        place = self.place
        for step, copy in enumerate(self.over_h, 1):
            copy.wait_recv()
            rows = self.block(place.h_from(step))
            self.over_x.append(
                self.mover.send(
                    self.full.at[rows, self.near], self.full.at[rows, self.far], place.x_peer
                )
            )

    def finish(self):
        for copy in self.over_x:
            copy.wait_recv()


def lane_swap(values):
    half = values.shape[-1] // 2
    return jnp.concatenate([values[:, half:], values[:, :half]], axis=-1)


def norm_rows(values, gain):
    scale = lax.rsqrt(jnp.mean(values * values, axis=-1, keepdims=True) + NORM_EPS)
    return values * scale * gain


def index_of(shape, dim):
    return lax.broadcasted_iota(jnp.int32, shape, dim)


def total_of(condition, values, axis):
    picked = jnp.where(condition, values.astype(F32), 0.0)
    return jnp.sum(picked, axis=axis, keepdims=True)


class Layout:
    def __init__(self, refs, part, row_count, body):
        len_row, perm_row, len_col, perm_col = refs
        docs = len_row.shape[-1]
        self.docs, self.body, self.row_count = docs, body, row_count
        self.bits = (docs // row_count).bit_length() - 1
        down, along = index_of((docs, docs), 0), index_of((docs, docs), 1)
        same_row = (down >> self.bits) == (along >> self.bits)
        before = jnp.where(same_row & (down < along), 1.0, 0.0).astype(BF16)
        self.lens = len_row[part].astype(F32)
        self.lens_col = len_col[part].astype(F32)
        perm, perm_of_col = perm_row[part], perm_col[part]
        matched = perm_of_col == along
        self.dest, self.dest_col = perm >> self.bits, perm_of_col >> self.bits
        self.starts = body + jnp.dot(self.lens.astype(BF16), before, preferred_element_type=F32)
        placed = total_of(matched, jnp.broadcast_to(self.lens_col, matched.shape), 0)
        new_at = body + jnp.dot(placed.astype(BF16), before, preferred_element_type=F32)
        self.new_col = total_of(matched, jnp.broadcast_to(new_at, matched.shape), 1)
        self.new = product(
            new_at.astype(BF16), jnp.where(matched, 1.0, 0.0).astype(BF16), CONTRACT_COLS
        )

    def labels(self, part, row, valid, tokens, row_len, column):
        shape = (tokens, self.docs) if column else (self.docs, tokens)
        axis = 1 if column else 0
        slot, doc = index_of(shape, 1 - axis).astype(F32), index_of(shape, axis)
        start, size, dest = (
            (self.new, self.lens, self.dest)
            if column
            else (self.new_col, self.lens_col, self.dest_col)
        )
        inside = (dest == row) & (slot >= start) & (slot < start + size)
        first = self.row_count + part * self.docs
        segment = total_of(inside, doc + first, axis).astype(jnp.int32)
        position = total_of(inside, slot - start, axis).astype(jnp.int32)
        here = total_of(inside, jnp.ones(shape, F32), axis) > 0.0
        local = index_of((tokens, 1) if column else (1, tokens), 1 - axis)
        long_position = part * self.body + local
        in_long = (local < self.body) & (long_position.astype(F32) < valid)
        empty = -1 - (row * row_len + part * tokens + local)
        segment = jnp.where(in_long, row, jnp.where(here, segment, empty))
        return segment, jnp.where(in_long, long_position, position), in_long, in_long | here

    def send_map(self, row, tokens):
        shape = (self.row_count * 16, self.docs)
        target, doc = index_of(shape, 0) >> 4, index_of(shape, 1)
        mine = ((doc >> self.bits) == row) & (self.dest == target)
        start = total_of(mine, jnp.broadcast_to(self.starts, shape), 1)
        size = total_of(mine, jnp.broadcast_to(self.lens, shape), 1)
        shape = (shape[0], tokens)
        token = ((index_of(shape, 0) >> 2) & 3).astype(F32)
        slot = index_of(shape, 1).astype(F32)
        return jnp.where((token < size) & (slot == start + token), 1.0, 0.0).astype(BF16)

    def recv_map(self, row, tokens):
        shape = (self.docs, self.row_count * 16)
        source, doc = index_of(shape, 1) >> 4, index_of(shape, 0)
        mine = ((doc >> self.bits) == source) & (self.dest_col == row)
        start = total_of(mine, jnp.broadcast_to(self.new_col, shape), 0)
        size = total_of(mine, jnp.broadcast_to(self.lens_col, shape), 0)
        shape = (tokens, shape[1])
        token = ((index_of(shape, 1) >> 2) & 3).astype(F32)
        slot = index_of(shape, 0).astype(F32)
        return jnp.where((token < size) & (slot == start + token), 1.0, 0.0).astype(BF16)


def spread_piece(piece, place, total):
    size = piece.shape[1]
    shape = (size, total)
    spot = index_of(shape, 1) == index_of(shape, 0) + place.d * size
    return jnp.dot(piece, jnp.where(spot, 1.0, 0.0).astype(BF16), preferred_element_type=F32)


def forward_kernel(sizes, *refs):
    (hidden, valid_row, len_row, perm_row, len_col, perm_col, attn_gain, mlp_gain, query_gain,
     key_gain, out_grad, wq, wk, wv, wo, wg, wu, wd) = refs[:18]
    (moved, gains, normed_out, qkv_out, wo_out, full_g, full_u, full_d, grad_y, lin_out, rot_out,
     attended_out, log_total, resid, full_nm, cosine, sine, seg_col, pos_col, seg_row, pos_row, keep, live,
     send_map, recv_map) = refs[18:43]
    (blocks_out, blocks_in, rows_in, gain_row, part_seg, part_pos, normed_own, bias, part_own,
     from_c, from_x, to_c, nm_own, normed, full_qkv, full_wo, lin, rot, attended, send_sems,
     recv_sems, local_sems) = refs[43:]
    place = Place(*sizes)
    mover = Mover(send_sems, recv_sems, local_sems)
    tokens, width = hidden.shape
    head = cosine.shape[1]
    query_width, key_width = wq.shape[1], wk.shape[1]
    columns = width // GROUP
    parts = sizes[1]
    repeat = query_width // key_width

    greet(dp_peers(place) + [place.x_peer, place.c_peer])
    key_parts = [(wk, query_width, key_width), (wv, query_width + key_width, key_width)]
    query = GatherDp(place, mover, [(wq, 0, query_width)], full_qkv)
    key = GatherDp(place, mover, key_parts, full_qkv)
    out = GatherDp(place, mover, [(wo, 0, wo.shape[1])], full_wo)
    gate = GatherColumns(place, mover, wg, full_g)
    upper = GatherColumns(place, mover, wu, full_u)
    lower = GatherColumns(place, mover, wd, full_d)
    gate.send_g()
    key.send_h()
    lower.send_g()
    row_len = parts * tokens
    body = tokens - (len_row.shape[2] // place.dp_size) * MAXSHORT
    layout_refs = (len_row, perm_row, len_col, perm_col)
    here = index_of(valid_row.shape, 1) == place.d
    valid = total_of(here, valid_row[...], 1)
    own = Layout(layout_refs, place.s, place.dp_size, body)
    send_map[...] = own.send_map(place.d, tokens)
    recv_map[...] = own.recv_map(place.d, tokens)
    _, _, own_long, own_live = own.labels(place.s, place.d, valid, tokens, row_len, True)
    keep[...] = jnp.where(own_long, 1.0, 0.0)
    live[...] = jnp.where(own_live, 1.0, 0.0)
    gain_row[:, :width] = spread_piece(attn_gain[...], place, width)
    gain_row[:, width : 2 * width] = spread_piece(mlp_gain[...], place, width)
    gain_row[:, 2 * width : 2 * width + head] = spread_piece(query_gain[...], place, head)
    gain_row[:, 2 * width + head :] = spread_piece(key_gain[...], place, head)
    piece_row = index_of((place.dp_size * 16, 1), 0) & 3
    for q in range(GROUP):
        lanes = pl.ds(q * columns, columns)
        piece = jnp.dot(send_map[...], hidden[:, lanes], preferred_element_type=F32)
        piece = jnp.where(piece_row == q, piece, 0.0)
        total = piece if q == 0 else total + piece
    blocks_out[...] = total.astype(BF16).reshape(blocks_out.shape)
    copies = []
    for step in range(1, place.dp_size):
        other = lax.rem(place.d + step, place.dp_size)
        copies.append(mover.send(blocks_out.at[other], blocks_in.at[place.d], (other, place.s)))
        copies.append(mover.send(gain_row, rows_in.at[place.d], (other, place.s)))
    blocks_in[place.d] = blocks_out[place.d]
    rows_in[place.d] = gain_row[...]
    for copy in copies:
        copy.wait_recv()
    all_gains = rows_in[0]
    for index in range(1, place.dp_size):
        all_gains = all_gains + rows_in[index]
    gains[...] = all_gains
    incoming = blocks_in[...].reshape(place.dp_size * 16, columns)
    for q in range(GROUP):
        lanes = pl.ds(q * columns, columns)
        chosen = jnp.where(piece_row == q, incoming, jnp.zeros_like(incoming))
        here = jnp.dot(recv_map[...], chosen, preferred_element_type=F32)
        here = here + jnp.where(keep[...] > 0.0, hidden[:, lanes].astype(F32), 0.0)
        moved[:, lanes] = here.astype(BF16)

    def norm_moved(index, carry):
        rows = pl.ds(pl.multiple_of(index * 32, 32), 32)
        normed_own[rows, :] = norm_rows(moved[rows, :].astype(F32), gains[:, :width]).astype(BF16)
        grad_y[rows, :] = (out_grad[rows, :].astype(F32) * live[rows, :]).astype(BF16)
        return carry

    lax.fori_loop(0, tokens // 32, norm_moved, 0)
    row = GatherSeq(place, mover, normed_own, normed)

    def label_part(part, carry):
        layout = Layout(layout_refs, part, place.dp_size, body)
        spots = pl.ds(pl.multiple_of(part * tokens, tokens), tokens)
        segment, position, _, _ = layout.labels(part, place.d, valid, tokens, row_len, True)
        seg_col[spots, :], pos_col[spots, :] = segment, position
        segment, position, _, _ = layout.labels(part, place.d, valid, tokens, row_len, False)
        part_seg[part], part_pos[part] = segment, position
        half = head // 2
        lane = index_of((1, head), 1)
        power = jnp.where(lane < half, lane, lane - half).astype(F32)
        angles = pos_col[spots, :].astype(F32) * jnp.exp(
            power * (-2.0 * math.log(ROPE_BASE) / head)
        )
        cosine[spots, :] = jnp.cos(angles)
        sine[spots, :] = jnp.where(lane < half, -1.0, 1.0) * jnp.sin(angles)
        return carry

    query.send_y()
    out.send_h()
    key.send_l()
    lower.wait_g()
    key.pass_h_to_l()
    key.pass_h_to_y()
    query.send_h()
    query.send_l()
    key.pass_own_l_to_y()
    gate.wait_g()
    gate.send_h()
    gate.send_x()
    key.send_y()
    query.pass_h_to_l()
    upper.send_g()
    out.send_l()
    key.pass_l_to_y()
    lower.send_x()
    query.pass_h_to_y()
    query.pass_own_l_to_y()
    row.forward()
    lower.send_h()
    out.pass_h_to_l()
    query.pass_l_to_y()
    out.pass_h_to_y()
    upper.wait_g()
    upper.send_x()
    out.send_y()
    upper.send_h()
    lax.fori_loop(0, parts, label_part, 0)
    seg_row[...] = jnp.concatenate([part_seg[part] for part in range(parts)], axis=1)
    pos_row[...] = jnp.concatenate([part_pos[part] for part in range(parts)], axis=1)
    row.finish()
    query.finish()
    key.finish()
    stores = [mover.local(normed, normed_out), mover.local(full_qkv, qkv_out)]

    gain_query = gains[:, 2 * width : 2 * width + head]
    gain_key = gains[:, 2 * width + head : 2 * width + 2 * head]
    rotated = query_width + key_width
    tile = 2 * head

    def project(part, carry):
        spots = pl.ds(pl.multiple_of(part * tokens, tokens), tokens)
        source = normed[part]
        cos_part, sin_part = cosine[spots, :], sine[spots, :]
        for start in range(0, rotated + key_width, tile):
            result = jnp.dot(source, full_qkv[:, start : start + tile], preferred_element_type=F32)
            if start < rotated:
                lin[spots, start : start + tile] = result.astype(BF16)
                gain = gain_query if start < query_width else gain_key
                for inner in (0, head):
                    unit = norm_rows(result[:, inner : inner + head], gain)
                    turned = unit * cos_part + lane_swap(unit) * sin_part
                    rot[spots, start + inner : start + inner + head] = turned.astype(BF16)
            else:
                rot[spots, start : start + tile] = result.astype(BF16)
        return carry

    lax.fori_loop(0, parts, project, 0)
    stores += [mover.local(lin, lin_out), mover.local(rot, rot_out)]
    out.pass_own_l_to_y()
    gate.pass_h_to_x()
    scale = head ** (-0.5)
    for part in range(parts):
        keys = (part + 1) * tokens
        spots = pl.ds(part * tokens, tokens)
        allowed = (seg_col[spots, :] == seg_row[:, :keys]) & (pos_row[:, :keys] <= pos_col[spots, :])
        some = jnp.where(allowed, 0.0, MASKED)
        for copy in range(repeat):
            bias[copy * tokens : (copy + 1) * tokens, :keys] = some

        def attend(pair, carry):
            key_lanes = pl.ds(pl.multiple_of(query_width + pair * head, head), head)
            value_lanes = pl.ds(pl.multiple_of(rotated + pair * head, head), head)
            query_lanes = [
                pl.ds(pl.multiple_of((pair * repeat + copy) * head, head), head)
                for copy in range(repeat)
            ]
            queries = jnp.concatenate([rot[spots, lanes] for lanes in query_lanes], axis=0)
            scores = product(queries, rot[:keys, key_lanes], CONTRACT_COLS) * scale
            scores = scores + bias[:, :keys]
            peak = jnp.max(scores, axis=-1, keepdims=True)
            expd = jnp.exp(scores - peak)
            weight = jnp.sum(expd, axis=-1, keepdims=True)
            probs = (expd / weight).astype(BF16)
            log_total[pair, part] = jnp.broadcast_to(
                peak + jnp.log(weight), (weight.shape[0], head)
            ).T[0:1, :]
            context = jnp.dot(probs, rot[:keys, value_lanes], preferred_element_type=F32)
            for copy in range(repeat):
                attended[spots, query_lanes[copy]] = context[
                    copy * tokens : (copy + 1) * tokens
                ].astype(BF16)
            return carry

        lax.fori_loop(0, key_width // head, attend, 0)
        if part == 2:
            out.pass_l_to_y()
    out.finish()
    stores += [mover.local(full_wo, wo_out), mover.local(attended, attended_out)]

    def project_out(part, target):
        source = attended[pl.ds(pl.multiple_of(part * tokens, tokens), tokens), :]

        def step(index, carry):
            block = pl.ds(pl.multiple_of(index * 256, 256), 256)
            target[:, block] = product(source, full_wo[block, :], CONTRACT_COLS).astype(BF16)
            return carry

        lax.fori_loop(0, width // 256, step, 0)

    cores = place.cores
    places = ((1 - place.x) * cores, place.x * cores)
    project_out(places[0] + 1 - place.c, to_c.at[0])
    over_c = [mover.send(to_c.at[0], from_c.at[0], place.c_peer)]
    project_out(places[0] + place.c, part_own.at[0])
    over_c[0].wait_recv()
    add_rows(part_own.at[0], [part_own.at[0], from_c.at[0]], tokens, 32)
    over_x = mover.send(part_own.at[0], from_x, place.x_peer)
    project_out(places[1] + 1 - place.c, to_c.at[1])
    over_c.append(mover.send(to_c.at[1], from_c.at[1], place.c_peer))
    project_out(places[1] + place.c, part_own.at[1])
    lower.pass_h_to_x()
    over_c[1].wait_recv()
    over_x.wait_recv()

    def norm_resid(index, carry):
        rows = pl.ds(pl.multiple_of(index * 32, 32), 32)
        total = moved[rows, :].astype(F32) + part_own[1, rows, :].astype(F32)
        total = total + from_c[1, rows, :].astype(F32) + from_x[rows, :].astype(F32)
        resid[rows, :] = total
        nm_own[rows, :] = norm_rows(total, gains[:, width : 2 * width]).astype(BF16)
        return carry

    lax.fori_loop(0, tokens // 32, norm_resid, 0)
    group = GatherGroup(place, mover, nm_own, full_nm)
    upper.pass_h_to_x()
    group.forward()
    group.finish_ici()
    for part in (group, gate, upper, lower):
        part.finish()
    for copy in stores:
        copy.wait()
    mover.finish()


def forward(sizes, collective_id, head_size, args):
    dp_size, seq_size = sizes
    hidden, wq, wk, wo, wg = args[0], args[11], args[12], args[14], args[15]
    tokens, width = hidden.shape
    high = dp_size // GROUP
    rows = wq.shape[0]
    row_len = seq_size * tokens
    rotated = wq.shape[1] + wk.shape[1]
    inner = wg.shape[1] // 2
    group = (GROUP, seq_size // 2, tokens, width)
    heads = wq.shape[1] // head_size
    gain_width = 2 * (width + head_size)
    routes = dp_size * 16
    column, line = (row_len, 1), (1, row_len)
    outs = [
        ((tokens, width), BF16, VMEM),
        ((1, gain_width), F32, VMEM),
        ((seq_size, tokens, width), BF16, HBM),
        ((width, rotated + wk.shape[1]), BF16, HBM),
        ((width, wo.shape[1]), BF16, HBM),
        ((width, inner), BF16, HBM),
        ((width, inner), BF16, HBM),
        ((width, inner), BF16, HBM),
        ((tokens, width), BF16, VMEM),
        ((row_len, rotated), BF16, HBM),
        ((row_len, rotated + wk.shape[1]), BF16, HBM),
        ((row_len, wq.shape[1]), BF16, HBM),
        ((wk.shape[1] // head_size, seq_size, 1, heads * head_size // wk.shape[1] * tokens), F32, VMEM),
        ((tokens, width), F32, VMEM),
        (group, BF16, HBM),
        ((row_len, head_size), F32, VMEM),
        ((row_len, head_size), F32, VMEM),
        (column, jnp.int32, VMEM),
        (column, jnp.int32, VMEM),
        (line, jnp.int32, VMEM),
        (line, jnp.int32, VMEM),
        ((tokens, 1), F32, VMEM),
        ((tokens, 1), F32, VMEM),
        ((routes, tokens), BF16, VMEM),
        ((tokens, routes), BF16, VMEM),
    ]
    scratch = [
        pltpu.VMEM((dp_size, 16, width // GROUP), BF16),
        pltpu.VMEM((dp_size, 16, width // GROUP), BF16),
        pltpu.VMEM((dp_size, 1, gain_width), F32),
        pltpu.VMEM((1, gain_width), F32),
        pltpu.VMEM((seq_size, 1, tokens), jnp.int32),
        pltpu.VMEM((seq_size, 1, tokens), jnp.int32),
        pltpu.VMEM((tokens, width), BF16),
        pltpu.VMEM((wq.shape[1] // wk.shape[1] * tokens, row_len), F32),
        pltpu.VMEM((2, tokens, width), BF16),
        pltpu.VMEM((2, tokens, width), BF16),
        pltpu.VMEM((tokens, width), BF16),
        pltpu.VMEM((2, tokens, width), BF16),
        pltpu.VMEM((tokens, width), BF16),
    ]
    scratch += [
        pltpu.VMEM((seq_size, tokens, width), BF16),
        pltpu.VMEM((width, rotated + wk.shape[1]), BF16),
        pltpu.VMEM((width, wo.shape[1]), BF16),
        pltpu.VMEM((row_len, rotated), BF16),
        pltpu.VMEM((row_len, rotated + wk.shape[1]), BF16),
        pltpu.VMEM((row_len, wq.shape[1]), BF16),
    ]
    sends = 2 * (dp_size - 1) + 4 * (high + 1) + 9 * high
    sends += 3 * (3 + 2 * high) + 2 * GatherGroup.sends + GatherSeq.sends + 3
    return pl.pallas_call(
        functools.partial(forward_kernel, sizes),
        out_shape=[jax.ShapeDtypeStruct(shape, dtype) for shape, dtype, _ in outs],
        in_specs=[VMEM] * 11 + [HBM] * 4 + [VMEM] * 3,
        out_specs=[spec for _, _, spec in outs],
        scratch_shapes=scratch + sems(sends, 24),
        compiler_params=comm_params(collective_id),
        name="forward_attention",
    )(*args)


class ScatterColumns:
    stage_rows = 512

    @staticmethod
    def scratch(high, rows, quarter):
        group_rows = GROUP * rows
        return [
            pltpu.VMEM((high * group_rows, quarter), BF16),
            pltpu.VMEM((max(high - 1, 1), group_rows, quarter), BF16),
            pltpu.VMEM((GROUP - 1, rows, quarter), BF16),
        ]

    def __init__(self, place, mover, parts, from_x, from_h, from_g, mine=None):
        self.place, self.mover, self.parts, self.mine = place, mover, parts, mine
        self.from_x, self.from_h, self.from_g = from_x, from_h, from_g
        self.group_rows, self.quarter = (from_h.shape[1:] if mine is None else mine.shape)

    def rows_of(self, step):
        high = lax.rem(self.place.h + step, self.place.high)
        return high * self.group_rows

    def start(self, steps):
        quarter = self.quarter
        for step in steps:
            rows = pl.ds(pl.multiple_of(self.rows_of(step), self.group_rows), self.group_rows)
            self.over_x[step] = self.mover.send(
                self.parts.at[rows, pl.ds(quarter, quarter)],
                self.from_x.at[rows],
                self.place.x_peer,
            )

    def start_far(self):
        self.over_x = {}
        self.start(range(1, self.place.high))

    def start_near(self):
        self.start((0,))

    def add_x(self, step, stage):
        mover, total = self.mover, self.from_x
        rows = stage.shape[1]
        base = self.rows_of(step)
        near = pl.ds(0, self.quarter)
        pieces = self.group_rows // rows

        def block(index):
            return pl.ds(pl.multiple_of(base + index * rows, rows), rows)

        def load(index):
            return mover.local(self.parts.at[block(index), near], stage.at[index % 2])

        copies = [load(0)]
        self.over_x[step].wait_recv()
        for index in range(pieces):
            if index + 1 < pieces:
                copies.append(load(index + 1))
            copies[index].wait()
            part = total.at[block(index)]
            add_rows(part, [part, stage.at[index % 2]], rows, 64)

    def forward_far(self, stage):
        place = self.place
        self.over_h = []
        for step in range(1, place.high):
            self.add_x(step, stage)
            block = pl.ds(pl.multiple_of(self.rows_of(step), self.group_rows), self.group_rows)
            self.over_h.append(
                self.mover.send(
                    self.from_x.at[block], self.from_h.at[step - 1], place.h_peer(step)
                )
            )

    def send_far(self, added):
        self.over_x, self.over_h = {}, []
        for step in range(1, self.place.high):
            rows = pl.ds(pl.multiple_of(self.rows_of(step), self.group_rows), self.group_rows)
            peer = self.place.h_peer(step)
            self.over_h.append(
                self.mover.send(added.at[rows], self.from_h.at[step - 1], peer)
            )

    def add_near(self, stage):
        self.add_x(0, stage)

    def merge(self):
        rows = pl.ds(pl.multiple_of(self.rows_of(0), self.group_rows), self.group_rows)
        self.mine = self.from_x.at[rows]
        for copy in self.over_h:
            copy.wait_recv()
        terms = [self.mine] + [self.from_h.at[step] for step in range(self.place.high - 1)]
        add_rows(self.mine, terms, self.group_rows, 64)

    def block(self, index):
        rows = self.group_rows // GROUP
        return self.mine.at[pl.ds(pl.multiple_of(index * rows, rows), rows)]

    def send_g(self):
        place = self.place
        self.over_g = []
        for step in (3, 1, 2):
            block = self.block(lax.rem(place.g + step, GROUP))
            copy = self.mover.send(block, self.from_g.at[step - 1], place.g_peer(step))
            self.over_g.append((step, copy))

    def finish(self, stage, out):
        place, quarter = self.place, self.quarter
        columns = pl.ds(pl.multiple_of(place.g * quarter, quarter), quarter)
        stage[:, columns] = self.block(place.g)[...].astype(F32)
        for step, copy in self.over_g:
            copy.wait_recv()
            source = lax.rem(place.g + GROUP - step, GROUP)
            columns = pl.ds(pl.multiple_of(source * quarter, quarter), quarter)
            stage[:, columns] = self.from_g[step - 1].astype(F32)
        if out is not None:
            self.mover.local(stage, out).wait()


class ScatterDp:
    @staticmethod
    def sends(high):
        return 2 * high + high + high - 1

    @staticmethod
    def scratch(high, rows, width):
        return [
            pltpu.VMEM((2, high, rows, width), BF16),
            pltpu.VMEM((high, rows, width), BF16),
            pltpu.VMEM((max(high - 1, 1), rows, width), BF16),
        ]

    def __init__(self, place, mover, parts, out, from_y, from_l, from_h):
        self.place, self.mover, self.parts, self.out = place, mover, parts, out
        self.from_y, self.from_l, self.from_h = from_y, from_l, from_h
        self.rows = out.shape[0]

    def block(self, high, l_index, y_index):
        index = high * GROUP + l_index * 2 + y_index
        return self.parts.at[pl.ds(pl.multiple_of(index * self.rows, self.rows), self.rows)]

    def start(self):
        place = self.place
        self.owners = (1 - place.l, place.l)
        self.over_y = []
        for index, l_owner in enumerate(self.owners):
            for high in range(place.high):
                source = self.block(high, l_owner, 1 - place.y)
                self.over_y.append(
                    self.mover.send(source, self.from_y.at[index, high], place.y_peer)
                )

    def ready(self, index, extra=None):
        place = self.place
        for high in range(place.high):
            self.over_y[index * place.high + high].wait_recv()
            mine = self.block(high, self.owners[index], place.y)
            terms = [mine, self.from_y.at[index, high]]
            if extra is not None:
                extra[high].wait_recv()
                terms.append(self.from_l.at[high])
            add_rows(mine, terms, self.rows, 32)

    def forward_y(self):
        place = self.place
        self.ready(0)
        self.over_l = []
        for high in range(place.high):
            source = self.block(high, 1 - place.l, place.y)
            self.over_l.append(self.mover.send(source, self.from_l.at[high], place.l_peer))

    def forward_l(self):
        place = self.place
        self.ready(1, self.over_l)
        self.over_h = []
        for step in range(1, place.high):
            source = self.block(lax.rem(place.h + step, place.high), place.l, place.y)
            self.over_h.append(
                self.mover.send(source, self.from_h.at[step - 1], place.h_peer(step))
            )

    def finish(self):
        place = self.place
        for copy in self.over_h:
            copy.wait_recv()
        terms = [self.block(place.h, place.l, place.y)]
        terms += [self.from_h.at[step] for step in range(place.high - 1)]
        add_rows(self.out, terms, self.rows, 32)


class ScatterGroup:
    sends = 10

    @staticmethod
    def scratch(rows, width):
        return [
            pltpu.VMEM((GROUP, rows, width), BF16),
            pltpu.VMEM((6, rows // 2, width), BF16),
        ]

    def __init__(self, place, mover, parts, from_c, landed):
        self.place, self.mover, self.parts = place, mover, parts
        self.from_c, self.landed = from_c, landed
        self.owners = (place.gd, place.gy, place.gl, place.g)
        self.over_c = []
        half = from_c.shape[1] // 2
        self.low, self.top = pl.ds(0, half), pl.ds(half, half)

    def start(self, index):
        place = self.place
        source = self.parts.at[self.owners[index], 1 - place.c]
        self.over_c.append(self.mover.send(source, self.from_c.at[index], place.c_peer))

    def forward(self, index):
        place, mover, sums, landed = self.place, self.mover, self.from_c, self.landed
        low, top = self.low, self.top
        self.over_c[index].wait_recv()
        total = sums.at[index]
        own = self.parts.at[self.owners[index], place.c]
        add_rows(total, [total, own], total.shape[0], 32)
        if index == 0:
            self.y_diag = mover.send(sums.at[0, low], landed.at[0], place.y_peer)
            self.l_diag = mover.send(sums.at[0, top], landed.at[1], place.l_peer)
        if index == 1:
            self.y_own = mover.send(sums.at[1, low], landed.at[2], place.y_peer)
        if index == 2:
            self.l_own = mover.send(sums.at[2, top], landed.at[3], place.l_peer)

    def forward_diag(self):
        place, mover, sums, landed = self.place, self.mover, self.from_c, self.landed
        half = sums.shape[1] // 2
        low, top = self.low, self.top
        self.y_diag.wait_recv()
        add_rows(sums.at[2, low], [sums.at[2, low], landed.at[0]], half, 32)
        self.l_last = mover.send(sums.at[2, low], landed.at[4], place.l_peer)
        self.l_diag.wait_recv()
        add_rows(sums.at[1, top], [sums.at[1, top], landed.at[1]], half, 32)
        self.y_last = mover.send(sums.at[1, top], landed.at[5], place.y_peer)

    def finish(self, take):
        half = self.from_c.shape[1] // 2
        chunk = 32
        self.y_own.wait_recv()
        self.l_last.wait_recv()
        self.l_own.wait_recv()
        self.y_last.wait_recv()
        for base, first, second in ((0, 2, 4), (half, 3, 5)):

            def step(index, carry):
                rows = pl.ds(pl.multiple_of(base + index * chunk, chunk), chunk)
                inner = pl.ds(pl.multiple_of(index * chunk, chunk), chunk)
                total = self.from_c[3, rows, :].astype(F32)
                total = total + self.landed[first, inner, :].astype(F32)
                take(rows, total + self.landed[second, inner, :].astype(F32))
                return carry

            lax.fori_loop(0, half // chunk, step, 0)


def norm_back(values, gain, cotangent):
    scale = lax.rsqrt(jnp.mean(values * values, axis=-1, keepdims=True) + NORM_EPS)
    weighted = cotangent * gain
    inner = jnp.mean(weighted * values, axis=-1, keepdims=True)
    unit = values * scale
    return scale * (weighted - unit * (scale * inner)), cotangent * unit


def feed_forward_kernel(sizes, *refs):
    nm_hbm, wg_hbm, wu_hbm, wd_hbm, grad_y, resid, live, gains = refs[:8]
    mixed, grad_resid, full_proj, gain_sum, part_gd, out_gd, out_gg, out_gu = refs[8:16]
    (nm, gy, wg, wu, wd, hidden, gate_grad, up_grad, part_nmlp, part_down, nmlp_c, nmlp_landed,
     down_c, down_landed, grad_proj, stage, column_stage, gd_from_x, gd_from_h) = refs[16:35]
    send_sems, recv_sems, local_sems = refs[35:]
    place = Place(*sizes)
    mover = Mover(send_sems, recv_sems, local_sems)
    tokens, width = resid.shape
    cores = place.cores
    block = cores * tokens
    inner = wg.shape[1]
    tile = 256
    loads = [mover.local(wg_hbm, wg), mover.local(wu_hbm, wu)]
    nm_loads = [mover.local(nm_hbm.at[index], nm.at[index]) for index in range(GROUP)]
    wd_load = mover.local(wd_hbm, wd)
    greet([place.y_peer, place.l_peer, place.c_peer, place.x_peer])
    gather = GatherGroup(place, mover, grad_y, gy)
    gain_sum[...] = jnp.zeros_like(gain_sum)
    for copy in loads:
        copy.wait()

    def gate_up(index, carry):
        source = nm[index].reshape(block, width)
        rows = pl.ds(pl.multiple_of(index * block, block), block)
        for start in range(0, inner, tile):
            lanes = slice(start, start + tile)
            gate = jnp.dot(source, wg[:, lanes], preferred_element_type=F32)
            upper = jnp.dot(source, wu[:, lanes], preferred_element_type=F32)
            gain = 1.0 / (1.0 + jnp.exp(-gate))
            silu = gate * gain
            hidden[rows, lanes] = (silu * upper).astype(BF16)
            up_grad[rows, lanes] = silu.astype(BF16)
            gate_grad[rows, lanes] = (upper * (gain + silu * (1.0 - gain))).astype(BF16)
        return carry

    def weight_grads(source, grads, targets):
        copies = []
        count = len(grads)
        for index in range(width // tile):
            lanes = pl.ds(index * tile, tile)
            left = source[:, :, :, lanes].reshape(GROUP * block, tile)
            for which in range(count):
                slot = (index * count + which) % 2
                if len(copies) >= 2:
                    copies[-2].wait()
                stage[slot] = product(left, grads[which][...], CONTRACT_ROWS).astype(BF16)
                copies.append(mover.local(stage.at[slot], targets[which].at[lanes]))
        copies[-2].wait()
        copies[-1].wait()

    nm_loads[0].wait()
    nm_loads[1].wait()
    lax.fori_loop(0, 2, gate_up, 0)
    gather.forward()
    nm_loads[2].wait()
    nm_loads[3].wait()
    lax.fori_loop(2, GROUP, gate_up, 0)
    wd_load.wait()

    def down_block(owner):
        rows = pl.ds(pl.multiple_of(owner * block, block), block)

        def step(index, carry):
            lanes = pl.ds(pl.multiple_of(index * tile, tile), tile)
            result = product(hidden[rows, :], wd[lanes, :], CONTRACT_COLS).astype(BF16)
            part_down[owner, :, :, lanes] = result.reshape(cores, tokens, tile)
            return carry

        lax.fori_loop(0, width // tile, step, 0)

    down = ScatterGroup(place, mover, part_down, down_c, down_landed)
    for index in range(GROUP):
        down_block(down.owners[index])
        down.start(index)
    gather.finish_ici()
    gather.finish()
    lower = ScatterColumns(place, mover, part_gd, gd_from_x, gd_from_h, None)

    def back_block(owner):
        rows = pl.ds(pl.multiple_of(owner * block, block), block)
        source = gy[owner].reshape(block, width)
        for start in range(0, inner, tile):
            lanes = slice(start, start + tile)
            grad_mid = jnp.dot(source, wd[:, lanes], preferred_element_type=F32)
            gate_grad[rows, lanes] = (grad_mid * gate_grad[rows, lanes].astype(F32)).astype(BF16)
            up_grad[rows, lanes] = (grad_mid * up_grad[rows, lanes].astype(F32)).astype(BF16)

        def step(index, carry):
            lanes = pl.ds(pl.multiple_of(index * tile, tile), tile)
            result = product(gate_grad[rows, :], wg[lanes, :], CONTRACT_COLS)
            result = result + product(up_grad[rows, :], wu[lanes, :], CONTRACT_COLS)
            part_nmlp[owner, :, :, lanes] = result.astype(BF16).reshape(cores, tokens, tile)
            return carry

        lax.fori_loop(0, width // tile, step, 0)

    down.forward(0)
    nmlp = ScatterGroup(place, mover, part_nmlp, nmlp_c, nmlp_landed)
    back_block(nmlp.owners[0])
    nmlp.start(0)
    back_block(nmlp.owners[1])
    nmlp.start(1)
    nmlp.forward(0)
    back_block(nmlp.owners[2])
    nmlp.start(2)
    nmlp.forward(1)
    nmlp.forward(2)
    weight_grads(gy, [hidden], [part_gd])
    lower.start_far()
    nmlp.forward_diag()
    back_block(nmlp.owners[3])
    nmlp.start(3)
    nmlp.forward(3)

    def back_mlp(rows, total):
        grad, terms = norm_back(resid[rows, :], gains[:, width : 2 * width], total)
        grad = grad + grad_y[rows, :].astype(F32)
        grad_resid[rows, :] = grad
        grad_proj[rows, :] = grad.astype(BF16)
        gain_sum[...] += jnp.sum(terms, axis=0, keepdims=True)

    def mix(rows, total):
        mixed[rows, :] = ((resid[rows, :] + total) * live[rows, :]).astype(BF16)

    nmlp.finish(back_mlp)
    row = GatherSeq(place, mover, grad_proj, full_proj)
    for index in range(1, GROUP):
        down.forward(index)
    down.forward_diag()
    weight_grads(nm, [gate_grad, up_grad], [out_gg, out_gu])
    row.forward()
    added = []
    for step in range(1, place.high):
        lower.add_x(step, column_stage)
        rows = pl.ds(pl.multiple_of(lower.rows_of(step), lower.group_rows), lower.group_rows)
        added.append(mover.local(gd_from_x.at[rows], out_gd.at[rows]))
    down.finish(mix)
    row.finish()
    for copy in added:
        copy.wait()
    mover.finish()


def feed_forward(sizes, collective_id, args):
    dp_size, seq_size = sizes
    nm, wg, resid, gains = args[0], args[1], args[5], args[7]
    tokens, width = resid.shape
    inner = wg.shape[1]
    high = dp_size // GROUP
    piece = min(width // high, ScatterColumns.stage_rows)
    rows = GROUP * (seq_size // 2) * tokens
    outs = [
        ((tokens, width), BF16, VMEM),
        ((tokens, width), F32, VMEM),
        ((seq_size, tokens, width), BF16, HBM),
        ((1, width), F32, VMEM),
        ((width, inner), BF16, HBM),
        ((width, inner // 2), BF16, HBM),
        ((width, inner), BF16, HBM),
        ((width, inner), BF16, HBM),
    ]
    scratch = [pltpu.VMEM(nm.shape, BF16)] * 2
    scratch += [pltpu.VMEM((width, inner), BF16)] * 3
    scratch += [pltpu.VMEM((rows, inner), BF16)] * 3
    scratch += [pltpu.VMEM(nm.shape, BF16)] * 2
    scratch += ScatterGroup.scratch(tokens, width) * 2
    scratch += [pltpu.VMEM((tokens, width), BF16), pltpu.VMEM((2, 256, inner), BF16)]
    scratch += [pltpu.VMEM((2, piece, inner // 2), BF16)]
    scratch += ScatterColumns.scratch(high, width // dp_size, inner // 2)[:2]
    sends = 3 * 10 + GatherSeq.sends + 2 * high
    local = 10 + 3 * (width // 256) + high * (width // high // piece)
    return pl.pallas_call(
        functools.partial(feed_forward_kernel, sizes),
        out_shape=[jax.ShapeDtypeStruct(shape, dtype) for shape, dtype, _ in outs],
        in_specs=[HBM] * 4 + [VMEM] * 4,
        out_specs=[spec for _, _, spec in outs],
        scratch_shapes=scratch + sems(sends, local),
        compiler_params=comm_params(collective_id, 63 * 1024 * 1024),
        name="feed_forward",
    )(*args)


def backward_kernel(sizes, *refs):
    part_gg, part_gu, part_gd, gd_far = refs[:4]
    moved, keep, gain_mlp, gains, cosine, sine = refs[12:18]
    seg_col, pos_col, seg_row, pos_row, log_row, recv_map, send_map = refs[18:25]
    grad_hidden, gain_sums, out_gd, out_gg, out_gu, out_q, out_k, out_v, out_wo = refs[25:34]
    send_sems, recv_sems, local_sems = refs[-3:]
    scratch = list(refs[34:-3])

    def take(count):
        taken = scratch[:count]
        del scratch[:count]
        return taken

    place = Place(*sizes)
    mover = Mover(send_sems, recv_sems, local_sems)
    tokens, width = moved.shape
    parts = sizes[1]
    head = cosine.shape[1]
    query_width = refs[6].shape[1]
    key_width = (refs[7].shape[1] - query_width) // 2
    rotated = query_width + key_width
    columns = width // GROUP
    repeat = query_width // key_width
    column_stage, out_stage = take(2)
    grad_wo, grad_key, grad_query = take(3)
    loaded = take(8)
    wo, full_proj, attended, rot, lin, normed, full_qkv, grad_resid = loaded
    lower = ScatterColumns(place, mover, part_gd, *take(3))
    gate = ScatterColumns(place, mover, part_gg, *take(3))
    upper = ScatterColumns(place, mover, part_gu, *take(3))
    wo_total, key_total = take(2)
    wo_sum = ScatterDp(place, mover, grad_wo, wo_total, *take(3))
    key_sum = ScatterDp(place, mover, grad_key, key_total, *take(3))
    query_sum = ScatterDp(place, mover, grad_query, out_q, *take(3))
    grad_moved, to_c, from_c, from_x = take(4)
    grad_att, grad_keys, grad_values, grad_lin, bias = take(5)
    blocks_out, blocks_in, rows_in, row_c, row_x = take(5)

    loads = [mover.local(source, target) for source, target in zip(refs[4:12], loaded)]
    greet(dp_peers(place) + [place.x_peer, place.c_peer])
    gain_sums[...] = jnp.zeros_like(gain_sums)
    gain_sums[:, width : 2 * width] = gain_mlp[...]
    grad_keys[...] = jnp.zeros_like(grad_keys)
    grad_values[...] = jnp.zeros_like(grad_values)

    def attended_grad(part, carry):
        spots = pl.ds(pl.multiple_of(part * tokens, tokens), tokens)
        for start in range(0, query_width, 256):
            result = jnp.dot(full_proj[part], wo[:, start : start + 256], preferred_element_type=F32)
            grad_att[spots, start : start + 256] = result.astype(BF16)
        return carry


    def out_weight_grad(index, carry):
        lanes = pl.ds(pl.multiple_of(index * 256, 256), 256)
        source = full_proj[:, :, lanes].reshape(parts * tokens, 256)
        grad_wo[lanes, :] = product(source, attended[...], CONTRACT_ROWS).astype(BF16)
        return carry

    scale = head ** (-0.5)
    gain_query = gains[:, 2 * width : 2 * width + head]
    gain_key = gains[:, 2 * width + head : 2 * width + 2 * head]

    def unrotate(spots, lanes, grad, gain, gain_lanes):
        turned = grad * cosine[spots, :] - lane_swap(grad) * sine[spots, :]
        values, terms = norm_back(lin[spots, lanes].astype(F32), gain, turned)
        grad_lin[spots, lanes] = values.astype(BF16)
        gain_sums[:, gain_lanes] += jnp.sum(terms, axis=0, keepdims=True)

    def attention_part(part):
        keys = (part + 1) * tokens
        spots = pl.ds(part * tokens, tokens)
        allowed = (seg_col[:keys, :] == seg_row[:, spots]) & (pos_col[:keys, :] <= pos_row[:, spots])
        some = jnp.where(allowed, 0.0, MASKED)
        for copy in range(repeat):
            bias[:keys, copy * tokens : (copy + 1) * tokens] = some

        def attend(pair, carry):
            key_lanes = pl.ds(pl.multiple_of(query_width + pair * head, head), head)
            value_lanes = pl.ds(pl.multiple_of(rotated + pair * head, head), head)
            own_lanes = pl.ds(pl.multiple_of(pair * head, head), head)
            query_lanes = [
                pl.ds(pl.multiple_of((pair * repeat + copy) * head, head), head)
                for copy in range(repeat)
            ]
            queries = jnp.concatenate([rot[spots, lanes] for lanes in query_lanes], axis=0)
            grads = jnp.concatenate([grad_att[spots, lanes] for lanes in query_lanes], axis=0)
            key_rows, value_rows = rot[:keys, key_lanes], rot[:keys, value_lanes]
            scores = product(key_rows, queries, CONTRACT_COLS) * scale + bias[:keys, :]
            probs = jnp.exp(scores - log_row[pair, part])
            grad_values[:keys, own_lanes] += jnp.dot(
                probs.astype(BF16), grads, preferred_element_type=F32
            )
            grad_probs = product(value_rows, grads, CONTRACT_COLS)
            spread = jnp.sum(probs * grad_probs, axis=0, keepdims=True)
            grad_scores = (probs * (grad_probs - spread)).astype(BF16)
            grad_keys[:keys, own_lanes] += jnp.dot(
                grad_scores, queries, preferred_element_type=F32
            )
            grad_queries = product(grad_scores, key_rows, CONTRACT_ROWS) * scale
            for copy in range(repeat):
                unrotate(
                    spots,
                    query_lanes[copy],
                    grad_queries[copy * tokens : (copy + 1) * tokens],
                    gain_query,
                    pl.ds(2 * width, head),
                )
            return carry

        lax.fori_loop(0, key_width // head, attend, 0)

    def back_all_keys():
        for pair in range(key_width // head):

            def back_keys(part, carry):
                spots = pl.ds(pl.multiple_of(part * tokens, tokens), tokens)
                lanes = pl.ds(pair * head, head)
                unrotate(
                    spots,
                    pl.ds(query_width + pair * head, head),
                    grad_keys[spots, lanes] * scale,
                    gain_key,
                    pl.ds(2 * width + head, head),
                )
                grad_lin[spots, pl.ds(rotated + pair * head, head)] = grad_values[spots, lanes].astype(
                    BF16
                )
                return carry

            lax.fori_loop(0, parts, back_keys, 0)

    def weight_grad(target, start, size):
        def step(index, carry):
            lanes = pl.ds(pl.multiple_of(index * 256, 256), 256)
            source = normed[:, :, lanes].reshape(parts * tokens, 256)
            target[lanes, :] = product(
                source, grad_lin[:, start : start + size], CONTRACT_ROWS
            ).astype(BF16)
            return carry

        lax.fori_loop(0, width // 256, step, 0)

    def normed_grad(part, target):
        source = grad_lin[pl.ds(pl.multiple_of(part * tokens, tokens), tokens), :]

        def step(index, carry):
            block = pl.ds(pl.multiple_of(index * 256, 256), 256)
            target[:, block] = product(source, full_qkv[block, :], CONTRACT_COLS).astype(BF16)
            return carry

        lax.fori_loop(0, width // 256, step, 0)

    cores = place.cores
    places = ((1 - place.x) * cores, place.x * cores)
    over = {}

    def send_other_row():
        normed_grad(places[0] + 1 - place.c, to_c.at[0])
        first = mover.send(to_c.at[0], from_c.at[0], place.c_peer)
        normed_grad(places[0] + place.c, to_c.at[1])
        first.wait_recv()
        add_rows(to_c.at[1], [to_c.at[1], from_c.at[0]], tokens, 32)
        over["x"] = mover.send(to_c.at[1], from_x, place.x_peer)

    def send_own_row():
        normed_grad(places[1] + 1 - place.c, to_c.at[2])
        over["c"] = mover.send(to_c.at[2], from_c.at[1], place.c_peer)
        normed_grad(places[1] + place.c, to_c.at[3])

    def back_normed(index, carry):
        rows = pl.ds(pl.multiple_of(index * 32, 32), 32)
        total = to_c[3, rows, :].astype(F32) + from_c[1, rows, :].astype(F32)
        total = total + from_x[rows, :].astype(F32)
        grad, terms = norm_back(moved[rows, :].astype(F32), gains[:, :width], total)
        grad_moved[rows, :] = (grad_resid[rows, :] + grad).astype(BF16)
        gain_sums[:, :width] += jnp.sum(terms, axis=0, keepdims=True)
        return carry

    piece_row = index_of((place.dp_size * 16, 1), 0) & 3
    copies = []

    def finish_row():
        over["c"].wait_recv()
        over["x"].wait_recv()
        lax.fori_loop(0, tokens // 32, back_normed, 0)
        for q in range(GROUP):
            lanes = pl.ds(q * columns, columns)
            piece = product(recv_map[...], grad_moved[:, lanes], CONTRACT_ROWS)
            piece = jnp.where(piece_row == q, piece, 0.0)
            total = piece if q == 0 else total + piece
        blocks_out[...] = total.astype(BF16).reshape(blocks_out.shape)
        for step in range(1, place.dp_size):
            other = lax.rem(place.d + step, place.dp_size)
            copies.append(mover.send(blocks_out.at[other], blocks_in.at[place.d], (other, place.s)))
            copies.append(mover.send(gain_sums, rows_in.at[place.d], (other, place.s)))
        blocks_in[place.d] = blocks_out[place.d]
        rows_in[place.d] = gain_sums[...]

    def finish_hidden():
        for copy in copies:
            copy.wait_recv()
        row_total = rows_in[0]
        for index in range(1, place.dp_size):
            row_total = row_total + rows_in[index]
        row_c[0] = row_total
        over["gc"] = mover.send(row_c.at[0], row_c.at[1], place.c_peer)
        returned = blocks_in[...].reshape(place.dp_size * 16, columns)
        for q in range(GROUP):
            lanes = pl.ds(q * columns, columns)
            chosen = jnp.where(piece_row == q, returned, jnp.zeros_like(returned))
            here = product(send_map[...], chosen, CONTRACT_ROWS)
            here = here + jnp.where(keep[...] > 0.0, grad_moved[:, lanes].astype(F32), 0.0)
            grad_hidden[:, lanes] = here.astype(BF16)

    def pass_gains():
        over["gc"].wait_recv()
        row_x[0] = row_c[0] + row_c[1]
        over["gx"] = mover.send(row_x.at[0], row_x.at[1], place.x_peer)

    gate.start_far()
    lower.send_far(gd_far)
    lower.start_near()
    for copy in loads[:2]:
        copy.wait()
    lax.fori_loop(0, parts, attended_grad, 0)
    for copy in loads[2:5]:
        copy.wait()
    lax.fori_loop(0, width // 256, out_weight_grad, 0)
    attention_part(0)
    upper.start_far()
    wo_sum.start()
    attention_part(1)
    attention_part(2)
    gate.forward_far(column_stage)
    wo_sum.forward_y()
    for part in range(3, parts):
        attention_part(part)
    upper.start_near()
    back_all_keys()
    for copy in loads[5:]:
        copy.wait()
    weight_grad(grad_key, query_width, 2 * key_width)
    key_sum.start()
    weight_grad(grad_query, 0, query_width)
    upper.forward_far(column_stage)
    lower.add_near(column_stage)
    query_sum.start()
    key_sum.forward_y()
    send_other_row()
    query_sum.forward_y()
    gate.start_near()
    wo_sum.forward_l()
    lower.merge()
    lower.send_g()
    key_sum.forward_l()
    gate.add_near(column_stage)
    wo_sum.finish()
    out_wo[...] = wo_total[...].T
    gate.merge()
    gate.send_g()
    send_own_row()
    finish_row()
    query_sum.forward_l()
    upper.add_near(column_stage)
    upper.merge()
    upper.send_g()
    lower.finish(out_stage, None)
    out_gd[...] = out_stage[...].T
    finish_hidden()
    gate.finish(out_stage, out_gg)
    key_sum.finish()
    out_k[...] = key_total[:, :key_width]
    out_v[...] = key_total[:, key_width:]
    pass_gains()
    upper.finish(out_stage, out_gu)
    query_sum.finish()
    over["gx"].wait_recv()
    mover.finish()
    gain_sums[...] = row_x[0] + row_x[1]


def backward(sizes, collective_id, args):
    dp_size, seq_size = sizes
    part_gg, attended, rot, moved, gains = args[0], args[6], args[7], args[12], args[15]
    tokens, width = moved.shape
    high = dp_size // GROUP
    rows = width // dp_size
    quarter = part_gg.shape[1] // 2
    row_len = seq_size * tokens
    query_width = attended.shape[1]
    key_width = (rot.shape[1] - query_width) // 2
    repeat = query_width // key_width
    outs = [
        ((tokens, width), BF16, VMEM),
        (gains.shape, F32, VMEM),
        ((GROUP * quarter, rows), F32, VMEM),
        ((rows, GROUP * quarter), F32, HBM),
        ((rows, GROUP * quarter), F32, HBM),
        ((rows, query_width), F32, VMEM),
        ((rows, key_width), F32, VMEM),
        ((rows, key_width), F32, VMEM),
        ((query_width, rows), F32, VMEM),
    ]
    piece = min(GROUP * rows, ScatterColumns.stage_rows)
    scratch = [
        pltpu.VMEM((2, piece, quarter), BF16),
        pltpu.VMEM((rows, GROUP * quarter), F32),
    ]
    scratch += [
        pltpu.VMEM((width, query_width), BF16),
        pltpu.VMEM((width, 2 * key_width), BF16),
        pltpu.VMEM((width, query_width), BF16),
    ]
    scratch += [pltpu.VMEM(array.shape, array.dtype) for array in args[4:12]]
    for _ in range(3):
        scratch += ScatterColumns.scratch(high, rows, quarter)
    scratch += [
        pltpu.VMEM((rows, query_width), F32),
        pltpu.VMEM((rows, 2 * key_width), F32),
    ]
    scratch += ScatterDp.scratch(high, rows, query_width)
    scratch += ScatterDp.scratch(high, rows, 2 * key_width)
    scratch += ScatterDp.scratch(high, rows, query_width)
    scratch += [
        pltpu.VMEM((tokens, width), BF16),
        pltpu.VMEM((seq_size, tokens, width), BF16),
        pltpu.VMEM((2, tokens, width), BF16),
        pltpu.VMEM((tokens, width), BF16),
        pltpu.VMEM((row_len, query_width), BF16),
        pltpu.VMEM((row_len, key_width), F32),
        pltpu.VMEM((row_len, key_width), F32),
        pltpu.VMEM((row_len, rot.shape[1]), BF16),
        pltpu.VMEM((row_len, repeat * tokens), F32),
        pltpu.VMEM((dp_size, 16, width // GROUP), BF16),
        pltpu.VMEM((dp_size, 16, width // GROUP), BF16),
        pltpu.VMEM((dp_size,) + gains.shape, F32),
        pltpu.VMEM((2,) + gains.shape, F32),
        pltpu.VMEM((2,) + gains.shape, F32),
    ]
    sends = 3 * (2 * high + 2) + 3 * ScatterDp.sends(high)
    sends += 3 + 2 * (dp_size - 1) + 2
    local = 3 * (high * GROUP * rows // piece + 1) + 9
    return pl.pallas_call(
        functools.partial(backward_kernel, sizes),
        out_shape=[jax.ShapeDtypeStruct(shape, dtype) for shape, dtype, _ in outs],
        in_specs=[HBM] * 12 + [VMEM] * 13,
        out_specs=[spec for _, _, spec in outs],
        scratch_shapes=scratch + sems(sends, local),
        compiler_params=comm_params(collective_id, 63 * 1024 * 1024),
        name="backward_attention",
    )(*args)


def hand_over_kernel(count, *refs):
    held = refs[2 * count : 3 * count]
    sems_in, sems_out = refs[3 * count :]
    loads = [
        pltpu.make_async_copy(refs[index], held[index], sems_in.at[index])
        for index in range(count)
    ]
    stores = [
        pltpu.make_async_copy(held[index], refs[count + index], sems_out.at[index])
        for index in range(count)
    ]
    for copy in loads:
        copy.start()
    for load, store in zip(loads, stores):
        load.wait()
        store.start()
    for copy in stores:
        copy.wait()


def hand_over(arrays):
    count = len(arrays)
    return pl.pallas_call(
        functools.partial(hand_over_kernel, count),
        out_shape=[jax.ShapeDtypeStruct(array.shape, array.dtype) for array in arrays],
        in_specs=[HBM] * count,
        out_specs=[HBM] * count,
        scratch_shapes=[pltpu.VMEM(array.shape, array.dtype) for array in arrays]
        + [pltpu.SemaphoreType.DMA((count,)), pltpu.SemaphoreType.DMA((count,))],
        compiler_params=pltpu.CompilerParams(vmem_limit_bytes=62 * 1024 * 1024),
        name="hand_over",
    )(*arrays)


def per_device(
    sizes,
    hidden_in,
    valid_len,
    doc_lengths,
    doc_perm,
    attn_norm,
    w_query,
    key_weight,
    value_weight,
    w_out,
    query_norm,
    key_norm_gain,
    mlp_norm,
    w_gate,
    w_up,
    w_down,
    out_grad,
):
    model_width = hidden_in.shape[1]
    seq_count, row_count, _ = doc_lengths.shape
    my_row = lax.axis_index("dp")
    my_part = lax.axis_index("seq")
    head_size = query_norm.shape[0] * row_count
    lengths = doc_lengths.reshape(seq_count, -1)
    (
        moved_low,
        gains,
        normed,
        qkv_mat,
        out_mat,
        gate_mat,
        up_mat,
        down_mat,
        grad_y_own,
        rotated_lin,
        rotated_all,
        attended,
        log_total,
        resid_rows,
        normed_mlp,
        cosine,
        sine,
        seg_col,
        pos_col,
        seg_row,
        pos_row,
        keep,
        live,
        send_map,
        recv_map,
    ) = forward(
        sizes,
        1,
        head_size,
        (
            hidden_in,
            valid_len[None, :],
            lengths[:, None, :],
            doc_perm[:, None, :],
            lengths[:, :, None],
            doc_perm[:, :, None],
            attn_norm[None, :],
            mlp_norm[None, :],
            query_norm[None, :],
            key_norm_gain[None, :],
            out_grad,
            w_query,
            key_weight,
            value_weight,
            w_out.T,
            w_gate,
            w_up,
            w_down.T,
        ),
    )
    cuts = (model_width, 2 * model_width, 2 * model_width + head_size)
    mixed, grad_resid, grad_proj, gain_mlp_sum, part_down, grad_down, grad_gate, grad_up = feed_forward(
        sizes,
        2,
        (normed_mlp, gate_mat, up_mat, down_mat, grad_y_own, resid_rows, live, gains),
    )
    (
        grad_hidden,
        gain_sums,
        out_down,
        out_gate,
        out_up,
        out_query,
        out_key,
        out_value,
        out_wo,
    ) = backward(
        sizes,
        3,
        (
            grad_gate,
            grad_up,
            part_down,
            grad_down,
            out_mat,
            grad_proj,
            attended,
            rotated_all,
            rotated_lin,
            normed,
            qkv_mat,
            grad_resid,
            moved_low,
            keep,
            gain_mlp_sum,
            gains,
            cosine,
            sine,
            seg_col,
            pos_col,
            seg_row,
            pos_row,
            log_total,
            recv_map,
            send_map,
        ),
    )
    device = my_row * seq_count + my_part

    def own_piece(vector):
        size = vector.shape[0] // (row_count * seq_count)
        return lax.dynamic_slice_in_dim(vector, device * size, size)

    sum_attn, sum_mlp, sum_query, sum_key = [own_piece(v) for v in jnp.split(gain_sums[0], cuts)]
    (
        mixed,
        grad_hidden,
        out_query,
        out_key,
        out_value,
        out_wo,
        out_gate,
        out_up,
        out_down,
    ) = hand_over(
        (
            mixed,
            grad_hidden,
            out_query,
            out_key,
            out_value,
            out_wo,
            out_gate,
            out_up,
            out_down,
        )
    )
    return (
        mixed,
        grad_hidden,
        sum_attn,
        out_query,
        out_key,
        out_value,
        out_wo,
        sum_query,
        sum_key,
        sum_mlp,
        out_gate,
        out_up,
        out_down,
    )


def solution(mesh):
    in_specs = (
        P(("dp", "seq"), None),
        P(),
        P(),
        P(),
        P("dp"),
        P("dp", "seq"),
        P("dp", "seq"),
        P("dp", "seq"),
        P("seq", "dp"),
        P("dp"),
        P("dp"),
        P("dp"),
        P("dp", "seq"),
        P("dp", "seq"),
        P("seq", "dp"),
        P(("dp", "seq"), None),
    )
    out_specs = (
        P(("dp", "seq"), None),
        P(("dp", "seq"), None),
        P(("dp", "seq")),
        P("dp", "seq"),
        P("dp", "seq"),
        P("dp", "seq"),
        P("seq", "dp"),
        P(("dp", "seq")),
        P(("dp", "seq")),
        P(("dp", "seq")),
        P("dp", "seq"),
        P("dp", "seq"),
        P("seq", "dp"),
    )
    return jax.shard_map(
        functools.partial(per_device, (mesh.shape["dp"], mesh.shape["seq"])), mesh=mesh, in_specs=in_specs, out_specs=out_specs, check_vma=False
    )
```
